32 devices in a mesh: gx: 8 (over y, x, core), gy: 4 (over z).
Axes of the slice: x: 2, y: 2, z: 4, core: 2. Of those that a mesh axis runs over, the one named last changes fastest.
Arguments:
- right_side: float32 [3, 32, 16, 128], P(None, 'gx', 'gy'), may hold values from -10 to 10
- node_mass: float32 [32, 16, 128], P('gx', 'gy'), may hold values from 0.5 to 4
- gradients: float32 [8, 4, 8, 3, 27, 128], P('gx', 'gy'), may hold values from -3 to 3
- stiffness: float32 [8, 4, 8, 128], P('gx', 'gy'), may hold values from 0.2 to 2
- valid: int32 [8, 4, 8, 128], P('gx', 'gy'), may hold values 0 or 1
- node_base: int32 [8, 4, 8, 128], P('gx', 'gy'), may hold values from 0 to 2857, as said below
Outputs:
- solution: float32 [3, 32, 16, 128], P(None, 'gx', 'gy')
- residual: float32 [3, 32, 16, 128], P(None, 'gx', 'gy')
The draws below stay inside these ranges and needn't reach their ends.
Inputs may be any that keep to these rules, and one draw needn't show every extreme that they name: node_base = (i * 6 + j) * 130 + k with 0 <= i < 4, 0 <= j < 4, 0 <= k < 128.
All inputs are finite; a program needn't handle non-finite values. No bound on the sum of `valid` on one device may be relied on, other than what follows from the above.
Results may differ from the reference program's by a relative error of at most 0.00011.
Values sent between devices are 32-bit elements; how exact they have to be, the bound alone decides.
No kernel may reach another device: no remote copies, remote signals or barrier semaphores. Data moves between devices by JAX's collectives and lax.ppermute only.
A program may use at most 64 MiB of HBM per device.

```python
import math
import jax
import jax.numpy as jnp
from jax import lax

CX = 4
CY = 4
NZ = 128
BLK_DEV = 8
PB = 128
TILE = 27
ITERS = 2
SWEEPS = 4
NX = 32
NY = 16
N_GX = 8
N_GY = 4


def draw_right_side(key, part):
    x_pos = jnp.arange(NX, dtype=jnp.float32).reshape(1, NX, 1, 1)
    x_ramp = 1.0 + 2.0 * x_pos / max(NX - 1, 1)
    noise_part = jnp.clip(jax.random.normal(key, (3, NX, NY, NZ), jnp.float32), -3.3, 3.3)
    values = noise_part * x_ramp
    return values.astype(jnp.float32)


def draw_node_base(key, part):
    key_list = jax.random.split(key, 4)
    dims_all = (N_GX, N_GY, BLK_DEV, PB)
    row_x = jax.random.randint(key_list[0], dims_all, 0, CX)
    row_y = jax.random.randint(key_list[1], dims_all, 0, CY)
    row_z = jax.random.randint(key_list[2], dims_all, 0, NZ)
    flattened = (row_x * (CY + 2) + row_y) * (NZ + 2) + row_z
    corner_max = ((CX - 1) * (CY + 2) + CY - 1) * (NZ + 2) + NZ - 1
    chosen = jax.random.randint(key_list[3], (), 0, PB)
    flattened = flattened.at[0, 0, 0, chosen].set(corner_max)
    flattened = flattened.at[0, 0, 0, (chosen + 1) % PB].set(0)
    return flattened.astype(jnp.int32)


def set_ends(drawn, rng, least, largest):
    place = [jax.random.randint(jax.random.fold_in(rng, axis), (), 0, length) for axis, length in enumerate(drawn.shape)]
    main_axis = drawn.shape.index(max(drawn.shape))
    neighbour = place[:main_axis] + [(place[main_axis] + 1) % drawn.shape[main_axis]] + place[main_axis + 1:]
    return drawn.at[tuple(place)].set(least).at[tuple(neighbour)].set(largest)


def level_of(own_key, extent, cuts, smallest, largest):
    factor_of = 1.0
    for axis_at, parts in cuts:
        draws = jax.random.uniform(jax.random.fold_in(jax.random.fold_in(own_key, 6), axis_at), (parts,), jnp.float32, smallest / len(cuts), largest / len(cuts))
        factor_of = factor_of * jnp.repeat(jnp.exp(draws), extent[axis_at] // parts).reshape((-1,) + (1,) * (len(extent) - 1 - axis_at))
    return factor_of


def gaussian(stream_key, shape, spread, limit, cuts=(), kind=jnp.bfloat16):
    gain = level_of(stream_key, shape, cuts, -0.22, 0.18) if cuts else 1.0
    entries = jax.random.normal(stream_key, shape, jnp.float32) * spread * gain
    return jnp.minimum(jnp.maximum(entries, -limit), limit).astype(kind)


def setup_inputs(seed: int = 0) -> dict:
    key_of = jax.random.split(jax.random.key(seed), 7)
    return {
        "right_side": draw_right_side(jax.random.fold_in(key_of[6], 71), 0),
        "node_mass": jnp.clip(jnp.exp(math.log(4.0) - 2.0794415 * jax.random.uniform(key_of[1], (NX, NY, NZ), jnp.float32) ** level_of(key_of[1], (NX, NY, NZ), ((0, 8), (1, 4)), -0.2, 0.2)), 0.5, 4.0),
        "gradients": gaussian(key_of[2], (N_GX, N_GY, BLK_DEV, 3, TILE, PB), 0.5, 3.0, ((0, 8), (1, 4)), jnp.float32),
        "stiffness": jnp.clip(jnp.exp(math.log(2.0) - 2.3025851 * jax.random.uniform(key_of[3], (N_GX, N_GY, BLK_DEV, PB), jnp.float32) ** level_of(key_of[3], (N_GX, N_GY, BLK_DEV, PB), ((0, 8), (1, 4)), -0.2, 0.2)), 0.2, 2.0),
        "valid": set_ends((jax.random.randint(key_of[4], (N_GX, N_GY, BLK_DEV, PB), 0, 8) < 7).astype(jnp.int32), jax.random.fold_in(key_of[4], 1), 0, 1),
        "node_base": draw_node_base(jax.random.fold_in(key_of[6], 71), 0),
    }


POISSON = 0.3
DAMPING = 0.7
LAPLACE_WEIGHT = 1.0


def tile_offsets(row_len, plane_len):
    corner = jnp.arange(27, dtype=jnp.int32)
    return ((corner // 9) * row_len + (corner // 3) % 3) * plane_len + corner % 3


def particle_forces(values, gradients, stiffness):
    grad_disp = jnp.einsum('...inp,...jnp->...ijp', values, gradients, precision=lax.Precision.HIGHEST)
    strain_trace = grad_disp[..., 0, 0, :] + grad_disp[..., 1, 1, :] + grad_disp[..., 2, 2, :]
    first_lame = stiffness * (POISSON / ((1.0 + POISSON) * (1.0 - 2.0 * POISSON)))
    shear_mod = stiffness * (0.5 / (1.0 + POISSON))
    identity = jnp.eye(3, dtype=values.dtype).reshape(3, 3, 1)
    stress = shear_mod[..., None, None, :] * (grad_disp + jnp.swapaxes(grad_disp, -3, -2))
    stress = stress + identity * (first_lame * strain_trace)[..., None, None, :]
    return jnp.einsum('...ijp,...jnp->...inp', stress, gradients, precision=lax.Precision.HIGHEST)


def grid_from_padded(padded, mass_diag, coupling):
    center = padded[:, 1:-1, 1:-1, 1:-1]
    beside = padded[:, 2:, 1:-1, 1:-1] + padded[:, :-2, 1:-1, 1:-1]
    beside = beside + padded[:, 1:-1, 2:, 1:-1] + padded[:, 1:-1, :-2, 1:-1]
    beside = beside + padded[:, 1:-1, 1:-1, 2:] + padded[:, 1:-1, 1:-1, :-2]
    return mass_diag * center + coupling * (6.0 * center - beside)


def grid_whole(nodal, mass_diag, coupling):
    return grid_from_padded(jnp.pad(nodal, ((0, 0), (1, 1), (1, 1), (1, 1))), mass_diag, coupling)


def aggregate(nodal):
    dims_in = nodal.shape
    leading = dims_in[:-3]
    blocked = nodal.reshape(leading + (dims_in[-3] // 2, 2, dims_in[-2] // 2, 2, dims_in[-1] // 2, 2))
    return blocked.sum(axis=(-5, -3, -1))


def expand(nodal):
    return jnp.repeat(jnp.repeat(jnp.repeat(nodal, 2, axis=-3), 2, axis=-2), 2, axis=-1)


def vcycle(source, masses, depth_index):
    mass_diag = masses[depth_index]
    coupling = LAPLACE_WEIGHT * 2.0 ** depth_index
    diagonal = mass_diag + 6.0 * coupling
    estimate = DAMPING * source / diagonal
    if depth_index == len(masses) - 1:
        for sweep_index in range(SWEEPS - 1):
            estimate = estimate + DAMPING * (source - grid_whole(estimate, mass_diag, coupling)) / diagonal
        return estimate
    remainder = source - grid_whole(estimate, mass_diag, coupling)
    estimate = estimate + expand(vcycle(aggregate(remainder), masses, depth_index + 1))
    return estimate + DAMPING * (source - grid_whole(estimate, mass_diag, coupling)) / diagonal


def stiffness_apply(nodal, gradients, effective, node_base):
    span_y = NY + 2
    span_z = NZ + 2
    padded = jnp.pad(nodal, ((0, 0), (1, 1), (1, 1), (1, 1))).reshape(3, -1)
    local_z = node_base % (NZ + 2)
    quotient = node_base // (NZ + 2)
    local_y = quotient % (CY + 2)
    local_x = quotient // (CY + 2)
    brick_x = jnp.arange(N_GX, dtype=jnp.int32).reshape(N_GX, 1, 1, 1) * CX
    brick_y = jnp.arange(N_GY, dtype=jnp.int32).reshape(1, N_GY, 1, 1) * CY
    global_base = (((brick_x + local_x) * span_y + brick_y + local_y) * span_z + local_z).astype(jnp.int32)
    offsets = tile_offsets(span_y, span_z)

    def per_column(accumulated, column):
        base_col, grad_col, stiff_col = column
        tile_index = base_col[:, :, None, :] + offsets[None, None, :, None]
        values = jnp.moveaxis(padded[:, tile_index], 0, -3)
        forces = particle_forces(values, grad_col, stiff_col)
        accumulated = accumulated.at[:, tile_index].add(jnp.moveaxis(forces, -3, 0))
        return accumulated, None

    accumulated, unused = lax.scan(per_column, jnp.zeros_like(padded), (global_base, gradients, effective))
    return accumulated.reshape(3, NX + 2, NY + 2, NZ + 2)[:, 1:-1, 1:-1, 1:-1]


def reference(right_side, node_mass, gradients, stiffness, valid, node_base):
    masses = [node_mass, aggregate(node_mass), aggregate(aggregate(node_mass))]
    effective = stiffness * valid.astype(stiffness.dtype)

    def operator(nodal):
        return node_mass * nodal + stiffness_apply(nodal, gradients, effective, node_base)

    solution = jnp.zeros_like(right_side)
    residual = right_side
    precond = vcycle(residual, masses, 0)
    direction = precond
    inner_now = jnp.sum(residual * precond)
    for iteration in range(ITERS):
        applied = operator(direction)
        step_size = inner_now / jnp.sum(direction * applied)
        solution = solution + step_size * direction
        residual = residual - step_size * applied
        if iteration + 1 < ITERS:
            precond = vcycle(residual, masses, 0)
            inner_next = jnp.sum(residual * precond)
            direction = precond + (inner_next / inner_now) * direction
            inner_now = inner_next
    return solution, residual
```

```python
import functools

import jax
import jax.numpy as jnp
from jax import lax
from jax.experimental import pallas as pl
from jax.experimental.pallas import tpu as pltpu
from jax.sharding import PartitionSpec as P

POISSON = 0.3
DAMPING = 0.7
SWEEPS = 4
LANES = 128
BRICK = 4
AXES = ("gx", "gy")
VMEM_BYTES = 40 * 1024 * 1024
F32 = jnp.float32


def pairing_even(count):
    return [(i, i ^ 1) for i in range(count)]


def pairing_odd(count):
    return [(i, (i + 1) % count if i % 2 else (i - 1) % count) for i in range(count)]


def exchange(first, second, axis, count):
    return (
        lax.ppermute(first, axis, pairing_even(count)),
        lax.ppermute(second, axis, pairing_odd(count)),
    )


def lane_index():
    return lax.broadcasted_iota(jnp.int32, (1, LANES), 1)


def as_f32(cond):
    return jnp.where(cond, 1.0, 0.0).astype(F32)


def turn(x, shift):
    return pltpu.roll(x, shift % LANES, x.ndim - 1)


class Place:
    def __init__(self, count_x, count_y):
        self.gx = lax.axis_index("gx")
        self.gy = lax.axis_index("gy")
        self.count_x, self.count_y = count_x, count_y
        flag = lambda cond: jnp.where(cond, 1.0, 0.0).astype(F32)
        self.even_x = flag(self.gx % 2 == 0)
        self.even_y = flag(self.gy % 2 == 0)
        self.in_x = {-1: flag(self.gx > 0), 0: None, 1: flag(self.gx < count_x - 1)}
        self.in_y = {-1: flag(self.gy > 0), 0: None, 1: flag(self.gy < count_y - 1)}

    def keep(self, value, x, y, size):
        side_x = -1 if x < 0 else 1 if x >= size else 0
        side_y = -1 if y < 0 else 1 if y >= size else 0
        if side_x:
            value = value * self.in_x[side_x]
        if side_y:
            value = value * self.in_y[side_y]
        return value


class Shifts:
    def __init__(self):
        lane = lane_index()
        self.low = {d: as_f32(lane >= d) for d in (1, 2, 4)}
        self.high = {d: as_f32(lane < LANES - d) for d in (1, 2, 4)}
        self.even = as_f32(lane % 2 == 0)
        self.odd = 1.0 - self.even
        self.half = as_f32(lane % 4 < 2)

    def beside(self, x, d):
        return turn(x, d) * self.low[d] + turn(x, -d) * self.high[d]

    def pair_sum(self, x):
        t = (x + turn(x, -1)) * self.even
        return t + turn(t, 1)

    def quad_sum(self, x):
        t = (x + turn(x, -2)) * self.half
        return t + turn(t, 2)


def memo(fn):
    kept = {}

    def wrapped(x, y):
        if (x, y) not in kept:
            kept[(x, y)] = fn(x, y)
        return kept[(x, y)]

    return wrapped


def grid_apply(e, mass, coupling, shifts, step):
    def at(x, y):
        c = e(x, y)
        beside = e(x + 1, y) + e(x - 1, y) + e(x, y + 1) + e(x, y - 1) + shifts.beside(c, step)
        return mass(x, y) * c + coupling * (6.0 * c - beside)

    return at


def restriction(r, mass0, weight0, mass1, weight1, place, shifts):
    e0 = memo(lambda x, y: weight0(x, y) * r(x, y))
    g0 = grid_apply(e0, mass0, 1.0, shifts, 1)
    rem0 = memo(lambda x, y: r(x, y) - g0(x, y))

    def r1_at(x, y):
        total = rem0(2 * x, 2 * y) + rem0(2 * x + 1, 2 * y) + rem0(2 * x, 2 * y + 1) + rem0(2 * x + 1, 2 * y + 1)
        return place.keep(shifts.pair_sum(total), x, y, 2)

    r1 = memo(r1_at)
    e1 = memo(lambda x, y: weight1(x, y) * r1(x, y))
    g1 = grid_apply(e1, mass1, 2.0, shifts, 2)
    total = 0.0
    for x in range(2):
        for y in range(2):
            total = total + (r1(x, y) - g1(x, y))
    return r1, shifts.quad_sum(total)


def pack_slot(r1, r2_row, dots_row, shifts):
    top = r1(0, 0) * shifts.even + r1(0, 1) * shifts.odd
    low = r1(1, 0) * shifts.even + r1(1, 1) * shifts.odd
    return jnp.concatenate([top[0:3], r2_row, low[0:3], dots_row], axis=0)


def pack_quads(column):
    lane = lax.broadcasted_iota(jnp.int32, (4, LANES), 1)
    row = lax.broadcasted_iota(jnp.int32, (4, LANES), 0)
    return jnp.sum(column * as_f32(lane % 4 == row), axis=0, keepdims=True)


def unpack_quads(row):
    lane = lax.broadcasted_iota(jnp.int32, (4, LANES), 1)
    index = lax.broadcasted_iota(jnp.int32, (4, LANES), 0)
    x = jnp.broadcast_to(row, (4, LANES)) * as_f32(lane % 4 == index)
    return spread_quads(x, lane)


def spread_quads(x, lane):
    even = as_f32(lane % 2 == 0)
    odd = 1.0 - even
    x = x + turn(x, -1) * even + turn(x, 1) * odd
    half = as_f32(lane % 4 < 2)
    return x + turn(x, -2) * half + turn(x, 2) * (1.0 - half)


def coarse_solve(r2, m2, count_x, count_y):
    rows = count_x * count_y
    lane = lax.broadcasted_iota(jnp.int32, (rows, LANES), 1)
    row = lax.broadcasted_iota(jnp.int32, (rows, LANES), 0)
    column = row % count_y
    z_low, z_high = as_f32(lane >= 4), as_f32(lane < LANES - 4)
    x_low, x_high = as_f32(row >= count_y), as_f32(row < rows - count_y)
    y_low, y_high = as_f32(column > 0), as_f32(column < count_y - 1)
    up = lambda v, k: pltpu.roll(v, k % rows, 0)
    weight = DAMPING / (m2 + 24.0)
    e = weight * r2
    for _ in range(SWEEPS - 1):
        beside = turn(e, 4) * z_low + turn(e, -4) * z_high
        beside = beside + up(e, count_y) * x_low + up(e, -count_y) * x_high
        beside = beside + up(e, 1) * y_low + up(e, -1) * y_high
        e = e + weight * (r2 - (m2 * e + 4.0 * (6.0 * e - beside)))
    return e


def prolongation(r, r1, e2, mass0, weight0, mass1, weight1, place, shifts):
    e1 = memo(lambda x, y: weight1(x, y) * r1(x, y) + e2(x // 2, y // 2))
    g1 = grid_apply(e1, mass1, 2.0, shifts, 2)
    f1 = memo(lambda x, y: place.keep(e1(x, y) + weight1(x, y) * (r1(x, y) - g1(x, y)), x, y, 2))
    e0 = memo(lambda x, y: weight0(x, y) * r(x, y) + f1(x // 2, y // 2))
    g0 = grid_apply(e0, mass0, 1.0, shifts, 1)
    return memo(lambda x, y: place.keep(e0(x, y) + weight0(x, y) * (r(x, y) - g0(x, y)), x, y, BRICK))


def stiffness_apply(z, base_ref, stiff_ref, valid_ref, grad_ref, hot, stack, picked, spread_sums, shifts):
    blocks = grad_ref.shape[0]
    particles = blocks * LANES
    nodes = BRICK * BRICK * LANES

    base = base_ref[...]
    plane = base // (LANES + 2)
    depth = base - plane * (LANES + 2)
    node_xy = (plane // (BRICK + 2)) * BRICK + plane % (BRICK + 2)
    sub = lax.broadcasted_iota(jnp.int32, (LANES, LANES), 0)
    for s in range(blocks):
        depth_s, xy_s = depth[s : s + 1], node_xy[s : s + 1]
        for q in range(BRICK * BRICK):
            wanted = jnp.where(xy_s == q, depth_s, -1)
            hot[q * LANES : (q + 1) * LANES, s * LANES : (s + 1) * LANES] = as_f32(sub == wanted).astype(jnp.bfloat16)

    def halves(x):
        high = x.astype(jnp.bfloat16).astype(F32)
        return jnp.concatenate([high, x - high], axis=0)

    split = {}
    for x in range(BRICK + 2):
        for y in range(BRICK + 2):
            whole = halves(z(x - 1, y - 1))
            split[x, y, 1] = whole
            split[x, y, 0] = turn(whole, 1) * shifts.low[1]
            split[x, y, 2] = turn(whole, -1) * shifts.high[1]
    tiles = [(a, b, c) for a in range(3) for b in range(3) for c in range(3)]
    zero = jnp.zeros((8, LANES), F32)
    for i in range(BRICK):
        for j in range(BRICK):
            q = i * BRICK + j
            parts = [split[i + a, j + b, c] for a, b, c in tiles] + [zero]
            for t in range(0, 28, 2):
                pair = jnp.concatenate([parts[t], parts[t + 1]], axis=0).astype(jnp.bfloat16)
                stack[t * 8 : t * 8 + 16, q * LANES : (q + 1) * LANES] = pair
    picked[...] = jnp.dot(stack[...], hot[...], preferred_element_type=F32)

    first = POISSON / ((1.0 + POISSON) * (1.0 - 2.0 * POISSON))
    shear_of = 0.5 / (1.0 + POISSON)
    row4 = lax.broadcasted_iota(jnp.int32, (8, LANES), 0) % 4
    row_is = [as_f32(row4 == m) for m in range(3)]
    is_high = as_f32(lax.broadcasted_iota(jnp.int32, (8, LANES), 0) < 4)
    wide = lambda row: jnp.broadcast_to(row, (8, LANES))
    for s in range(blocks):
        lanes = slice(s * LANES, (s + 1) * LANES)
        grad = lambda l, t: wide(grad_ref[s, l, t : t + 1, :])
        h = [None] * 3
        for t in range(27):
            value = picked[t * 8 : t * 8 + 8, lanes]
            for l in range(3):
                term = value * grad(l, t)
                h[l] = term if h[l] is None else h[l] + term
        h = [x[0:4] + x[4:8] for x in h]
        h = [[h[l][m : m + 1] for l in range(3)] for m in range(3)]
        effective = stiff_ref[s : s + 1] * valid_ref[s : s + 1].astype(F32)
        shear = effective * shear_of
        bulk = effective * first * (h[0][0] + h[1][1] + h[2][2])
        stress = []
        for l in range(3):
            column = 0.0
            for m in range(3):
                entry = shear * (h[m][l] + h[l][m])
                if l == m:
                    entry = entry + bulk
                column = column + wide(entry) * row_is[m]
            stress.append(column)
        parts = []
        for t in range(28):
            if t < 27:
                f = stress[0] * grad(0, t) + stress[1] * grad(1, t) + stress[2] * grad(2, t)
                high = f.astype(jnp.bfloat16).astype(F32)
                parts.append(is_high * high + (1.0 - is_high) * (f - high))
            else:
                parts.append(zero)
            if t % 2:
                pair = jnp.concatenate(parts, axis=0).astype(jnp.bfloat16)
                stack[t * 8 - 8 : t * 8 + 8, lanes] = pair
                parts = []
    spread_sums[...] = lax.dot_general(
        stack[:, :particles], hot[...], (((1,), (1,)), ((), ())), preferred_element_type=F32
    )
    out = {}
    for x in range(BRICK + 2):
        for y in range(BRICK + 2):
            sums = [0.0, 0.0, 0.0]
            for t, (a, b, c) in enumerate(tiles):
                i, j = x - a, y - b
                if 0 <= i < BRICK and 0 <= j < BRICK:
                    q = i * BRICK + j
                    sums[c] = sums[c] + spread_sums[t * 8 : t * 8 + 8, q * LANES : (q + 1) * LANES]
            total = sums[1] + turn(sums[0], -1) * shifts.high[1] + turn(sums[2], 1) * shifts.low[1]
            out[x - 1, y - 1] = total[0:4] + total[4:8]
    return out


def start_kernel(counts, wide_ref, up_ref, down_ref, r_ref, mass0_ref, weight0_ref, mass1_ref, weight1_ref, slot_ref):
    place, shifts = Place(*counts), Shifts()
    below = (place.in_y[-1] * place.even_y, place.in_y[-1] * (1.0 - place.even_y))
    above = (place.in_y[1] * (1.0 - place.even_y), place.in_y[1] * place.even_y)

    def load(x, y):
        if 0 <= y < BRICK:
            return wide_ref[x + 4, y]
        odd, even = below if y < 0 else above
        return down_ref[x + 4, y % BRICK] * odd + up_ref[x + 4, y % BRICK] * even

    load = memo(load)
    live = as_f32(lax.broadcasted_iota(jnp.int32, (4, LANES), 0) < 3)
    r = memo(lambda x, y: load(x, y) * live)
    mass0 = memo(lambda x, y: jnp.broadcast_to(load(x, y)[3:4], (4, LANES)))
    weight0 = memo(lambda x, y: DAMPING / (mass0(x, y) + 6.0))

    def mass1_at(x, y):
        total = mass0(2 * x, 2 * y) + mass0(2 * x + 1, 2 * y) + mass0(2 * x, 2 * y + 1) + mass0(2 * x + 1, 2 * y + 1)
        return shifts.pair_sum(total)

    mass1 = memo(mass1_at)
    weight1 = memo(lambda x, y: DAMPING / (mass1(x, y) + 12.0))
    r1, r2 = restriction(r, mass0, weight0, mass1, weight1, place, shifts)
    m2 = shifts.quad_sum(mass1(0, 0) + mass1(0, 1) + mass1(1, 0) + mass1(1, 1))
    r2_row = pack_quads(jnp.concatenate([r2[0:3], m2[3:4]], axis=0))
    slot_ref[...] = pack_slot(r1, r2_row, jnp.zeros((1, LANES), F32), shifts)
    for x in range(-3, 7):
        for y in range(-3, 7):
            mass0_ref[x + 3, y + 3] = mass0(x, y)
            weight0_ref[x + 3, y + 3] = weight0(x, y)
            if -2 <= x < 6 and -2 <= y < 6:
                r_ref[x + 2, y + 2] = r(x, y)
    for x in range(-2, 4):
        for y in range(-2, 4):
            mass1_ref[x + 2, y + 2] = mass1(x, y)
            weight1_ref[x + 2, y + 2] = weight1(x, y)


def reader(ref, offset):
    return memo(lambda x, y: ref[x + offset, y + offset])


def cycle_and_apply(place, shifts, r, gathered, mass_rows, fields, particles, scratch):
    count_x, count_y = place.count_x, place.count_y
    mass0, weight0, mass1, weight1 = fields
    coarse, hot, stack, picked, spread_sums = scratch
    bricks = count_x * count_y
    r2 = gathered(3, bricks, 8)
    lane = lax.broadcasted_iota(jnp.int32, (bricks, LANES), 1)
    m2 = spread_quads(mass_rows * as_f32(lane % 4 == 3), lane)
    margin = coarse.shape[0] - bricks
    coarse[...] = jnp.zeros_like(coarse)
    coarse[margin // 2 : margin // 2 + bricks, :] = coarse_solve(r2, m2, count_x, count_y)

    def e2_at(x, y):
        row = (place.gx + x) * count_y + place.gy + y + margin // 2
        return place.keep(unpack_quads(coarse[pl.ds(row, 1), :]), x, y, 1)

    e2 = memo(e2_at)

    def neighbour(x, y):
        other_x = jnp.clip(place.gx + x, 0, count_x - 1)
        other_y = jnp.clip(place.gy + y, 0, count_y - 1)
        row = pl.multiple_of((other_x * count_y + other_y) * 8, 8)
        slot = gathered(row, 8, 1)
        first, second = slot * shifts.even, slot * shifts.odd
        return first + turn(first, 1), second + turn(second, -1)

    neighbour = memo(neighbour)

    def r1_at(x, y):
        both = neighbour(x // 2, y // 2)[y % 2]
        return place.keep(both[4 * (x % 2) : 4 * (x % 2) + 4], x, y, 2)

    r1 = memo(r1_at)
    live = as_f32(lax.broadcasted_iota(jnp.int32, (4, LANES), 0) < 3)
    full = prolongation(r, r1, e2, mass0, weight0, mass1, weight1, place, shifts)
    z = memo(lambda x, y: full(x, y) * live)
    image = stiffness_apply(z, *particles, hot, stack, picked, spread_sums, shifts)
    for x in range(BRICK):
        for y in range(BRICK):
            image[x, y] = image[x, y] + mass0(x, y) * z(x, y)
    return z, image


def total_of(pairs):
    acc = 0.0
    for a, b in pairs:
        acc = acc + a * b
    return jnp.sum(jnp.sum(acc, axis=0, keepdims=True), axis=1, keepdims=True)


def dots_row(*values):
    lane = lane_index()
    row = 0.0
    for k, v in enumerate(values):
        row = row + as_f32(lane == k) * v
    return row


INNER = [(x, y) for x in range(BRICK) for y in range(BRICK)]
RIMMED = [(x, y) for x in range(-1, BRICK + 1) for y in range(-1, BRICK + 1)]


def first_kernel(counts, level_ref, r_ref, mass0_ref, weight0_ref, mass1_ref, weight1_ref,
                 base_ref, stiff_ref, valid_ref, grad_ref, z_ref, image_ref, even_ref, odd_ref, dots_ref, *scratch):
    place, shifts = Place(*counts), Shifts()
    r = reader(r_ref, 2)
    gathered = lambda start, size, stride: level_ref[pl.ds(start, size, stride=stride) if stride > 1 else pl.ds(start, size), :]
    fields = (reader(mass0_ref, 3), reader(weight0_ref, 3), reader(mass1_ref, 2), reader(weight1_ref, 2))
    mass_rows = gathered(3, counts[0] * counts[1], 8)
    particles = (base_ref, stiff_ref, valid_ref, grad_ref)
    z, image = cycle_and_apply(place, shifts, r, gathered, mass_rows, fields, particles, scratch)
    for x, y in INNER:
        z_ref[x, y] = z(x, y)
    for x, y in RIMMED:
        image_ref[x + 1, y + 1] = image[x, y]
    even = place.even_x
    for k in range(4):
        for y in range(-1, BRICK + 1):
            right, left = image[k + 1, y], image[k - 1, y]
            even_ref[k, y + 1] = right * even + left * (1.0 - even)
            odd_ref[k, y + 1] = left * even + right * (1.0 - even)
    rz = total_of((r(x, y), z(x, y)) for x, y in INNER)
    zaz = total_of((image[x, y], z(x, y)) for x, y in RIMMED)
    dots_ref[...] = dots_row(rz, zaz)


def along_x_kernel(counts, image_ref, even_ref, odd_ref, wide_ref, up_ref, down_ref):
    place = Place(*counts)
    left_of = (place.in_x[-1] * place.even_x, place.in_x[-1] * (1.0 - place.even_x))
    right_of = (place.in_x[1] * (1.0 - place.even_x), place.in_x[1] * place.even_x)

    def value(x, y):
        total = None
        if -1 <= x <= 4:
            total = place.keep(image_ref[x + 1, y + 1], x, 0, BRICK)
        if x <= 0:
            part = odd_ref[x + 3, y + 1] * left_of[0] + even_ref[x + 3, y + 1] * left_of[1]
            total = part if total is None else total + part
        if x >= 3:
            part = odd_ref[x - 3, y + 1] * right_of[0] + even_ref[x - 3, y + 1] * right_of[1]
            total = part if total is None else total + part
        return total

    value = memo(value)
    even = place.even_y
    for x in range(-3, 7):
        for y in range(-1, BRICK + 1):
            wide_ref[x + 3, y + 1] = value(x, y)
        for k in range(4):
            above, below = value(x, k + 1), value(x, k - 1)
            up_ref[x + 3, k] = above * even + below * (1.0 - even)
            down_ref[x + 3, k] = below * even + above * (1.0 - even)


def middle_kernel(counts, wide_ref, up_ref, down_ref, mass0_ref, weight0_ref, mass1_ref, weight1_ref, dots_ref,
                  w_ref, slot_ref):
    place, shifts = Place(*counts), Shifts()
    below = (place.in_y[-1] * place.even_y, place.in_y[-1] * (1.0 - place.even_y))
    above = (place.in_y[1] * (1.0 - place.even_y), place.in_y[1] * place.even_y)

    def value(x, y):
        total = None
        if -1 <= y <= 4:
            total = place.keep(wide_ref[x + 3, y + 1], 0, y, BRICK)
        if y <= 0:
            part = down_ref[x + 3, y + 3] * below[0] + up_ref[x + 3, y + 3] * below[1]
            total = part if total is None else total + part
        if y >= 3:
            part = down_ref[x + 3, y - 3] * above[0] + up_ref[x + 3, y - 3] * above[1]
            total = part if total is None else total + part
        return total

    w = memo(value)
    r1, r2 = restriction(w, reader(mass0_ref, 3), reader(weight0_ref, 3), reader(mass1_ref, 2), reader(weight1_ref, 2),
                         place, shifts)
    slot_ref[...] = pack_slot(r1, pack_quads(r2), dots_ref[...], shifts)
    for x in range(-2, 6):
        for y in range(-2, 6):
            w_ref[x + 2, y + 2] = w(x, y)


def sums_of(ref, count, first, stride):
    return jnp.sum(ref[pl.ds(first, count, stride=stride), :], axis=0, keepdims=True)


def second_kernel(counts, level_ref, change_ref, r_ref, w_ref, mass0_ref, weight0_ref, mass1_ref, weight1_ref,
                  base_ref, stiff_ref, valid_ref, grad_ref, z_ref, image_ref, slots_ref, *scratch):
    place, shifts = Place(*counts), Shifts()
    bricks = counts[0] * counts[1]
    sums = sums_of(change_ref, bricks, 7, 8)
    step = sums[:, 0:1] / sums[:, 1:2]
    r = memo(lambda x, y: r_ref[x + 2, y + 2] - step * w_ref[x + 2, y + 2])

    def gathered(start, size, stride):
        rows = pl.ds(start, size, stride=stride) if stride > 1 else pl.ds(start, size)
        return level_ref[rows, :] - step * change_ref[rows, :]

    mass_rows = level_ref[pl.ds(3, bricks, stride=8), :]
    fields = (reader(mass0_ref, 3), reader(weight0_ref, 3), reader(mass1_ref, 2), reader(weight1_ref, 2))
    particles = (base_ref, stiff_ref, valid_ref, grad_ref)
    z, image = cycle_and_apply(place, shifts, r, gathered, mass_rows, fields, particles, scratch)
    for x, y in INNER:
        z_ref[x, y] = z(x, y)
        image_ref[x, y] = image[x, y]
    rz = total_of((r(x, y), z(x, y)) for x, y in INNER)
    zaz = total_of((image[x, y], z(x, y)) for x, y in RIMMED)
    zw = total_of((w_ref[x + 2, y + 2], z(x, y)) for x, y in INNER)
    row = dots_row(rz, zaz, zw)
    filled = jnp.concatenate([jnp.zeros((3, LANES), F32), row] + [jnp.zeros((4, LANES), F32)] * 3, axis=0)

    def fill(k, carry):
        slots_ref[k] = filled
        return carry

    lax.fori_loop(0, bricks, fill, 0)
    for dx in (-1, 0, 1):
        for dy in (-1, 0, 1):
            if dx == 0 and dy == 0:
                continue
            xs = [-1] if dx < 0 else [BRICK] if dx > 0 else range(BRICK)
            ys = [-1] if dy < 0 else [BRICK] if dy > 0 else range(BRICK)
            columns = [image[x, y] for x in xs for y in ys]
            there_x = (place.gx + dx >= 0) & (place.gx + dx < counts[0])
            there_y = (place.gy + dy >= 0) & (place.gy + dy < counts[1])

            @pl.when(there_x & there_y)
            def _(columns=columns, dx=dx, dy=dy):
                other = (place.gx + dx) * counts[1] + place.gy + dy
                for k, column in enumerate(columns):
                    slots_ref[other, 4 * k : 4 * k + 3, :] = column[0:3]


def last_kernel(counts, slots_ref, change_ref, z1_ref, z2_ref, r_ref, w_ref, image_ref, solution_ref, residual_ref):
    place = Place(*counts)
    bricks = counts[0] * counts[1]
    sums1 = sums_of(change_ref, bricks, 7, 8)
    sums2 = sums_of(slots_ref, bricks, 3, 16)
    rz1, zaz1 = sums1[:, 0:1], sums1[:, 1:2]
    rz2, zaz2, zw = sums2[:, 0:1], sums2[:, 1:2], sums2[:, 2:3]
    step1 = rz1 / zaz1
    ratio = rz2 / rz1
    step2 = rz2 / (zaz2 + 2.0 * ratio * zw + ratio * ratio * zaz1)
    image = {(x, y): image_ref[x, y] for x, y in INNER}
    for dx in (-1, 0, 1):
        for dy in (-1, 0, 1):
            if dx == 0 and dy == 0:
                continue
            xs = [0] if dx < 0 else [BRICK - 1] if dx > 0 else range(BRICK)
            ys = [0] if dy < 0 else [BRICK - 1] if dy > 0 else range(BRICK)
            other_x = jnp.clip(place.gx + dx, 0, counts[0] - 1)
            other_y = jnp.clip(place.gy + dy, 0, counts[1] - 1)
            row = pl.multiple_of((other_x * counts[1] + other_y) * 16, 16)
            block = slots_ref[pl.ds(row, 16), :]
            for k, (x, y) in enumerate((x, y) for x in xs for y in ys):
                image[x, y] = image[x, y] + place.keep(block[4 * k : 4 * k + 4], dx, dy, 1)
    for x, y in INNER:
        w = w_ref[x + 2, y + 2]
        z1 = z1_ref[x, y]
        solution = step1 * z1 + step2 * (z2_ref[x, y] + ratio * z1)
        residual = r_ref[x + 2, y + 2] - step1 * w - step2 * (image[x, y] + ratio * w)
        for m in range(3):
            solution_ref[m, x, y : y + 1, :] = solution[m : m + 1]
            residual_ref[m, x, y : y + 1, :] = residual[m : m + 1]


def call(kernel, counts, shapes, *args, scratch=()):
    out = [jax.ShapeDtypeStruct(s, F32) for s in shapes]
    return pl.pallas_call(
        functools.partial(kernel, counts),
        out_shape=out,
        scratch_shapes=scratch,
        compiler_params=pltpu.CompilerParams(vmem_limit_bytes=VMEM_BYTES),
    )(*args)


def per_device(counts, right_side, node_mass, gradients, stiffness, valid, node_base):
    count_x, count_y = counts
    bricks = count_x * count_y
    blocks = gradients.shape[2]
    particles = (node_base[0, 0], stiffness[0, 0], valid[0, 0], gradients[0, 0])
    nodes = BRICK * BRICK * LANES
    scratch = (
        pltpu.VMEM((bricks + 2 * (8 + count_y), LANES), F32),
        pltpu.VMEM((nodes, blocks * LANES), jnp.bfloat16),
        pltpu.VMEM((224, nodes), jnp.bfloat16),
        pltpu.VMEM((224, blocks * LANES), F32),
        pltpu.VMEM((224, nodes), F32),
    )
    gx, gy = lax.axis_index("gx"), lax.axis_index("gy")

    own = jnp.concatenate([right_side, node_mass[None]], axis=0).transpose(1, 2, 0, 3)
    even, odd = exchange(own, own, "gx", count_x)
    is_even = gx % 2 == 0
    left = jnp.where(gx > 0, jnp.where(is_even, odd, even), 0.0)
    right = jnp.where(gx < count_x - 1, jnp.where(is_even, even, odd), 0.0)
    wide = jnp.concatenate([left, own, right], axis=0)
    up, down = exchange(wide, wide, "gy", count_y)
    r, *fields, slot = call(
        start_kernel, counts,
        [(8, 8, 4, LANES), (10, 10, 4, LANES), (10, 10, 4, LANES), (6, 6, 4, LANES), (6, 6, 4, LANES), (8, LANES)],
        wide, up, down,
    )

    def share(slot):
        sent = jnp.broadcast_to(slot[None], (bricks, 8, LANES))
        return lax.all_to_all(sent, AXES, 0, 0).reshape(bricks * 8, LANES)

    level = share(slot)
    z1, image, to_even, to_odd, dots = call(
        first_kernel, counts,
        [(4, 4, 4, LANES), (6, 6, 4, LANES), (4, 6, 4, LANES), (4, 6, 4, LANES), (1, LANES)],
        level, r, *fields, *particles, scratch=scratch,
    )
    even, odd = exchange(to_even, to_odd, "gx", count_x)
    wide, to_up, to_down = call(
        along_x_kernel, counts, [(10, 6, 4, LANES), (10, 4, 4, LANES), (10, 4, 4, LANES)], image, even, odd
    )
    up, down = exchange(to_up, to_down, "gy", count_y)
    w, slot = call(middle_kernel, counts, [(8, 8, 4, LANES), (8, LANES)], wide, up, down, *fields, dots)
    change = share(slot)
    z2, image, slots = call(
        second_kernel, counts, [(4, 4, 4, LANES), (4, 4, 4, LANES), (bricks, 16, LANES)],
        level, change, r, w, *fields, *particles, scratch=scratch,
    )
    slots = lax.all_to_all(slots, AXES, 0, 0).reshape(bricks * 16, LANES)
    return tuple(
        call(last_kernel, counts, [right_side.shape, right_side.shape], slots, change, z1, z2, r, w, image)
    )


def solution(mesh):
    counts = (mesh.shape["gx"], mesh.shape["gy"])
    return jax.shard_map(
        functools.partial(per_device, counts),
        mesh=mesh,
        in_specs=(
            P(None, "gx", "gy", None),
            P("gx", "gy", None),
            P("gx", "gy", None, None, None, None),
            P("gx", "gy", None, None),
            P("gx", "gy", None, None),
            P("gx", "gy", None, None),
        ),
        out_specs=(P(None, "gx", "gy", None), P(None, "gx", "gy", None)),
        check_vma=False,
    )
```

```python
import functools

import jax
import jax.numpy as jnp
from jax import lax
from jax.experimental import pallas as pl
from jax.experimental.pallas import tpu as pltpu
from jax.sharding import PartitionSpec as P

POISSON = 0.3
DAMPING = 0.7
SWEEPS = 4
LANES = 128
BRICK = 4
AXES = ("gx", "gy")
VMEM_BYTES = 24 * 1024 * 1024
F32 = jnp.float32


def pairings(axis, counts):
    count_x, count_y = counts
    even, odd = [], []
    for x in range(count_x):
        for y in range(count_y):
            k, count = (x, count_x) if axis == "gx" else (y, count_y)
            move = lambda to: (to, y) if axis == "gx" else (x, to)
            even.append(((x, y), move(k ^ 1)))
            if 0 < k < count - 1:
                odd.append(((x, y), move(k + 1 if k % 2 else k - 1)))
            else:
                odd.append(((x, y), (x, y ^ 1) if axis == "gx" else (x ^ 1, y)))
    flat = lambda pairs: [(a * count_y + b, c * count_y + d) for (a, b), (c, d) in pairs]
    return flat(even), flat(odd)


def exchange(first, second, axis, counts):
    even, odd = pairings(axis, counts)
    return lax.ppermute(first, AXES, even), lax.ppermute(second, AXES, odd)


SIDE = (
    [(x, -1) for x in range(-2, 6)] + [(x, -2) for x in range(-1, 5)] + [(x, -3) for x in range(4)]
)
SIDE_MASS = [(x, y) for y in (-1, -2) for x in range(-4, 8)] + [(x, y) for y in (-3, -4) for x in range(-2, 6)]
SIDE_IMAGE = [(x, 0) for x in range(-3, 7)] + SIDE
SIDE_X = [(x, y) for x in range(-3, 1) for y in range(-1, 5)]


def mirror(x, y):
    return x, BRICK - 1 - y


def mirror_x(x, y):
    return BRICK - 1 - x, y


def lane_index():
    return lax.broadcasted_iota(jnp.int32, (1, LANES), 1)


def as_f32(cond):
    return jnp.where(cond, 1.0, 0.0).astype(F32)


def turn(x, shift):
    return pltpu.roll(x, shift % LANES, x.ndim - 1)


class Place:
    def __init__(self, count_x, count_y):
        self.gx = lax.axis_index("gx")
        self.gy = lax.axis_index("gy")
        self.count_x, self.count_y = count_x, count_y
        flag = lambda cond: jnp.where(cond, 1.0, 0.0).astype(F32)
        self.even_x = flag(self.gx % 2 == 0)
        self.even_y = flag(self.gy % 2 == 0)
        self.in_x = {-1: flag(self.gx > 0), 0: None, 1: flag(self.gx < count_x - 1)}
        self.in_y = {-1: flag(self.gy > 0), 0: None, 1: flag(self.gy < count_y - 1)}

    def keep(self, value, x, y, size):
        side_x = -1 if x < 0 else 1 if x >= size else 0
        side_y = -1 if y < 0 else 1 if y >= size else 0
        if side_x:
            value = value * self.in_x[side_x]
        if side_y:
            value = value * self.in_y[side_y]
        return value


class Shifts:
    def __init__(self):
        lane = lane_index()
        self.low = {d: as_f32(lane >= d) for d in (1, 2, 4)}
        self.high = {d: as_f32(lane < LANES - d) for d in (1, 2, 4)}
        self.even = as_f32(lane % 2 == 0)
        self.odd = 1.0 - self.even
        self.half = as_f32(lane % 4 < 2)

    def beside(self, x, d):
        return turn(x, d) * self.low[d] + turn(x, -d) * self.high[d]

    def pair_sum(self, x):
        t = (x + turn(x, -1)) * self.even
        return t + turn(t, 1)

    def quad_sum(self, x):
        t = (x + turn(x, -2)) * self.half
        return t + turn(t, 2)


def memo(fn):
    kept = {}

    def wrapped(x, y):
        if (x, y) not in kept:
            kept[(x, y)] = fn(x, y)
        return kept[(x, y)]

    return wrapped


def grid_apply(e, mass, coupling, shifts, step):
    def at(x, y):
        c = e(x, y)
        beside = e(x + 1, y) + e(x - 1, y) + e(x, y + 1) + e(x, y - 1) + shifts.beside(c, step)
        return mass(x, y) * c + coupling * (6.0 * c - beside)

    return at


def restriction(r, mass0, weight0, mass1, weight1, place, shifts):
    e0 = memo(lambda x, y: weight0(x, y) * r(x, y))
    g0 = grid_apply(e0, mass0, 1.0, shifts, 1)
    rem0 = memo(lambda x, y: r(x, y) - g0(x, y))

    def r1_at(x, y):
        total = rem0(2 * x, 2 * y) + rem0(2 * x + 1, 2 * y) + rem0(2 * x, 2 * y + 1) + rem0(2 * x + 1, 2 * y + 1)
        return place.keep(shifts.pair_sum(total), x, y, 2)

    r1 = memo(r1_at)
    e1 = memo(lambda x, y: weight1(x, y) * r1(x, y))
    g1 = grid_apply(e1, mass1, 2.0, shifts, 2)
    total = 0.0
    for x in range(2):
        for y in range(2):
            total = total + (r1(x, y) - g1(x, y))
    return r1, shifts.quad_sum(total)


def pack_slot(r1, r2_row, dots_row, shifts):
    top = r1(0, 0) * shifts.even + r1(0, 1) * shifts.odd
    low = r1(1, 0) * shifts.even + r1(1, 1) * shifts.odd
    return jnp.concatenate([top[0:3], r2_row, low[0:3], dots_row], axis=0)


def pack_quads(column):
    lane = lax.broadcasted_iota(jnp.int32, (4, LANES), 1)
    row = lax.broadcasted_iota(jnp.int32, (4, LANES), 0)
    return jnp.sum(column * as_f32(lane % 4 == row), axis=0, keepdims=True)


def unpack_quads(row):
    lane = lax.broadcasted_iota(jnp.int32, (4, LANES), 1)
    index = lax.broadcasted_iota(jnp.int32, (4, LANES), 0)
    x = jnp.broadcast_to(row, (4, LANES)) * as_f32(lane % 4 == index)
    return spread_quads(x, lane)


def spread_quads(x, lane):
    even = as_f32(lane % 2 == 0)
    odd = 1.0 - even
    x = x + turn(x, -1) * even + turn(x, 1) * odd
    half = as_f32(lane % 4 < 2)
    return x + turn(x, -2) * half + turn(x, 2) * (1.0 - half)


def coarse_solve(r2, m2, count_x, count_y):
    rows = count_x * count_y
    lane = lax.broadcasted_iota(jnp.int32, (rows, LANES), 1)
    row = lax.broadcasted_iota(jnp.int32, (rows, LANES), 0)
    column = row % count_y
    z_low, z_high = as_f32(lane >= 4), as_f32(lane < LANES - 4)
    x_low, x_high = as_f32(row >= count_y), as_f32(row < rows - count_y)
    y_low, y_high = as_f32(column > 0), as_f32(column < count_y - 1)
    up = lambda v, k: pltpu.roll(v, k % rows, 0)
    weight = DAMPING / (m2 + 24.0)
    e = weight * r2
    for _ in range(SWEEPS - 1):
        beside = turn(e, 4) * z_low + turn(e, -4) * z_high
        beside = beside + up(e, count_y) * x_low + up(e, -count_y) * x_high
        beside = beside + up(e, 1) * y_low + up(e, -1) * y_high
        e = e + weight * (r2 - (m2 * e + 4.0 * (6.0 * e - beside)))
    return e


def prolongation(r, r1, e2, mass0, weight0, mass1, weight1, place, shifts):
    e1 = memo(lambda x, y: weight1(x, y) * r1(x, y) + e2(x // 2, y // 2))
    g1 = grid_apply(e1, mass1, 2.0, shifts, 2)
    f1 = memo(lambda x, y: place.keep(e1(x, y) + weight1(x, y) * (r1(x, y) - g1(x, y)), x, y, 2))
    e0 = memo(lambda x, y: weight0(x, y) * r(x, y) + f1(x // 2, y // 2))
    g0 = grid_apply(e0, mass0, 1.0, shifts, 1)
    return memo(lambda x, y: place.keep(e0(x, y) + weight0(x, y) * (r(x, y) - g0(x, y)), x, y, BRICK))


def one_hot_kernel(counts, base_ref, grad_in_ref, hot_ref, grad_ref):
    grad_ref[...] = grad_in_ref[...]
    base = base_ref[...]
    plane = base // (LANES + 2)
    depth = base - plane * (LANES + 2)
    node_xy = (plane // (BRICK + 2)) * BRICK + plane % (BRICK + 2)
    sub = lax.broadcasted_iota(jnp.int32, (LANES, LANES), 0)
    for s in range(base_ref.shape[0]):
        depth_s, xy_s = depth[s : s + 1], node_xy[s : s + 1]
        for q in range(BRICK * BRICK):
            wanted = jnp.where(xy_s == q, depth_s, -1)
            hot_ref[q * LANES : (q + 1) * LANES, s * LANES : (s + 1) * LANES] = as_f32(sub == wanted).astype(jnp.bfloat16)


def stiffness_apply(z, hot, stiff_ref, valid_ref, grad_ref, stack, picked, spread_sums, shifts):
    blocks = grad_ref.shape[0]
    particles = blocks * LANES

    def halves(x):
        high = x.astype(jnp.bfloat16).astype(F32)
        return jnp.concatenate([high, x - high], axis=0)

    split = {}
    for x in range(BRICK + 2):
        for y in range(BRICK + 2):
            whole = halves(z(x - 1, y - 1))
            split[x, y, 1] = whole
            split[x, y, 0] = turn(whole, 1) * shifts.low[1]
            split[x, y, 2] = turn(whole, -1) * shifts.high[1]
    tiles = [(a, b, c) for a in range(3) for b in range(3) for c in range(3)]
    zero = jnp.zeros((8, LANES), F32)
    for i in range(BRICK):
        for j in range(BRICK):
            q = i * BRICK + j
            parts = [split[i + a, j + b, c] for a, b, c in tiles] + [zero]
            for t in range(0, 28, 2):
                pair = jnp.concatenate([parts[t], parts[t + 1]], axis=0).astype(jnp.bfloat16)
                stack[t * 8 : t * 8 + 16, q * LANES : (q + 1) * LANES] = pair
    picked[...] = jnp.dot(stack[...], hot[...], preferred_element_type=F32)

    first = POISSON / ((1.0 + POISSON) * (1.0 - 2.0 * POISSON))
    shear_of = 0.5 / (1.0 + POISSON)
    row4 = lax.broadcasted_iota(jnp.int32, (8, LANES), 0) % 4
    row_is = [as_f32(row4 == m) for m in range(3)]
    is_high = as_f32(lax.broadcasted_iota(jnp.int32, (8, LANES), 0) < 4)
    wide = lambda row: jnp.broadcast_to(row, (8, LANES))
    for s in range(blocks):
        lanes = slice(s * LANES, (s + 1) * LANES)
        grad = lambda l, t: wide(grad_ref[s, l, t : t + 1, :])
        h = [None] * 3
        for t in range(27):
            value = picked[t * 8 : t * 8 + 8, lanes]
            for l in range(3):
                term = value * grad(l, t)
                h[l] = term if h[l] is None else h[l] + term
        h = [x[0:4] + x[4:8] for x in h]
        h = [[h[l][m : m + 1] for l in range(3)] for m in range(3)]
        effective = stiff_ref[s : s + 1] * valid_ref[s : s + 1].astype(F32)
        shear = effective * shear_of
        bulk = effective * first * (h[0][0] + h[1][1] + h[2][2])
        stress = []
        for l in range(3):
            column = 0.0
            for m in range(3):
                entry = shear * (h[m][l] + h[l][m])
                if l == m:
                    entry = entry + bulk
                column = column + wide(entry) * row_is[m]
            stress.append(column)
        parts = []
        for t in range(28):
            if t < 27:
                f = stress[0] * grad(0, t) + stress[1] * grad(1, t) + stress[2] * grad(2, t)
                high = f.astype(jnp.bfloat16).astype(F32)
                parts.append(is_high * high + (1.0 - is_high) * (f - high))
            else:
                parts.append(zero)
            if t % 2:
                pair = jnp.concatenate(parts, axis=0).astype(jnp.bfloat16)
                stack[t * 8 - 8 : t * 8 + 8, lanes] = pair
                parts = []
    spread_sums[...] = lax.dot_general(
        stack[:, :particles], hot[...], (((1,), (1,)), ((), ())), preferred_element_type=F32
    )
    out = {}
    for x in range(BRICK + 2):
        for y in range(BRICK + 2):
            sums = [0.0, 0.0, 0.0]
            for t, (a, b, c) in enumerate(tiles):
                i, j = x - a, y - b
                if 0 <= i < BRICK and 0 <= j < BRICK:
                    q = i * BRICK + j
                    sums[c] = sums[c] + spread_sums[t * 8 : t * 8 + 8, q * LANES : (q + 1) * LANES]
            total = sums[1] + turn(sums[0], -1) * shifts.high[1] + turn(sums[2], 1) * shifts.low[1]
            out[x - 1, y - 1] = total[0:4] + total[4:8]
    return out


def side_parts(even_ref, odd_ref, is_even, inside_low, inside_high):
    odd = 1.0 - is_even
    below_odd, below_even = inside_low * is_even, inside_low * odd
    above_odd, above_even = inside_high * odd, inside_high * is_even

    def below(row, size):
        return odd_ref[row : row + size, :] * below_odd + even_ref[row : row + size, :] * below_even

    def above(row, size):
        return odd_ref[row : row + size, :] * above_odd + even_ref[row : row + size, :] * above_even

    return below, above


def put_sides(to_even_ref, to_odd_ref, row, size, up, down, is_even):
    odd = 1.0 - is_even
    to_even_ref[row : row + size, :] = (up * is_even + down * odd)[0:size]
    to_odd_ref[row : row + size, :] = (down * is_even + up * odd)[0:size]


def clear_tail(*refs):
    for ref in refs:
        ref[ref.shape[0] - 8 :, :] = jnp.zeros((8, LANES), F32)


def widen_kernel(counts, own_ref, even_ref, odd_ref, wide_ref, to_even_ref, to_odd_ref):
    place = Place(*counts)
    odd_x = 1.0 - place.even_x
    left = (place.in_x[-1] * place.even_x, place.in_x[-1] * odd_x)
    right = (place.in_x[1] * odd_x, place.in_x[1] * place.even_x)

    def value(x, y):
        if 0 <= x < BRICK:
            return own_ref[x, y]
        odd, even = left if x < 0 else right
        return odd_ref[x % BRICK, y] * odd + even_ref[x % BRICK, y] * even

    value = memo(value)
    for x in range(-4, 8):
        for y in range(BRICK):
            wide_ref[x + 4, y] = value(x, y)
    clear_tail(to_even_ref, to_odd_ref)
    for k, (x, y) in enumerate(SIDE):
        put_sides(to_even_ref, to_odd_ref, 3 * k, 3, value(x, y + 4), value(x, -1 - y), place.even_y)
    first = 3 * len(SIDE)
    for k, (x, y) in enumerate(SIDE_MASS):
        put_sides(to_even_ref, to_odd_ref, first + k, 1, value(x, y + 4)[3:4], value(x, -1 - y)[3:4], place.even_y)


def start_kernel(counts, wide_ref, even_ref, odd_ref, r_ref, mass0_ref, weight0_ref, mass1_ref, weight1_ref, slot_ref):
    place, shifts = Place(*counts), Shifts()
    below, above = side_parts(even_ref, odd_ref, place.even_y, place.in_y[-1], place.in_y[1])
    live = as_f32(lax.broadcasted_iota(jnp.int32, (4, LANES), 0) < 3)
    zero = jnp.zeros((4, LANES), F32)

    def r_at(x, y):
        if 0 <= y < BRICK:
            return wide_ref[x + 4, y] * live
        part = below if y < 0 else above
        key = (x, y) if y < 0 else mirror(x, y)
        return part(3 * SIDE.index(key), 4) * live if key in SIDE else zero

    def mass0_at(x, y):
        if 0 <= y < BRICK:
            return jnp.broadcast_to(wide_ref[x + 4, y, 3:4, :], (4, LANES))
        part = below if y < 0 else above
        key = (x, y) if y < 0 else mirror(x, y)
        if key not in SIDE_MASS:
            return zero
        return jnp.broadcast_to(part(3 * len(SIDE) + SIDE_MASS.index(key), 1), (4, LANES))

    r, mass0 = memo(r_at), memo(mass0_at)
    weight0 = memo(lambda x, y: DAMPING / (mass0(x, y) + 6.0))

    def mass1_at(x, y):
        total = mass0(2 * x, 2 * y) + mass0(2 * x + 1, 2 * y) + mass0(2 * x, 2 * y + 1) + mass0(2 * x + 1, 2 * y + 1)
        return shifts.pair_sum(total)

    mass1 = memo(mass1_at)
    weight1 = memo(lambda x, y: DAMPING / (mass1(x, y) + 12.0))
    r1, r2 = restriction(r, mass0, weight0, mass1, weight1, place, shifts)
    m2 = shifts.quad_sum(mass1(0, 0) + mass1(0, 1) + mass1(1, 0) + mass1(1, 1))
    r2_row = pack_quads(jnp.concatenate([r2[0:3], m2[3:4]], axis=0))
    slot_ref[...] = pack_slot(r1, r2_row, jnp.zeros((1, LANES), F32), shifts)
    for x in range(-3, 7):
        for y in range(-3, 7):
            mass0_ref[x + 3, y + 3] = mass0(x, y)
            weight0_ref[x + 3, y + 3] = weight0(x, y)
            if -2 <= x < 6 and -2 <= y < 6:
                r_ref[x + 2, y + 2] = r(x, y)
    for x in range(-2, 4):
        for y in range(-2, 4):
            mass1_ref[x + 2, y + 2] = mass1(x, y)
            weight1_ref[x + 2, y + 2] = weight1(x, y)


def reader(ref, offset):
    return memo(lambda x, y: ref[x + offset, y + offset])


def cycle_and_apply(place, shifts, r, gathered, mass_rows, fields, particles, scratch):
    count_x, count_y = place.count_x, place.count_y
    mass0, weight0, mass1, weight1 = fields
    coarse, stack, picked, spread_sums = scratch
    bricks = count_x * count_y
    r2 = gathered(3, bricks, 8)
    lane = lax.broadcasted_iota(jnp.int32, (bricks, LANES), 1)
    m2 = spread_quads(mass_rows * as_f32(lane % 4 == 3), lane)
    margin = coarse.shape[0] - bricks
    coarse[...] = jnp.zeros_like(coarse)
    coarse[margin // 2 : margin // 2 + bricks, :] = coarse_solve(r2, m2, count_x, count_y)

    def e2_at(x, y):
        row = (place.gx + x) * count_y + place.gy + y + margin // 2
        return place.keep(unpack_quads(coarse[pl.ds(row, 1), :]), x, y, 1)

    e2 = memo(e2_at)

    def neighbour(x, y):
        other_x = jnp.clip(place.gx + x, 0, count_x - 1)
        other_y = jnp.clip(place.gy + y, 0, count_y - 1)
        row = pl.multiple_of((other_x * count_y + other_y) * 8, 8)
        slot = gathered(row, 8, 1)
        first, second = slot * shifts.even, slot * shifts.odd
        return first + turn(first, 1), second + turn(second, -1)

    neighbour = memo(neighbour)

    def r1_at(x, y):
        both = neighbour(x // 2, y // 2)[y % 2]
        return place.keep(both[4 * (x % 2) : 4 * (x % 2) + 4], x, y, 2)

    r1 = memo(r1_at)
    live = as_f32(lax.broadcasted_iota(jnp.int32, (4, LANES), 0) < 3)
    full = prolongation(r, r1, e2, mass0, weight0, mass1, weight1, place, shifts)
    z = memo(lambda x, y: full(x, y) * live)
    image = stiffness_apply(z, *particles, stack, picked, spread_sums, shifts)
    for x in range(BRICK):
        for y in range(BRICK):
            image[x, y] = image[x, y] + mass0(x, y) * z(x, y)
    return z, image


def total_of(pairs):
    acc = 0.0
    for a, b in pairs:
        acc = acc + a * b
    return jnp.sum(jnp.sum(acc, axis=0, keepdims=True), axis=1, keepdims=True)


def dots_row(*values):
    lane = lane_index()
    row = 0.0
    for k, v in enumerate(values):
        row = row + as_f32(lane == k) * v
    return row


INNER = [(x, y) for x in range(BRICK) for y in range(BRICK)]
RIMMED = [(x, y) for x in range(-1, BRICK + 1) for y in range(-1, BRICK + 1)]


def first_kernel(counts, level_ref, r_ref, mass0_ref, weight0_ref, mass1_ref, weight1_ref,
                 hot_ref, stiff_ref, valid_ref, grad_ref, z_ref, image_ref, even_ref, odd_ref, dots_ref, *scratch):
    place, shifts = Place(*counts), Shifts()
    r = reader(r_ref, 2)
    gathered = lambda start, size, stride: level_ref[pl.ds(start, size, stride=stride) if stride > 1 else pl.ds(start, size), :]
    fields = (reader(mass0_ref, 3), reader(weight0_ref, 3), reader(mass1_ref, 2), reader(weight1_ref, 2))
    mass_rows = gathered(3, counts[0] * counts[1], 8)
    particles = (hot_ref, stiff_ref, valid_ref, grad_ref)
    z, image = cycle_and_apply(place, shifts, r, gathered, mass_rows, fields, particles, scratch)
    for x, y in INNER:
        z_ref[x, y] = z(x, y)
    for x, y in RIMMED:
        image_ref[x + 1, y + 1] = image[x, y]
    clear_tail(even_ref, odd_ref)
    for k, (x, y) in enumerate(SIDE_X):
        put_sides(even_ref, odd_ref, 3 * k, 3, image[x + 4, y], image[-1 - x, y], place.even_x)
    rz = total_of((r(x, y), z(x, y)) for x, y in INNER)
    zaz = total_of((image[x, y], z(x, y)) for x, y in RIMMED)
    dots_ref[...] = dots_row(rz, zaz)


def along_x_kernel(counts, image_ref, even_ref, odd_ref, wide_ref, to_even_ref, to_odd_ref):
    place = Place(*counts)
    left, right = side_parts(even_ref, odd_ref, place.even_x, place.in_x[-1], place.in_x[1])

    def value(x, y):
        total = None
        if -1 <= x <= 4:
            total = place.keep(image_ref[x + 1, y + 1], x, 0, BRICK)
        for part, key in ((left, (x, y)), (right, mirror_x(x, y))):
            if key in SIDE_X:
                more = part(3 * SIDE_X.index(key), 4)
                total = more if total is None else total + more
        return total

    value = memo(value)
    for x in range(-3, 7):
        for y in range(-1, BRICK + 1):
            wide_ref[x + 3, y + 1] = value(x, y)
    clear_tail(to_even_ref, to_odd_ref)
    for k, (x, y) in enumerate(SIDE_IMAGE):
        put_sides(to_even_ref, to_odd_ref, 3 * k, 3, value(x, y + 4), value(x, -1 - y), place.even_y)


def middle_kernel(counts, wide_ref, even_ref, odd_ref, mass0_ref, weight0_ref, mass1_ref, weight1_ref, dots_ref,
                  w_ref, slot_ref):
    place, shifts = Place(*counts), Shifts()
    below, above = side_parts(even_ref, odd_ref, place.even_y, place.in_y[-1], place.in_y[1])
    live = as_f32(lax.broadcasted_iota(jnp.int32, (4, LANES), 0) < 3)

    def value(x, y):
        total = None
        if -1 <= y <= 4:
            total = place.keep(wide_ref[x + 3, y + 1], 0, y, BRICK)
        for part, key in ((below, (x, y)), (above, mirror(x, y))):
            if key in SIDE_IMAGE:
                more = part(3 * SIDE_IMAGE.index(key), 4)
                total = more if total is None else total + more
        return jnp.zeros((4, LANES), F32) if total is None else total * live

    w = memo(value)
    r1, r2 = restriction(w, reader(mass0_ref, 3), reader(weight0_ref, 3), reader(mass1_ref, 2), reader(weight1_ref, 2),
                         place, shifts)
    slot_ref[...] = pack_slot(r1, pack_quads(r2), dots_ref[...], shifts)
    for x in range(-2, 6):
        for y in range(-2, 6):
            w_ref[x + 2, y + 2] = w(x, y)


def sums_of(ref, count, first, stride):
    return jnp.sum(ref[pl.ds(first, count, stride=stride), :], axis=0, keepdims=True)


def second_kernel(counts, level_ref, change_ref, r_ref, w_ref, mass0_ref, weight0_ref, mass1_ref, weight1_ref,
                  hot_ref, stiff_ref, valid_ref, grad_ref, z_ref, image_ref, slots_ref, *scratch):
    place, shifts = Place(*counts), Shifts()
    bricks = counts[0] * counts[1]
    sums = sums_of(change_ref, bricks, 7, 8)
    step = sums[:, 0:1] / sums[:, 1:2]
    r = memo(lambda x, y: r_ref[x + 2, y + 2] - step * w_ref[x + 2, y + 2])

    def gathered(start, size, stride):
        rows = pl.ds(start, size, stride=stride) if stride > 1 else pl.ds(start, size)
        return level_ref[rows, :] - step * change_ref[rows, :]

    mass_rows = level_ref[pl.ds(3, bricks, stride=8), :]
    fields = (reader(mass0_ref, 3), reader(weight0_ref, 3), reader(mass1_ref, 2), reader(weight1_ref, 2))
    particles = (hot_ref, stiff_ref, valid_ref, grad_ref)
    z, image = cycle_and_apply(place, shifts, r, gathered, mass_rows, fields, particles, scratch)
    for x, y in INNER:
        z_ref[x, y] = z(x, y)
        image_ref[x, y] = image[x, y]
    rz = total_of((r(x, y), z(x, y)) for x, y in INNER)
    zaz = total_of((image[x, y], z(x, y)) for x, y in RIMMED)
    zw = total_of((w_ref[x + 2, y + 2], z(x, y)) for x, y in INNER)
    row = dots_row(rz, zaz, zw)
    none = jnp.zeros((12, 1, LANES), F32)

    def fill(k, carry):
        slots_ref[k, 0:12] = none
        slots_ref[k, 12] = row
        return carry

    lax.fori_loop(0, bricks, fill, 0)
    for dx in (-1, 0, 1):
        for dy in (-1, 0, 1):
            if dx == 0 and dy == 0:
                continue
            xs = [-1] if dx < 0 else [BRICK] if dx > 0 else range(BRICK)
            ys = [-1] if dy < 0 else [BRICK] if dy > 0 else range(BRICK)
            columns = [image[x, y] for x in xs for y in ys]
            there_x = (place.gx + dx >= 0) & (place.gx + dx < counts[0])
            there_y = (place.gy + dy >= 0) & (place.gy + dy < counts[1])

            @pl.when(there_x & there_y)
            def _(columns=columns, dx=dx, dy=dy):
                other = (place.gx + dx) * counts[1] + place.gy + dy
                for k, column in enumerate(columns):
                    for m in range(3):
                        slots_ref[other, 3 * k + m] = column[m : m + 1]


def last_kernel(counts, slots_ref, change_ref, z1_ref, z2_ref, r_ref, w_ref, image_ref, solution_ref, residual_ref):
    place = Place(*counts)
    bricks = counts[0] * counts[1]
    sums1 = sums_of(change_ref, bricks, 7, 8)
    sums2 = jnp.sum(slots_ref[:, 12], axis=0)
    rz1, zaz1 = sums1[:, 0:1], sums1[:, 1:2]
    rz2, zaz2, zw = sums2[:, 0:1], sums2[:, 1:2], sums2[:, 2:3]
    step1 = rz1 / zaz1
    ratio = rz2 / rz1
    step2 = rz2 / (zaz2 + 2.0 * ratio * zw + ratio * ratio * zaz1)
    image = {(x, y): image_ref[x, y] for x, y in INNER}
    for dx in (-1, 0, 1):
        for dy in (-1, 0, 1):
            if dx == 0 and dy == 0:
                continue
            xs = [0] if dx < 0 else [BRICK - 1] if dx > 0 else range(BRICK)
            ys = [0] if dy < 0 else [BRICK - 1] if dy > 0 else range(BRICK)
            other_x = jnp.clip(place.gx + dx, 0, counts[0] - 1)
            other_y = jnp.clip(place.gy + dy, 0, counts[1] - 1)
            other = other_x * counts[1] + other_y
            for k, (x, y) in enumerate((x, y) for x in xs for y in ys):
                rows = [slots_ref[other, 3 * k + m] for m in range(3)] + [jnp.zeros((1, LANES), F32)]
                image[x, y] = image[x, y] + place.keep(jnp.concatenate(rows, axis=0), dx, dy, 1)
    for x, y in INNER:
        w = w_ref[x + 2, y + 2]
        z1 = z1_ref[x, y]
        solution = step1 * z1 + step2 * (z2_ref[x, y] + ratio * z1)
        residual = r_ref[x + 2, y + 2] - step1 * w - step2 * (image[x, y] + ratio * w)
        for m in range(3):
            solution_ref[m, x, y : y + 1, :] = solution[m : m + 1]
            residual_ref[m, x, y : y + 1, :] = residual[m : m + 1]


def call(kernel, counts, shapes, *args, scratch=()):
    out = [jax.ShapeDtypeStruct(*s) if isinstance(s[0], tuple) else jax.ShapeDtypeStruct(s, F32) for s in shapes]
    return pl.pallas_call(
        functools.partial(kernel, counts),
        out_shape=out,
        scratch_shapes=scratch,
        compiler_params=pltpu.CompilerParams(vmem_limit_bytes=VMEM_BYTES),
    )(*args)


def per_device(counts, right_side, node_mass, gradients, stiffness, valid, node_base):
    bricks = counts[0] * counts[1]
    blocks = gradients.shape[2]
    nodes = BRICK * BRICK * LANES
    scratch = (
        pltpu.VMEM((bricks + 2 * (8 + counts[1]), LANES), F32),
        pltpu.VMEM((224, nodes), jnp.bfloat16),
        pltpu.VMEM((224, blocks * LANES), F32),
        pltpu.VMEM((224, nodes), F32),
    )
    rows = lambda columns, more=0: (-(-(3 * len(columns) + more + 1) // 8) * 8, LANES)

    own = jnp.concatenate([right_side, node_mass[None]], axis=0).transpose(1, 2, 0, 3)
    even, odd = exchange(own, own, "gx", counts)
    side = rows(SIDE, len(SIDE_MASS))
    wide, to_even, to_odd = call(widen_kernel, counts, [(12, 4, 4, LANES), side, side], own, even, odd)
    even, odd = exchange(to_even, to_odd, "gy", counts)
    hot, grads = call(
        one_hot_kernel, counts, [((nodes, blocks * LANES), jnp.bfloat16), gradients.shape[2:]],
        node_base[0, 0], gradients[0, 0],
    )
    particles = (hot, stiffness[0, 0], valid[0, 0], grads)
    r, *fields, slot = call(
        start_kernel, counts,
        [(8, 8, 4, LANES), (10, 10, 4, LANES), (10, 10, 4, LANES), (6, 6, 4, LANES), (6, 6, 4, LANES), (8, LANES)],
        wide, even, odd,
    )

    def share(slot):
        sent = jnp.broadcast_to(slot[None], (bricks, 8, LANES))
        return lax.all_to_all(sent, AXES, 0, 0).reshape(bricks * 8, LANES)

    level = share(slot)
    z1, image, to_even, to_odd, dots = call(
        first_kernel, counts,
        [(4, 4, 4, LANES), (6, 6, 4, LANES), rows(SIDE_X), rows(SIDE_X), (1, LANES)],
        level, r, *fields, *particles, scratch=scratch,
    )
    even, odd = exchange(to_even, to_odd, "gx", counts)
    wide, to_even, to_odd = call(
        along_x_kernel, counts, [(10, 6, 4, LANES), rows(SIDE_IMAGE), rows(SIDE_IMAGE)], image, even, odd
    )
    even, odd = exchange(to_even, to_odd, "gy", counts)
    w, slot = call(middle_kernel, counts, [(8, 8, 4, LANES), (8, LANES)], wide, even, odd, *fields, dots)
    change = share(slot)
    z2, image, slots = call(
        second_kernel, counts, [(4, 4, 4, LANES), (4, 4, 4, LANES), (bricks, 13, 1, LANES)],
        level, change, r, w, *fields, *particles, scratch=scratch,
    )
    slots = lax.all_to_all(slots, AXES, 0, 0)
    return tuple(
        call(last_kernel, counts, [right_side.shape, right_side.shape], slots, change, z1, z2, r, w, image)
    )


def solution(mesh):
    counts = (mesh.shape["gx"], mesh.shape["gy"])
    return jax.shard_map(
        functools.partial(per_device, counts),
        mesh=mesh,
        in_specs=(
            P(None, "gx", "gy", None),
            P("gx", "gy", None),
            P("gx", "gy", None, None, None, None),
            P("gx", "gy", None, None),
            P("gx", "gy", None, None),
            P("gx", "gy", None, None),
        ),
        out_specs=(P(None, "gx", "gy", None), P(None, "gx", "gy", None)),
        check_vma=False,
    )
```

```python
import functools

import jax
import jax.numpy as jnp
from jax import lax
from jax.experimental import pallas as pl
from jax.experimental.pallas import tpu as pltpu
from jax.sharding import PartitionSpec as P

POISSON = 0.3
DAMPING = 0.7
SWEEPS = 4
LANES = 128
BRICK = 4
AXES = ("gx", "gy")
VMEM_BYTES = 24 * 1024 * 1024
F32 = jnp.float32


def pairings(axis, counts):
    count_x, count_y = counts
    even, odd = [], []
    for x in range(count_x):
        for y in range(count_y):
            k, count = (x, count_x) if axis == "gx" else (y, count_y)
            move = lambda to: (to, y) if axis == "gx" else (x, to)
            even.append(((x, y), move(k ^ 1)))
            if 0 < k < count - 1:
                odd.append(((x, y), move(k + 1 if k % 2 else k - 1)))
            else:
                odd.append(((x, y), (x, y ^ 1) if axis == "gx" else (x ^ 1, y)))
    flat = lambda pairs: [(a * count_y + b, c * count_y + d) for (a, b), (c, d) in pairs]
    return flat(even), flat(odd)


def exchange(first, second, axis, counts):
    even, odd = pairings(axis, counts)
    return lax.ppermute(first, AXES, even), lax.ppermute(second, AXES, odd)


SIDE = (
    [(x, -1) for x in range(-2, 6)] + [(x, -2) for x in range(-1, 5)] + [(x, -3) for x in range(4)]
)
SIDE_MASS = [(x, y) for y in (-1, -2) for x in range(-4, 8)] + [(x, y) for y in (-3, -4) for x in range(-2, 6)]
SIDE_IMAGE = [(x, 0) for x in range(-3, 7)] + SIDE
SIDE_X = [(x, y) for x in range(-3, 1) for y in range(-1, 5)]


def mirror(x, y):
    return x, BRICK - 1 - y


def mirror_x(x, y):
    return BRICK - 1 - x, y


def lane_index():
    return lax.broadcasted_iota(jnp.int32, (1, LANES), 1)


def as_f32(cond):
    return jnp.where(cond, 1.0, 0.0).astype(F32)


def turn(x, shift):
    return pltpu.roll(x, shift % LANES, x.ndim - 1)


class Place:
    def __init__(self, count_x, count_y):
        self.gx = lax.axis_index("gx")
        self.gy = lax.axis_index("gy")
        self.count_x, self.count_y = count_x, count_y
        flag = lambda cond: jnp.where(cond, 1.0, 0.0).astype(F32)
        self.even_x = flag(self.gx % 2 == 0)
        self.even_y = flag(self.gy % 2 == 0)
        self.in_x = {-1: flag(self.gx > 0), 0: None, 1: flag(self.gx < count_x - 1)}
        self.in_y = {-1: flag(self.gy > 0), 0: None, 1: flag(self.gy < count_y - 1)}

    def keep(self, value, x, y, size):
        side_x = -1 if x < 0 else 1 if x >= size else 0
        side_y = -1 if y < 0 else 1 if y >= size else 0
        if side_x:
            value = value * self.in_x[side_x]
        if side_y:
            value = value * self.in_y[side_y]
        return value


class Shifts:
    def __init__(self):
        lane = lane_index()
        self.low = {d: as_f32(lane >= d) for d in (1, 2, 4)}
        self.high = {d: as_f32(lane < LANES - d) for d in (1, 2, 4)}
        self.even = as_f32(lane % 2 == 0)
        self.odd = 1.0 - self.even
        self.half = as_f32(lane % 4 < 2)

    def beside(self, x, d):
        return turn(x, d) * self.low[d] + turn(x, -d) * self.high[d]

    def pair_sum(self, x):
        t = (x + turn(x, -1)) * self.even
        return t + turn(t, 1)

    def quad_sum(self, x):
        t = (x + turn(x, -2)) * self.half
        return t + turn(t, 2)


def memo(fn):
    kept = {}

    def wrapped(x, y):
        if (x, y) not in kept:
            kept[(x, y)] = fn(x, y)
        return kept[(x, y)]

    return wrapped


def grid_apply(e, mass, coupling, shifts, step):
    def at(x, y):
        c = e(x, y)
        beside = e(x + 1, y) + e(x - 1, y) + e(x, y + 1) + e(x, y - 1) + shifts.beside(c, step)
        return mass(x, y) * c + coupling * (6.0 * c - beside)

    return at


def restriction(r, mass0, weight0, mass1, weight1, place, shifts):
    e0 = memo(lambda x, y: weight0(x, y) * r(x, y))
    g0 = grid_apply(e0, mass0, 1.0, shifts, 1)
    rem0 = memo(lambda x, y: r(x, y) - g0(x, y))

    def r1_at(x, y):
        total = rem0(2 * x, 2 * y) + rem0(2 * x + 1, 2 * y) + rem0(2 * x, 2 * y + 1) + rem0(2 * x + 1, 2 * y + 1)
        return place.keep(shifts.pair_sum(total), x, y, 2)

    r1 = memo(r1_at)
    e1 = memo(lambda x, y: weight1(x, y) * r1(x, y))
    g1 = grid_apply(e1, mass1, 2.0, shifts, 2)
    total = 0.0
    for x in range(2):
        for y in range(2):
            total = total + (r1(x, y) - g1(x, y))
    return r1, shifts.quad_sum(total)


def pack_slot(r1, r2_row, dots_row, shifts):
    top = r1(0, 0) * shifts.even + r1(0, 1) * shifts.odd
    low = r1(1, 0) * shifts.even + r1(1, 1) * shifts.odd
    return jnp.concatenate([top[0:3], r2_row, low[0:3], dots_row], axis=0)


def pack_quads(column):
    lane = lax.broadcasted_iota(jnp.int32, (4, LANES), 1)
    row = lax.broadcasted_iota(jnp.int32, (4, LANES), 0)
    return jnp.sum(column * as_f32(lane % 4 == row), axis=0, keepdims=True)


def unpack_quads(row):
    lane = lax.broadcasted_iota(jnp.int32, (4, LANES), 1)
    index = lax.broadcasted_iota(jnp.int32, (4, LANES), 0)
    x = jnp.broadcast_to(row, (4, LANES)) * as_f32(lane % 4 == index)
    return spread_quads(x, lane)


def spread_quads(x, lane):
    even = as_f32(lane % 2 == 0)
    odd = 1.0 - even
    x = x + turn(x, -1) * even + turn(x, 1) * odd
    half = as_f32(lane % 4 < 2)
    return x + turn(x, -2) * half + turn(x, 2) * (1.0 - half)


def coarse_solve(r2, m2, count_x, count_y):
    rows = count_x * count_y
    lane = lax.broadcasted_iota(jnp.int32, (rows, LANES), 1)
    row = lax.broadcasted_iota(jnp.int32, (rows, LANES), 0)
    column = row % count_y
    z_low, z_high = as_f32(lane >= 4), as_f32(lane < LANES - 4)
    x_low, x_high = as_f32(row >= count_y), as_f32(row < rows - count_y)
    y_low, y_high = as_f32(column > 0), as_f32(column < count_y - 1)
    up = lambda v, k: pltpu.roll(v, k % rows, 0)
    weight = DAMPING / (m2 + 24.0)
    e = weight * r2
    for _ in range(SWEEPS - 1):
        beside = turn(e, 4) * z_low + turn(e, -4) * z_high
        beside = beside + up(e, count_y) * x_low + up(e, -count_y) * x_high
        beside = beside + up(e, 1) * y_low + up(e, -1) * y_high
        e = e + weight * (r2 - (m2 * e + 4.0 * (6.0 * e - beside)))
    return e


def prolongation(r, r1, e2, mass0, weight0, mass1, weight1, place, shifts):
    e1 = memo(lambda x, y: weight1(x, y) * r1(x, y) + e2(x // 2, y // 2))
    g1 = grid_apply(e1, mass1, 2.0, shifts, 2)
    f1 = memo(lambda x, y: place.keep(e1(x, y) + weight1(x, y) * (r1(x, y) - g1(x, y)), x, y, 2))
    e0 = memo(lambda x, y: weight0(x, y) * r(x, y) + f1(x // 2, y // 2))
    g0 = grid_apply(e0, mass0, 1.0, shifts, 1)
    return memo(lambda x, y: place.keep(e0(x, y) + weight0(x, y) * (r(x, y) - g0(x, y)), x, y, BRICK))


def stiffness_apply(z, fetched, base_ref, stiff_ref, valid_ref, grad_ref, hot, nodes, forces, picked, spread_sums, shifts):
    blocks = grad_ref.shape[0]
    turns = [(b, c) for b in range(3) for c in range(3)]
    span = BRICK + 2

    def halves(x):
        high = x.astype(jnp.bfloat16).astype(F32)
        return jnp.concatenate([high, x - high], axis=0)

    split = {}
    for x in range(span):
        for y in range(span):
            whole = halves(z(x - 1, y - 1))
            split[x, y, 1] = whole
            split[x, y, 0] = turn(whole, 1) * shifts.low[1]
            split[x, y, 2] = turn(whole, -1) * shifts.high[1]
    for u, (b, c) in enumerate(turns):
        for j in range(BRICK):
            for x in range(0, span, 2):
                pair = jnp.concatenate([split[x, j + b, c], split[x + 1, j + b, c]], axis=0).astype(jnp.bfloat16)
                row = (u * span + x) * 8
                nodes[row : row + 16, j * LANES : (j + 1) * LANES] = pair

    fetched()
    base = base_ref[...]
    plane = base // (LANES + 2)
    depth = base - plane * (LANES + 2)
    node_x = plane // span
    node_y = plane - node_x * span
    sub = lax.broadcasted_iota(jnp.int32, (LANES, LANES), 0)
    for s in range(blocks):
        for j in range(BRICK):
            wanted = jnp.where(node_y[s : s + 1] == j, depth[s : s + 1], -1)
            hot[j * LANES : (j + 1) * LANES, s * LANES : (s + 1) * LANES] = as_f32(sub == wanted).astype(jnp.bfloat16)
    picked[...] = jnp.dot(nodes[...], hot[...], preferred_element_type=F32)

    first = POISSON / ((1.0 + POISSON) * (1.0 - 2.0 * POISSON))
    shear_of = 0.5 / (1.0 + POISSON)
    row8 = lax.broadcasted_iota(jnp.int32, (8, LANES), 0)
    row_is = [as_f32(row8 % 4 == m) for m in range(3)]
    is_high = row8 < 4
    zero = jnp.zeros((8, LANES), F32)
    wide = lambda row: jnp.broadcast_to(row, (8, LANES))
    for s in range(blocks):
        lanes = slice(s * LANES, (s + 1) * LANES)
        grad = lambda l, a, b, c: wide(grad_ref[s, l, 9 * a + 3 * b + c : 9 * a + 3 * b + c + 1, :])
        at_x = [wide(node_x[s : s + 1]) == i for i in range(BRICK)]
        h = [None] * 3
        for u, (b, c) in enumerate(turns):
            tiles = [picked[(u * span + x) * 8 : (u * span + x) * 8 + 8, lanes] for x in range(span)]
            for a in range(3):
                value = tiles[3 + a]
                for i in (2, 1, 0):
                    value = jnp.where(at_x[i], tiles[i + a], value)
                for l in range(3):
                    term = value * grad(l, a, b, c)
                    h[l] = term if h[l] is None else h[l] + term
        h = [x[0:4] + x[4:8] for x in h]
        h = [[h[l][m : m + 1] for l in range(3)] for m in range(3)]
        effective = stiff_ref[s : s + 1] * valid_ref[s : s + 1].astype(F32)
        shear = effective * shear_of
        bulk = effective * first * (h[0][0] + h[1][1] + h[2][2])
        stress = []
        for l in range(3):
            column = 0.0
            for m in range(3):
                entry = shear * (h[m][l] + h[l][m])
                if l == m:
                    entry = entry + bulk
                column = column + wide(entry) * row_is[m]
            stress.append(column)
        for u, (b, c) in enumerate(turns):
            parts = []
            for a in range(3):
                f = stress[0] * grad(0, a, b, c) + stress[1] * grad(1, a, b, c) + stress[2] * grad(2, a, b, c)
                high = f.astype(jnp.bfloat16).astype(F32)
                parts.append(jnp.where(is_high, high, f - high))
            tiles = []
            for x in range(span):
                tile = zero
                for a in range(3):
                    if 0 <= x - a < BRICK:
                        tile = jnp.where(at_x[x - a], parts[a], tile)
                tiles.append(tile)
            for x in range(0, span, 2):
                row = (u * span + x) * 8
                pair = jnp.concatenate([tiles[x], tiles[x + 1]], axis=0).astype(jnp.bfloat16)
                forces[row : row + 16, lanes] = pair
    spread_sums[...] = lax.dot_general(
        forces[...], hot[...], (((1,), (1,)), ((), ())), preferred_element_type=F32
    )
    out = {}
    for x in range(span):
        for y in range(span):
            sums = [0.0, 0.0, 0.0]
            for u, (b, c) in enumerate(turns):
                j = y - b
                if 0 <= j < BRICK:
                    row = (u * span + x) * 8
                    sums[c] = sums[c] + spread_sums[row : row + 8, j * LANES : (j + 1) * LANES]
            total = sums[1] + turn(sums[0], -1) * shifts.high[1] + turn(sums[2], 1) * shifts.low[1]
            out[x - 1, y - 1] = total[0:4] + total[4:8]
    return out


def fetch(sources, targets, semaphores):
    copies = [pltpu.make_async_copy(a, b, semaphores.at[k]) for k, (a, b) in enumerate(zip(sources, targets))]
    for copy in copies:
        copy.start()

    def wait():
        for copy in copies:
            copy.wait()

    return wait


def side_parts(even_ref, odd_ref, is_even, inside_low, inside_high):
    odd = 1.0 - is_even
    below_odd, below_even = inside_low * is_even, inside_low * odd
    above_odd, above_even = inside_high * odd, inside_high * is_even

    def below(row, size):
        return odd_ref[row : row + size, :] * below_odd + even_ref[row : row + size, :] * below_even

    def above(row, size):
        return odd_ref[row : row + size, :] * above_odd + even_ref[row : row + size, :] * above_even

    return below, above


def put_sides(to_even_ref, to_odd_ref, row, size, up, down, is_even):
    odd = 1.0 - is_even
    to_even_ref[row : row + size, :] = (up * is_even + down * odd)[0:size]
    to_odd_ref[row : row + size, :] = (down * is_even + up * odd)[0:size]


def clear_tail(*refs):
    for ref in refs:
        ref[ref.shape[0] - 8 :, :] = jnp.zeros((8, LANES), F32)


def pack_kernel(counts, right_ref, mass_ref, own_ref):
    for x in range(BRICK):
        for y in range(BRICK):
            for m in range(3):
                own_ref[x, y, m : m + 1, :] = right_ref[m, x, y : y + 1, :]
            own_ref[x, y, 3:4, :] = mass_ref[x, y : y + 1, :]


def widen_kernel(counts, own_ref, even_ref, odd_ref, wide_ref, to_even_ref, to_odd_ref):
    place = Place(*counts)
    odd_x = 1.0 - place.even_x
    left = (place.in_x[-1] * place.even_x, place.in_x[-1] * odd_x)
    right = (place.in_x[1] * odd_x, place.in_x[1] * place.even_x)

    def value(x, y):
        if 0 <= x < BRICK:
            return own_ref[x, y]
        odd, even = left if x < 0 else right
        return odd_ref[x % BRICK, y] * odd + even_ref[x % BRICK, y] * even

    value = memo(value)
    for x in range(-4, 8):
        for y in range(BRICK):
            wide_ref[x + 4, y] = value(x, y)
    clear_tail(to_even_ref, to_odd_ref)
    for k, (x, y) in enumerate(SIDE):
        put_sides(to_even_ref, to_odd_ref, 3 * k, 3, value(x, y + 4), value(x, -1 - y), place.even_y)
    first = 3 * len(SIDE)
    for k, (x, y) in enumerate(SIDE_MASS):
        put_sides(to_even_ref, to_odd_ref, first + k, 1, value(x, y + 4)[3:4], value(x, -1 - y)[3:4], place.even_y)


def start_kernel(counts, wide_ref, even_ref, odd_ref, r_ref, mass0_ref, weight0_ref, mass1_ref, weight1_ref, slot_ref):
    place, shifts = Place(*counts), Shifts()
    below, above = side_parts(even_ref, odd_ref, place.even_y, place.in_y[-1], place.in_y[1])
    live = as_f32(lax.broadcasted_iota(jnp.int32, (4, LANES), 0) < 3)
    zero = jnp.zeros((4, LANES), F32)

    def r_at(x, y):
        if 0 <= y < BRICK:
            return wide_ref[x + 4, y] * live
        part = below if y < 0 else above
        key = (x, y) if y < 0 else mirror(x, y)
        return part(3 * SIDE.index(key), 4) * live if key in SIDE else zero

    def mass0_at(x, y):
        if 0 <= y < BRICK:
            return jnp.broadcast_to(wide_ref[x + 4, y, 3:4, :], (4, LANES))
        part = below if y < 0 else above
        key = (x, y) if y < 0 else mirror(x, y)
        if key not in SIDE_MASS:
            return zero
        return jnp.broadcast_to(part(3 * len(SIDE) + SIDE_MASS.index(key), 1), (4, LANES))

    r, mass0 = memo(r_at), memo(mass0_at)
    weight0 = memo(lambda x, y: DAMPING / (mass0(x, y) + 6.0))

    def mass1_at(x, y):
        total = mass0(2 * x, 2 * y) + mass0(2 * x + 1, 2 * y) + mass0(2 * x, 2 * y + 1) + mass0(2 * x + 1, 2 * y + 1)
        return shifts.pair_sum(total)

    mass1 = memo(mass1_at)
    weight1 = memo(lambda x, y: DAMPING / (mass1(x, y) + 12.0))
    r1, r2 = restriction(r, mass0, weight0, mass1, weight1, place, shifts)
    m2 = shifts.quad_sum(mass1(0, 0) + mass1(0, 1) + mass1(1, 0) + mass1(1, 1))
    r2_row = pack_quads(jnp.concatenate([r2[0:3], m2[3:4]], axis=0))
    slot_ref[...] = pack_slot(r1, r2_row, jnp.zeros((1, LANES), F32), shifts)
    for x in range(-3, 7):
        for y in range(-3, 7):
            mass0_ref[x + 3, y + 3] = mass0(x, y)
            weight0_ref[x + 3, y + 3] = weight0(x, y)
            if -2 <= x < 6 and -2 <= y < 6:
                r_ref[x + 2, y + 2] = r(x, y)
    for x in range(-2, 4):
        for y in range(-2, 4):
            mass1_ref[x + 2, y + 2] = mass1(x, y)
            weight1_ref[x + 2, y + 2] = weight1(x, y)


def reader(ref, offset):
    return memo(lambda x, y: ref[x + offset, y + offset])


def cycle_and_apply(place, shifts, r, gathered, mass_rows, fields, fetched, particles, scratch):
    count_x, count_y = place.count_x, place.count_y
    mass0, weight0, mass1, weight1 = fields
    coarse, *work = scratch
    bricks = count_x * count_y
    r2 = gathered(3, bricks, 8)
    lane = lax.broadcasted_iota(jnp.int32, (bricks, LANES), 1)
    m2 = spread_quads(mass_rows * as_f32(lane % 4 == 3), lane)
    margin = coarse.shape[0] - bricks
    coarse[...] = jnp.zeros_like(coarse)
    coarse[margin // 2 : margin // 2 + bricks, :] = coarse_solve(r2, m2, count_x, count_y)

    def e2_at(x, y):
        row = (place.gx + x) * count_y + place.gy + y + margin // 2
        return place.keep(unpack_quads(coarse[pl.ds(row, 1), :]), x, y, 1)

    e2 = memo(e2_at)

    def neighbour(x, y):
        other_x = jnp.clip(place.gx + x, 0, count_x - 1)
        other_y = jnp.clip(place.gy + y, 0, count_y - 1)
        row = pl.multiple_of((other_x * count_y + other_y) * 8, 8)
        slot = gathered(row, 8, 1)
        first, second = slot * shifts.even, slot * shifts.odd
        return first + turn(first, 1), second + turn(second, -1)

    neighbour = memo(neighbour)

    def r1_at(x, y):
        both = neighbour(x // 2, y // 2)[y % 2]
        return place.keep(both[4 * (x % 2) : 4 * (x % 2) + 4], x, y, 2)

    r1 = memo(r1_at)
    live = as_f32(lax.broadcasted_iota(jnp.int32, (4, LANES), 0) < 3)
    full = prolongation(r, r1, e2, mass0, weight0, mass1, weight1, place, shifts)
    z = memo(lambda x, y: full(x, y) * live)
    image = stiffness_apply(z, fetched, *particles, *work, shifts)
    for x in range(BRICK):
        for y in range(BRICK):
            image[x, y] = image[x, y] + mass0(x, y) * z(x, y)
    return z, image


def total_of(pairs):
    acc = 0.0
    for a, b in pairs:
        acc = acc + a * b
    return jnp.sum(jnp.sum(acc, axis=0, keepdims=True), axis=1, keepdims=True)


def dots_row(*values):
    lane = lane_index()
    row = 0.0
    for k, v in enumerate(values):
        row = row + as_f32(lane == k) * v
    return row


INNER = [(x, y) for x in range(BRICK) for y in range(BRICK)]
RIMMED = [(x, y) for x in range(-1, BRICK + 1) for y in range(-1, BRICK + 1)]


def first_kernel(counts, level_ref, r_ref, mass0_ref, weight0_ref, mass1_ref, weight1_ref,
                 base_in, stiff_in, valid_in, grad_in, z_ref, image_ref, even_ref, odd_ref, dots_ref,
                 base_ref, stiff_ref, valid_ref, grad_ref, semaphores, *scratch):
    particles = (base_ref, stiff_ref, valid_ref, grad_ref)
    fetched = fetch((base_in, stiff_in, valid_in, grad_in), particles, semaphores)
    place, shifts = Place(*counts), Shifts()
    r = reader(r_ref, 2)
    gathered = lambda start, size, stride: level_ref[pl.ds(start, size, stride=stride) if stride > 1 else pl.ds(start, size), :]
    fields = (reader(mass0_ref, 3), reader(weight0_ref, 3), reader(mass1_ref, 2), reader(weight1_ref, 2))
    mass_rows = gathered(3, counts[0] * counts[1], 8)
    z, image = cycle_and_apply(place, shifts, r, gathered, mass_rows, fields, fetched, particles, scratch)
    for x, y in INNER:
        z_ref[x, y] = z(x, y)
    for x, y in RIMMED:
        image_ref[x + 1, y + 1] = image[x, y]
    clear_tail(even_ref, odd_ref)
    for k, (x, y) in enumerate(SIDE_X):
        put_sides(even_ref, odd_ref, 3 * k, 3, image[x + 4, y], image[-1 - x, y], place.even_x)
    rz = total_of((r(x, y), z(x, y)) for x, y in INNER)
    zaz = total_of((image[x, y], z(x, y)) for x, y in RIMMED)
    dots_ref[...] = dots_row(rz, zaz)


def along_x_kernel(counts, image_ref, even_ref, odd_ref, wide_ref, to_even_ref, to_odd_ref):
    place = Place(*counts)
    left, right = side_parts(even_ref, odd_ref, place.even_x, place.in_x[-1], place.in_x[1])

    def value(x, y):
        total = None
        if -1 <= x <= 4:
            total = place.keep(image_ref[x + 1, y + 1], x, 0, BRICK)
        for part, key in ((left, (x, y)), (right, mirror_x(x, y))):
            if key in SIDE_X:
                more = part(3 * SIDE_X.index(key), 4)
                total = more if total is None else total + more
        return total

    value = memo(value)
    for x in range(-3, 7):
        for y in range(-1, BRICK + 1):
            wide_ref[x + 3, y + 1] = value(x, y)
    clear_tail(to_even_ref, to_odd_ref)
    for k, (x, y) in enumerate(SIDE_IMAGE):
        put_sides(to_even_ref, to_odd_ref, 3 * k, 3, value(x, y + 4), value(x, -1 - y), place.even_y)


def middle_kernel(counts, wide_ref, even_ref, odd_ref, mass0_ref, weight0_ref, mass1_ref, weight1_ref, dots_ref,
                  w_ref, slot_ref):
    place, shifts = Place(*counts), Shifts()
    below, above = side_parts(even_ref, odd_ref, place.even_y, place.in_y[-1], place.in_y[1])
    live = as_f32(lax.broadcasted_iota(jnp.int32, (4, LANES), 0) < 3)

    def value(x, y):
        total = None
        if -1 <= y <= 4:
            total = place.keep(wide_ref[x + 3, y + 1], 0, y, BRICK)
        for part, key in ((below, (x, y)), (above, mirror(x, y))):
            if key in SIDE_IMAGE:
                more = part(3 * SIDE_IMAGE.index(key), 4)
                total = more if total is None else total + more
        return jnp.zeros((4, LANES), F32) if total is None else total * live

    w = memo(value)
    r1, r2 = restriction(w, reader(mass0_ref, 3), reader(weight0_ref, 3), reader(mass1_ref, 2), reader(weight1_ref, 2),
                         place, shifts)
    slot_ref[...] = pack_slot(r1, pack_quads(r2), dots_ref[...], shifts)
    for x in range(-2, 6):
        for y in range(-2, 6):
            w_ref[x + 2, y + 2] = w(x, y)


def sums_of(ref, count, first, stride):
    return jnp.sum(ref[pl.ds(first, count, stride=stride), :], axis=0, keepdims=True)


def second_kernel(counts, level_ref, change_ref, r_ref, w_ref, mass0_ref, weight0_ref, mass1_ref, weight1_ref,
                  base_in, stiff_in, valid_in, grad_in, z_ref, image_ref, slots_ref,
                  base_ref, stiff_ref, valid_ref, grad_ref, semaphores, *scratch):
    particles = (base_ref, stiff_ref, valid_ref, grad_ref)
    fetched = fetch((base_in, stiff_in, valid_in, grad_in), particles, semaphores)
    place, shifts = Place(*counts), Shifts()
    bricks = counts[0] * counts[1]
    sums = sums_of(change_ref, bricks, 7, 8)
    step = sums[:, 0:1] / sums[:, 1:2]
    r = memo(lambda x, y: r_ref[x + 2, y + 2] - step * w_ref[x + 2, y + 2])

    def gathered(start, size, stride):
        rows = pl.ds(start, size, stride=stride) if stride > 1 else pl.ds(start, size)
        return level_ref[rows, :] - step * change_ref[rows, :]

    mass_rows = level_ref[pl.ds(3, bricks, stride=8), :]
    fields = (reader(mass0_ref, 3), reader(weight0_ref, 3), reader(mass1_ref, 2), reader(weight1_ref, 2))
    z, image = cycle_and_apply(place, shifts, r, gathered, mass_rows, fields, fetched, particles, scratch)
    for x, y in INNER:
        z_ref[x, y] = z(x, y)
        image_ref[x, y] = image[x, y]
    rz = total_of((r(x, y), z(x, y)) for x, y in INNER)
    zaz = total_of((image[x, y], z(x, y)) for x, y in RIMMED)
    zw = total_of((w_ref[x + 2, y + 2], z(x, y)) for x, y in INNER)
    row = dots_row(rz, zaz, zw)
    none = jnp.zeros((12, 1, LANES), F32)

    def fill(k, carry):
        slots_ref[k, 0:12] = none
        slots_ref[k, 12] = row
        return carry

    lax.fori_loop(0, bricks, fill, 0)
    for dx in (-1, 0, 1):
        for dy in (-1, 0, 1):
            if dx == 0 and dy == 0:
                continue
            xs = [-1] if dx < 0 else [BRICK] if dx > 0 else range(BRICK)
            ys = [-1] if dy < 0 else [BRICK] if dy > 0 else range(BRICK)
            columns = [image[x, y] for x in xs for y in ys]
            there_x = (place.gx + dx >= 0) & (place.gx + dx < counts[0])
            there_y = (place.gy + dy >= 0) & (place.gy + dy < counts[1])

            @pl.when(there_x & there_y)
            def _(columns=columns, dx=dx, dy=dy):
                other = (place.gx + dx) * counts[1] + place.gy + dy
                for k, column in enumerate(columns):
                    for m in range(3):
                        slots_ref[other, 3 * k + m] = column[m : m + 1]


def last_kernel(counts, slots_ref, change_ref, z1_ref, z2_ref, r_ref, w_ref, image_ref, solution_ref, residual_ref):
    place = Place(*counts)
    bricks = counts[0] * counts[1]
    sums1 = sums_of(change_ref, bricks, 7, 8)
    sums2 = jnp.sum(slots_ref[:, 12], axis=0)
    rz1, zaz1 = sums1[:, 0:1], sums1[:, 1:2]
    rz2, zaz2, zw = sums2[:, 0:1], sums2[:, 1:2], sums2[:, 2:3]
    step1 = rz1 / zaz1
    ratio = rz2 / rz1
    step2 = rz2 / (zaz2 + 2.0 * ratio * zw + ratio * ratio * zaz1)
    image = {(x, y): image_ref[x, y] for x, y in INNER}
    for dx in (-1, 0, 1):
        for dy in (-1, 0, 1):
            if dx == 0 and dy == 0:
                continue
            xs = [0] if dx < 0 else [BRICK - 1] if dx > 0 else range(BRICK)
            ys = [0] if dy < 0 else [BRICK - 1] if dy > 0 else range(BRICK)
            other_x = jnp.clip(place.gx + dx, 0, counts[0] - 1)
            other_y = jnp.clip(place.gy + dy, 0, counts[1] - 1)
            other = other_x * counts[1] + other_y
            for k, (x, y) in enumerate((x, y) for x in xs for y in ys):
                rows = [slots_ref[other, 3 * k + m] for m in range(3)] + [jnp.zeros((1, LANES), F32)]
                image[x, y] = image[x, y] + place.keep(jnp.concatenate(rows, axis=0), dx, dy, 1)
    for x, y in INNER:
        w = w_ref[x + 2, y + 2]
        z1 = z1_ref[x, y]
        solution = step1 * z1 + step2 * (z2_ref[x, y] + ratio * z1)
        residual = r_ref[x + 2, y + 2] - step1 * w - step2 * (image[x, y] + ratio * w)
        for m in range(3):
            solution_ref[m, x, y : y + 1, :] = solution[m : m + 1]
            residual_ref[m, x, y : y + 1, :] = residual[m : m + 1]


def call(kernel, counts, shapes, *args, scratch=(), far=0):
    near = len(args) - far
    return pl.pallas_call(
        functools.partial(kernel, counts),
        out_shape=[jax.ShapeDtypeStruct(s, F32) for s in shapes],
        in_specs=[pl.BlockSpec(memory_space=pltpu.VMEM)] * near + [pl.BlockSpec(memory_space=pl.ANY)] * far,
        scratch_shapes=scratch,
        compiler_params=pltpu.CompilerParams(vmem_limit_bytes=VMEM_BYTES),
    )(*args)


def per_device(counts, right_side, node_mass, gradients, stiffness, valid, node_base):
    bricks = counts[0] * counts[1]
    blocks = gradients.shape[2]
    particles = (node_base[0, 0], stiffness[0, 0], valid[0, 0], gradients[0, 0])
    tiles = 9 * (BRICK + 2) * 8
    depth = BRICK * LANES
    width = blocks * LANES
    scratch = (
        *(pltpu.VMEM(p.shape, p.dtype) for p in particles),
        pltpu.SemaphoreType.DMA((4,)),
        pltpu.VMEM((bricks + 2 * (8 + counts[1]), LANES), F32),
        pltpu.VMEM((depth, width), jnp.bfloat16),
        pltpu.VMEM((tiles, depth), jnp.bfloat16),
        pltpu.VMEM((tiles, width), jnp.bfloat16),
        pltpu.VMEM((tiles, width), F32),
        pltpu.VMEM((tiles, depth), F32),
    )
    rows = lambda columns, more=0: (-(-(3 * len(columns) + more + 1) // 8) * 8, LANES)

    (own,) = call(pack_kernel, counts, [(4, 4, 4, LANES)], right_side, node_mass)
    even, odd = exchange(own, own, "gx", counts)
    side = rows(SIDE, len(SIDE_MASS))
    wide, to_even, to_odd = call(widen_kernel, counts, [(12, 4, 4, LANES), side, side], own, even, odd)
    even, odd = exchange(to_even, to_odd, "gy", counts)
    r, *fields, slot = call(
        start_kernel, counts,
        [(8, 8, 4, LANES), (10, 10, 4, LANES), (10, 10, 4, LANES), (6, 6, 4, LANES), (6, 6, 4, LANES), (8, LANES)],
        wide, even, odd,
    )

    def share(slot):
        sent = jnp.broadcast_to(slot[None], (bricks, 8, LANES))
        return lax.all_to_all(sent, AXES, 0, 0).reshape(bricks * 8, LANES)

    level = share(slot)
    z1, image, to_even, to_odd, dots = call(
        first_kernel, counts,
        [(4, 4, 4, LANES), (6, 6, 4, LANES), rows(SIDE_X), rows(SIDE_X), (1, LANES)],
        level, r, *fields, *particles, scratch=scratch, far=4,
    )
    even, odd = exchange(to_even, to_odd, "gx", counts)
    wide, to_even, to_odd = call(
        along_x_kernel, counts, [(10, 6, 4, LANES), rows(SIDE_IMAGE), rows(SIDE_IMAGE)], image, even, odd
    )
    even, odd = exchange(to_even, to_odd, "gy", counts)
    w, slot = call(middle_kernel, counts, [(8, 8, 4, LANES), (8, LANES)], wide, even, odd, *fields, dots)
    change = share(slot)
    z2, image, slots = call(
        second_kernel, counts, [(4, 4, 4, LANES), (4, 4, 4, LANES), (bricks, 13, 1, LANES)],
        level, change, r, w, *fields, *particles, scratch=scratch, far=4,
    )
    slots = lax.all_to_all(slots, AXES, 0, 0)
    return tuple(
        call(last_kernel, counts, [right_side.shape, right_side.shape], slots, change, z1, z2, r, w, image)
    )


def solution(mesh):
    counts = (mesh.shape["gx"], mesh.shape["gy"])
    return jax.shard_map(
        functools.partial(per_device, counts),
        mesh=mesh,
        in_specs=(
            P(None, "gx", "gy", None),
            P("gx", "gy", None),
            P("gx", "gy", None, None, None, None),
            P("gx", "gy", None, None),
            P("gx", "gy", None, None),
            P("gx", "gy", None, None),
        ),
        out_specs=(P(None, "gx", "gy", None), P(None, "gx", "gy", None)),
        check_vma=False,
    )
```

```python
import functools

import jax
import jax.numpy as jnp
from jax import lax
from jax.experimental import pallas as pl
from jax.experimental.pallas import tpu as pltpu
from jax.sharding import PartitionSpec as P

POISSON = 0.3
DAMPING = 0.7
SWEEPS = 4
LANES = 128
BRICK = 4
AXES = ("gx", "gy")
VMEM_BYTES = 24 * 1024 * 1024
F32 = jnp.float32


def pairings(axis, counts):
    count_x, count_y = counts
    even, odd = [], []
    for x in range(count_x):
        for y in range(count_y):
            k, count = (x, count_x) if axis == "gx" else (y, count_y)
            move = lambda to: (to, y) if axis == "gx" else (x, to)
            even.append(((x, y), move(k ^ 1)))
            if 0 < k < count - 1:
                odd.append(((x, y), move(k + 1 if k % 2 else k - 1)))
            else:
                odd.append(((x, y), (x, y ^ 1) if axis == "gx" else (x ^ 1, y)))
    flat = lambda pairs: [(a * count_y + b, c * count_y + d) for (a, b), (c, d) in pairs]
    return flat(even), flat(odd)


def exchange(first, second, axis, counts):
    even, odd = pairings(axis, counts)
    return lax.ppermute(first, AXES, even), lax.ppermute(second, AXES, odd)


SIDE = (
    [(x, -1) for x in range(-2, 6)] + [(x, -2) for x in range(-1, 5)] + [(x, -3) for x in range(4)]
)
SIDE_MASS = [(x, y) for y in (-1, -2) for x in range(-4, 8)] + [(x, y) for y in (-3, -4) for x in range(-2, 6)]
SIDE_IMAGE = [(x, 0) for x in range(-3, 7)] + SIDE
SIDE_X = [(x, y) for x in range(-3, 1) for y in range(-1, 5)]


def mirror(x, y):
    return x, BRICK - 1 - y


def mirror_x(x, y):
    return BRICK - 1 - x, y


def lane_index():
    return lax.broadcasted_iota(jnp.int32, (1, LANES), 1)


def as_f32(cond):
    return jnp.where(cond, 1.0, 0.0).astype(F32)


def turn(x, shift):
    return pltpu.roll(x, shift % LANES, x.ndim - 1)


class Place:
    def __init__(self, count_x, count_y):
        self.gx = lax.axis_index("gx")
        self.gy = lax.axis_index("gy")
        self.count_x, self.count_y = count_x, count_y
        flag = lambda cond: jnp.where(cond, 1.0, 0.0).astype(F32)
        self.even_x = flag(self.gx % 2 == 0)
        self.even_y = flag(self.gy % 2 == 0)
        self.in_x = {-1: flag(self.gx > 0), 0: None, 1: flag(self.gx < count_x - 1)}
        self.in_y = {-1: flag(self.gy > 0), 0: None, 1: flag(self.gy < count_y - 1)}

    def keep(self, value, x, y, size):
        side_x = -1 if x < 0 else 1 if x >= size else 0
        side_y = -1 if y < 0 else 1 if y >= size else 0
        if side_x:
            value = value * self.in_x[side_x]
        if side_y:
            value = value * self.in_y[side_y]
        return value


class Shifts:
    def __init__(self):
        lane = lane_index()
        self.low = {d: as_f32(lane >= d) for d in (1, 2, 4)}
        self.high = {d: as_f32(lane < LANES - d) for d in (1, 2, 4)}
        self.even = as_f32(lane % 2 == 0)
        self.odd = 1.0 - self.even
        self.half = as_f32(lane % 4 < 2)

    def beside(self, x, d):
        return turn(x, d) * self.low[d] + turn(x, -d) * self.high[d]

    def pair_sum(self, x):
        t = (x + turn(x, -1)) * self.even
        return t + turn(t, 1)

    def quad_sum(self, x):
        t = (x + turn(x, -2)) * self.half
        return t + turn(t, 2)


def memo(fn):
    kept = {}

    def wrapped(x, y):
        if (x, y) not in kept:
            kept[(x, y)] = fn(x, y)
        return kept[(x, y)]

    return wrapped


def grid_apply(e, mass, coupling, shifts, step):
    def at(x, y):
        c = e(x, y)
        beside = e(x + 1, y) + e(x - 1, y) + e(x, y + 1) + e(x, y - 1) + shifts.beside(c, step)
        return mass(x, y) * c + coupling * (6.0 * c - beside)

    return at


def restriction(r, mass0, weight0, mass1, weight1, place, shifts):
    e0 = memo(lambda x, y: weight0(x, y) * r(x, y))
    g0 = grid_apply(e0, mass0, 1.0, shifts, 1)
    rem0 = memo(lambda x, y: r(x, y) - g0(x, y))

    def r1_at(x, y):
        total = rem0(2 * x, 2 * y) + rem0(2 * x + 1, 2 * y) + rem0(2 * x, 2 * y + 1) + rem0(2 * x + 1, 2 * y + 1)
        return place.keep(shifts.pair_sum(total), x, y, 2)

    r1 = memo(r1_at)
    e1 = memo(lambda x, y: weight1(x, y) * r1(x, y))
    g1 = grid_apply(e1, mass1, 2.0, shifts, 2)
    total = 0.0
    for x in range(2):
        for y in range(2):
            total = total + (r1(x, y) - g1(x, y))
    return r1, shifts.quad_sum(total)


def pack_slot(r1, r2_row, dots_row, shifts):
    top = r1(0, 0) * shifts.even + r1(0, 1) * shifts.odd
    low = r1(1, 0) * shifts.even + r1(1, 1) * shifts.odd
    return jnp.concatenate([top[0:3], r2_row, low[0:3], dots_row], axis=0)


def pack_quads(column):
    lane = lax.broadcasted_iota(jnp.int32, (4, LANES), 1)
    row = lax.broadcasted_iota(jnp.int32, (4, LANES), 0)
    return jnp.sum(column * as_f32(lane % 4 == row), axis=0, keepdims=True)


def unpack_quads(row):
    lane = lax.broadcasted_iota(jnp.int32, (4, LANES), 1)
    index = lax.broadcasted_iota(jnp.int32, (4, LANES), 0)
    x = jnp.broadcast_to(row, (4, LANES)) * as_f32(lane % 4 == index)
    return spread_quads(x, lane)


def spread_quads(x, lane):
    even = as_f32(lane % 2 == 0)
    odd = 1.0 - even
    x = x + turn(x, -1) * even + turn(x, 1) * odd
    half = as_f32(lane % 4 < 2)
    return x + turn(x, -2) * half + turn(x, 2) * (1.0 - half)


def coarse_solve(r2, m2, count_x, count_y):
    rows = count_x * count_y
    lane = lax.broadcasted_iota(jnp.int32, (rows, LANES), 1)
    row = lax.broadcasted_iota(jnp.int32, (rows, LANES), 0)
    column = row % count_y
    z_low, z_high = as_f32(lane >= 4), as_f32(lane < LANES - 4)
    x_low, x_high = as_f32(row >= count_y), as_f32(row < rows - count_y)
    y_low, y_high = as_f32(column > 0), as_f32(column < count_y - 1)
    up = lambda v, k: pltpu.roll(v, k % rows, 0)
    weight = DAMPING / (m2 + 24.0)
    e = weight * r2
    for _ in range(SWEEPS - 1):
        beside = turn(e, 4) * z_low + turn(e, -4) * z_high
        beside = beside + up(e, count_y) * x_low + up(e, -count_y) * x_high
        beside = beside + up(e, 1) * y_low + up(e, -1) * y_high
        e = e + weight * (r2 - (m2 * e + 4.0 * (6.0 * e - beside)))
    return e


def prolongation(r, r1, e2, mass0, weight0, mass1, weight1, place, shifts):
    e1 = memo(lambda x, y: weight1(x, y) * r1(x, y) + e2(x // 2, y // 2))
    g1 = grid_apply(e1, mass1, 2.0, shifts, 2)
    f1 = memo(lambda x, y: place.keep(e1(x, y) + weight1(x, y) * (r1(x, y) - g1(x, y)), x, y, 2))
    e0 = memo(lambda x, y: weight0(x, y) * r(x, y) + f1(x // 2, y // 2))
    g0 = grid_apply(e0, mass0, 1.0, shifts, 1)
    return memo(lambda x, y: place.keep(e0(x, y) + weight0(x, y) * (r(x, y) - g0(x, y)), x, y, BRICK))


def stiffness_apply(z, fetched, base_ref, stiff_ref, valid_ref, grad_ref, hot, nodes, forces, picked, spread_sums, shifts):
    blocks = grad_ref.shape[2]
    turns = [(b, c) for b in range(3) for c in range(3)]
    span = BRICK + 2

    def halves(x):
        high = x.astype(jnp.bfloat16).astype(F32)
        return jnp.concatenate([high, x - high], axis=0)

    split = {}
    for x in range(span):
        for y in range(span):
            whole = halves(z(x - 1, y - 1))
            split[x, y, 1] = whole
            split[x, y, 0] = turn(whole, 1) * shifts.low[1]
            split[x, y, 2] = turn(whole, -1) * shifts.high[1]
    for u, (b, c) in enumerate(turns):
        for j in range(BRICK):
            for x in range(0, span, 2):
                pair = jnp.concatenate([split[x, j + b, c], split[x + 1, j + b, c]], axis=0).astype(jnp.bfloat16)
                row = (u * span + x) * 8
                nodes[row : row + 16, j * LANES : (j + 1) * LANES] = pair

    fetched()
    base = base_ref[...]
    plane = base // (LANES + 2)
    depth = base - plane * (LANES + 2)
    node_x = plane // span
    node_y = plane - node_x * span
    sub = lax.broadcasted_iota(jnp.int32, (LANES, LANES), 0)
    for s in range(blocks):
        for j in range(BRICK):
            wanted = jnp.where(node_y[s : s + 1] == j, depth[s : s + 1], -1)
            hot[j * LANES : (j + 1) * LANES, s * LANES : (s + 1) * LANES] = as_f32(sub == wanted).astype(jnp.bfloat16)
    picked[...] = jnp.dot(nodes[...], hot[...], preferred_element_type=F32)

    first = POISSON / ((1.0 + POISSON) * (1.0 - 2.0 * POISSON))
    shear_of = 0.5 / (1.0 + POISSON)
    row8 = lax.broadcasted_iota(jnp.int32, (8, LANES), 0)
    row_is = [as_f32(row8 % 4 == m) for m in range(3)]
    is_high = row8 < 4
    zero = jnp.zeros((8, LANES), F32)
    wide = lambda row: jnp.broadcast_to(row, (8, LANES))
    for s in range(blocks):
        lanes = slice(s * LANES, (s + 1) * LANES)
        grad = lambda l, a, b, c: wide(grad_ref[l, 9 * a + 3 * b + c, s : s + 1, :])
        at_x = [wide(node_x[s : s + 1]) == i for i in range(BRICK)]
        h = [None] * 3
        for u, (b, c) in enumerate(turns):
            tiles = [picked[(u * span + x) * 8 : (u * span + x) * 8 + 8, lanes] for x in range(span)]
            for a in range(3):
                value = tiles[3 + a]
                for i in (2, 1, 0):
                    value = jnp.where(at_x[i], tiles[i + a], value)
                for l in range(3):
                    term = value * grad(l, a, b, c)
                    h[l] = term if h[l] is None else h[l] + term
        h = [x[0:4] + x[4:8] for x in h]
        h = [[h[l][m : m + 1] for l in range(3)] for m in range(3)]
        effective = stiff_ref[s : s + 1] * valid_ref[s : s + 1].astype(F32)
        shear = effective * shear_of
        bulk = effective * first * (h[0][0] + h[1][1] + h[2][2])
        stress = []
        for l in range(3):
            column = 0.0
            for m in range(3):
                entry = shear * (h[m][l] + h[l][m])
                if l == m:
                    entry = entry + bulk
                column = column + wide(entry) * row_is[m]
            stress.append(column)
        for u, (b, c) in enumerate(turns):
            parts = []
            for a in range(3):
                f = stress[0] * grad(0, a, b, c) + stress[1] * grad(1, a, b, c) + stress[2] * grad(2, a, b, c)
                high = f.astype(jnp.bfloat16).astype(F32)
                parts.append(jnp.where(is_high, high, f - high))
            tiles = []
            for x in range(span):
                tile = zero
                for a in range(3):
                    if 0 <= x - a < BRICK:
                        tile = jnp.where(at_x[x - a], parts[a], tile)
                tiles.append(tile)
            for x in range(0, span, 2):
                row = (u * span + x) * 8
                pair = jnp.concatenate([tiles[x], tiles[x + 1]], axis=0).astype(jnp.bfloat16)
                forces[row : row + 16, lanes] = pair
    spread_sums[...] = lax.dot_general(
        forces[...], hot[...], (((1,), (1,)), ((), ())), preferred_element_type=F32
    )
    out = {}
    for x in range(span):
        for y in range(span):
            sums = [0.0, 0.0, 0.0]
            for u, (b, c) in enumerate(turns):
                j = y - b
                if 0 <= j < BRICK:
                    row = (u * span + x) * 8
                    sums[c] = sums[c] + spread_sums[row : row + 8, j * LANES : (j + 1) * LANES]
            total = sums[1] + turn(sums[0], -1) * shifts.high[1] + turn(sums[2], 1) * shifts.low[1]
            out[x - 1, y - 1] = total[0:4] + total[4:8]
    return out


def fetch(sources, targets, semaphores):
    copies = [pltpu.make_async_copy(a, b, semaphores.at[k]) for k, (a, b) in enumerate(zip(sources, targets))]
    for copy in copies:
        copy.start()

    def wait():
        for copy in copies:
            copy.wait()

    return wait


def side_parts(even_ref, odd_ref, is_even, inside_low, inside_high):
    odd = 1.0 - is_even
    below_odd, below_even = inside_low * is_even, inside_low * odd
    above_odd, above_even = inside_high * odd, inside_high * is_even

    def below(row, size):
        return odd_ref[row : row + size, :] * below_odd + even_ref[row : row + size, :] * below_even

    def above(row, size):
        return odd_ref[row : row + size, :] * above_odd + even_ref[row : row + size, :] * above_even

    return below, above


def put_sides(to_even_ref, to_odd_ref, row, size, up, down, is_even):
    odd = 1.0 - is_even
    to_even_ref[row : row + size, :] = (up * is_even + down * odd)[0:size]
    to_odd_ref[row : row + size, :] = (down * is_even + up * odd)[0:size]


def clear_tail(*refs):
    for ref in refs:
        ref[ref.shape[0] - 8 :, :] = jnp.zeros((8, LANES), F32)


def pack_kernel(counts, right_in, mass_in, own_ref, right_ref, mass_ref, semaphores):
    fetch((right_in, mass_in), (right_ref, mass_ref), semaphores)()
    for x in range(BRICK):
        for y in range(BRICK):
            for m in range(3):
                own_ref[x, y, m : m + 1, :] = right_ref[m, x, y : y + 1, :]
            own_ref[x, y, 3:4, :] = mass_ref[x, y : y + 1, :]


def widen_kernel(counts, own_ref, even_ref, odd_ref, wide_ref, to_even_ref, to_odd_ref):
    place = Place(*counts)
    odd_x = 1.0 - place.even_x
    left = (place.in_x[-1] * place.even_x, place.in_x[-1] * odd_x)
    right = (place.in_x[1] * odd_x, place.in_x[1] * place.even_x)

    def value(x, y):
        if 0 <= x < BRICK:
            return own_ref[x, y]
        odd, even = left if x < 0 else right
        return odd_ref[x % BRICK, y] * odd + even_ref[x % BRICK, y] * even

    value = memo(value)
    for x in range(-4, 8):
        for y in range(BRICK):
            wide_ref[x + 4, y] = value(x, y)
    clear_tail(to_even_ref, to_odd_ref)
    for k, (x, y) in enumerate(SIDE):
        put_sides(to_even_ref, to_odd_ref, 3 * k, 3, value(x, y + 4), value(x, -1 - y), place.even_y)
    first = 3 * len(SIDE)
    for k, (x, y) in enumerate(SIDE_MASS):
        put_sides(to_even_ref, to_odd_ref, first + k, 1, value(x, y + 4)[3:4], value(x, -1 - y)[3:4], place.even_y)


def start_kernel(counts, wide_ref, even_ref, odd_ref, r_ref, mass0_ref, weight0_ref, mass1_ref, weight1_ref, slot_ref):
    place, shifts = Place(*counts), Shifts()
    below, above = side_parts(even_ref, odd_ref, place.even_y, place.in_y[-1], place.in_y[1])
    live = as_f32(lax.broadcasted_iota(jnp.int32, (4, LANES), 0) < 3)
    zero = jnp.zeros((4, LANES), F32)

    def r_at(x, y):
        if 0 <= y < BRICK:
            return wide_ref[x + 4, y] * live
        part = below if y < 0 else above
        key = (x, y) if y < 0 else mirror(x, y)
        return part(3 * SIDE.index(key), 4) * live if key in SIDE else zero

    def mass0_at(x, y):
        if 0 <= y < BRICK:
            return jnp.broadcast_to(wide_ref[x + 4, y, 3:4, :], (4, LANES))
        part = below if y < 0 else above
        key = (x, y) if y < 0 else mirror(x, y)
        if key not in SIDE_MASS:
            return zero
        return jnp.broadcast_to(part(3 * len(SIDE) + SIDE_MASS.index(key), 1), (4, LANES))

    r, mass0 = memo(r_at), memo(mass0_at)
    weight0 = memo(lambda x, y: DAMPING / (mass0(x, y) + 6.0))

    def mass1_at(x, y):
        total = mass0(2 * x, 2 * y) + mass0(2 * x + 1, 2 * y) + mass0(2 * x, 2 * y + 1) + mass0(2 * x + 1, 2 * y + 1)
        return shifts.pair_sum(total)

    mass1 = memo(mass1_at)
    weight1 = memo(lambda x, y: DAMPING / (mass1(x, y) + 12.0))
    r1, r2 = restriction(r, mass0, weight0, mass1, weight1, place, shifts)
    m2 = shifts.quad_sum(mass1(0, 0) + mass1(0, 1) + mass1(1, 0) + mass1(1, 1))
    r2_row = pack_quads(jnp.concatenate([r2[0:3], m2[3:4]], axis=0))
    slot_ref[...] = pack_slot(r1, r2_row, jnp.zeros((1, LANES), F32), shifts)
    for x in range(-3, 7):
        for y in range(-3, 7):
            mass0_ref[x + 3, y + 3] = mass0(x, y)
            weight0_ref[x + 3, y + 3] = weight0(x, y)
            if -2 <= x < 6 and -2 <= y < 6:
                r_ref[x + 2, y + 2] = r(x, y)
    for x in range(-2, 4):
        for y in range(-2, 4):
            mass1_ref[x + 2, y + 2] = mass1(x, y)
            weight1_ref[x + 2, y + 2] = weight1(x, y)


def reader(ref, offset):
    return memo(lambda x, y: ref[x + offset, y + offset])


def cycle_and_apply(place, shifts, r, gathered, mass_rows, fields, fetched, particles, scratch):
    count_x, count_y = place.count_x, place.count_y
    mass0, weight0, mass1, weight1 = fields
    coarse, *work = scratch
    bricks = count_x * count_y
    r2 = gathered(3, bricks, 8)
    lane = lax.broadcasted_iota(jnp.int32, (bricks, LANES), 1)
    m2 = spread_quads(mass_rows * as_f32(lane % 4 == 3), lane)
    margin = coarse.shape[0] - bricks
    coarse[...] = jnp.zeros_like(coarse)
    coarse[margin // 2 : margin // 2 + bricks, :] = coarse_solve(r2, m2, count_x, count_y)

    def e2_at(x, y):
        row = (place.gx + x) * count_y + place.gy + y + margin // 2
        return place.keep(unpack_quads(coarse[pl.ds(row, 1), :]), x, y, 1)

    e2 = memo(e2_at)

    def neighbour(x, y):
        other_x = jnp.clip(place.gx + x, 0, count_x - 1)
        other_y = jnp.clip(place.gy + y, 0, count_y - 1)
        row = pl.multiple_of((other_x * count_y + other_y) * 8, 8)
        slot = gathered(row, 8, 1)
        first, second = slot * shifts.even, slot * shifts.odd
        return first + turn(first, 1), second + turn(second, -1)

    neighbour = memo(neighbour)

    def r1_at(x, y):
        both = neighbour(x // 2, y // 2)[y % 2]
        return place.keep(both[4 * (x % 2) : 4 * (x % 2) + 4], x, y, 2)

    r1 = memo(r1_at)
    live = as_f32(lax.broadcasted_iota(jnp.int32, (4, LANES), 0) < 3)
    full = prolongation(r, r1, e2, mass0, weight0, mass1, weight1, place, shifts)
    z = memo(lambda x, y: full(x, y) * live)
    image = stiffness_apply(z, fetched, *particles, *work, shifts)
    for x in range(BRICK):
        for y in range(BRICK):
            image[x, y] = image[x, y] + mass0(x, y) * z(x, y)
    return z, image


def total_of(pairs):
    acc = 0.0
    for a, b in pairs:
        acc = acc + a * b
    return jnp.sum(jnp.sum(acc, axis=0, keepdims=True), axis=1, keepdims=True)


def dots_row(*values):
    lane = lane_index()
    row = 0.0
    for k, v in enumerate(values):
        row = row + as_f32(lane == k) * v
    return row


INNER = [(x, y) for x in range(BRICK) for y in range(BRICK)]
RIMMED = [(x, y) for x in range(-1, BRICK + 1) for y in range(-1, BRICK + 1)]


def first_kernel(counts, level_ref, r_ref, mass0_ref, weight0_ref, mass1_ref, weight1_ref,
                 base_in, stiff_in, valid_in, grad_in, z_ref, image_ref, even_ref, odd_ref, dots_ref,
                 base_ref, stiff_ref, valid_ref, grad_ref, semaphores, *scratch):
    particles = (base_ref, stiff_ref, valid_ref, grad_ref)
    fetched = fetch((base_in, stiff_in, valid_in, grad_in), particles, semaphores)
    place, shifts = Place(*counts), Shifts()
    r = reader(r_ref, 2)
    gathered = lambda start, size, stride: level_ref[pl.ds(start, size, stride=stride) if stride > 1 else pl.ds(start, size), :]
    fields = (reader(mass0_ref, 3), reader(weight0_ref, 3), reader(mass1_ref, 2), reader(weight1_ref, 2))
    mass_rows = gathered(3, counts[0] * counts[1], 8)
    z, image = cycle_and_apply(place, shifts, r, gathered, mass_rows, fields, fetched, particles, scratch)
    for x, y in INNER:
        z_ref[x, y] = z(x, y)
    for x, y in RIMMED:
        image_ref[x + 1, y + 1] = image[x, y]
    clear_tail(even_ref, odd_ref)
    for k, (x, y) in enumerate(SIDE_X):
        put_sides(even_ref, odd_ref, 3 * k, 3, image[x + 4, y], image[-1 - x, y], place.even_x)
    rz = total_of((r(x, y), z(x, y)) for x, y in INNER)
    zaz = total_of((image[x, y], z(x, y)) for x, y in RIMMED)
    dots_ref[...] = dots_row(rz, zaz)


def along_x_kernel(counts, image_ref, even_ref, odd_ref, wide_ref, to_even_ref, to_odd_ref):
    place = Place(*counts)
    left, right = side_parts(even_ref, odd_ref, place.even_x, place.in_x[-1], place.in_x[1])

    def value(x, y):
        total = None
        if -1 <= x <= 4:
            total = place.keep(image_ref[x + 1, y + 1], x, 0, BRICK)
        for part, key in ((left, (x, y)), (right, mirror_x(x, y))):
            if key in SIDE_X:
                more = part(3 * SIDE_X.index(key), 4)
                total = more if total is None else total + more
        return total

    value = memo(value)
    for x in range(-3, 7):
        for y in range(-1, BRICK + 1):
            wide_ref[x + 3, y + 1] = value(x, y)
    clear_tail(to_even_ref, to_odd_ref)
    for k, (x, y) in enumerate(SIDE_IMAGE):
        put_sides(to_even_ref, to_odd_ref, 3 * k, 3, value(x, y + 4), value(x, -1 - y), place.even_y)


def middle_kernel(counts, wide_ref, even_ref, odd_ref, mass0_ref, weight0_ref, mass1_ref, weight1_ref, dots_ref,
                  w_ref, slot_ref):
    place, shifts = Place(*counts), Shifts()
    below, above = side_parts(even_ref, odd_ref, place.even_y, place.in_y[-1], place.in_y[1])
    live = as_f32(lax.broadcasted_iota(jnp.int32, (4, LANES), 0) < 3)

    def value(x, y):
        total = None
        if -1 <= y <= 4:
            total = place.keep(wide_ref[x + 3, y + 1], 0, y, BRICK)
        for part, key in ((below, (x, y)), (above, mirror(x, y))):
            if key in SIDE_IMAGE:
                more = part(3 * SIDE_IMAGE.index(key), 4)
                total = more if total is None else total + more
        return jnp.zeros((4, LANES), F32) if total is None else total * live

    w = memo(value)
    r1, r2 = restriction(w, reader(mass0_ref, 3), reader(weight0_ref, 3), reader(mass1_ref, 2), reader(weight1_ref, 2),
                         place, shifts)
    slot_ref[...] = pack_slot(r1, pack_quads(r2), dots_ref[...], shifts)
    for x in range(-2, 6):
        for y in range(-2, 6):
            w_ref[x + 2, y + 2] = w(x, y)


def sums_of(ref, count, first, stride):
    return jnp.sum(ref[pl.ds(first, count, stride=stride), :], axis=0, keepdims=True)


def second_kernel(counts, level_ref, change_ref, r_ref, w_ref, mass0_ref, weight0_ref, mass1_ref, weight1_ref,
                  base_in, stiff_in, valid_in, grad_in, z_ref, image_ref, slots_ref,
                  base_ref, stiff_ref, valid_ref, grad_ref, semaphores, *scratch):
    particles = (base_ref, stiff_ref, valid_ref, grad_ref)
    fetched = fetch((base_in, stiff_in, valid_in, grad_in), particles, semaphores)
    place, shifts = Place(*counts), Shifts()
    bricks = counts[0] * counts[1]
    sums = sums_of(change_ref, bricks, 7, 8)
    step = sums[:, 0:1] / sums[:, 1:2]
    r = memo(lambda x, y: r_ref[x + 2, y + 2] - step * w_ref[x + 2, y + 2])

    def gathered(start, size, stride):
        rows = pl.ds(start, size, stride=stride) if stride > 1 else pl.ds(start, size)
        return level_ref[rows, :] - step * change_ref[rows, :]

    mass_rows = level_ref[pl.ds(3, bricks, stride=8), :]
    fields = (reader(mass0_ref, 3), reader(weight0_ref, 3), reader(mass1_ref, 2), reader(weight1_ref, 2))
    z, image = cycle_and_apply(place, shifts, r, gathered, mass_rows, fields, fetched, particles, scratch)
    for x, y in INNER:
        z_ref[x, y] = z(x, y)
        image_ref[x, y] = image[x, y]
    rz = total_of((r(x, y), z(x, y)) for x, y in INNER)
    zaz = total_of((image[x, y], z(x, y)) for x, y in RIMMED)
    zw = total_of((w_ref[x + 2, y + 2], z(x, y)) for x, y in INNER)
    row = dots_row(rz, zaz, zw)
    none = jnp.zeros((12, 1, LANES), F32)

    def fill(k, carry):
        slots_ref[k, 0:12] = none
        slots_ref[k, 12] = row
        return carry

    lax.fori_loop(0, bricks, fill, 0)
    for dx in (-1, 0, 1):
        for dy in (-1, 0, 1):
            if dx == 0 and dy == 0:
                continue
            xs = [-1] if dx < 0 else [BRICK] if dx > 0 else range(BRICK)
            ys = [-1] if dy < 0 else [BRICK] if dy > 0 else range(BRICK)
            columns = [image[x, y] for x in xs for y in ys]
            there_x = (place.gx + dx >= 0) & (place.gx + dx < counts[0])
            there_y = (place.gy + dy >= 0) & (place.gy + dy < counts[1])

            @pl.when(there_x & there_y)
            def _(columns=columns, dx=dx, dy=dy):
                other = (place.gx + dx) * counts[1] + place.gy + dy
                for k, column in enumerate(columns):
                    for m in range(3):
                        slots_ref[other, 3 * k + m] = column[m : m + 1]


def last_kernel(counts, slots_ref, change_ref, z1_ref, z2_ref, r_ref, w_ref, image_ref, solution_ref, residual_ref):
    place = Place(*counts)
    bricks = counts[0] * counts[1]
    sums1 = sums_of(change_ref, bricks, 7, 8)
    sums2 = jnp.sum(slots_ref[:, 12], axis=0)
    rz1, zaz1 = sums1[:, 0:1], sums1[:, 1:2]
    rz2, zaz2, zw = sums2[:, 0:1], sums2[:, 1:2], sums2[:, 2:3]
    step1 = rz1 / zaz1
    ratio = rz2 / rz1
    step2 = rz2 / (zaz2 + 2.0 * ratio * zw + ratio * ratio * zaz1)
    image = {(x, y): image_ref[x, y] for x, y in INNER}
    for dx in (-1, 0, 1):
        for dy in (-1, 0, 1):
            if dx == 0 and dy == 0:
                continue
            xs = [0] if dx < 0 else [BRICK - 1] if dx > 0 else range(BRICK)
            ys = [0] if dy < 0 else [BRICK - 1] if dy > 0 else range(BRICK)
            other_x = jnp.clip(place.gx + dx, 0, counts[0] - 1)
            other_y = jnp.clip(place.gy + dy, 0, counts[1] - 1)
            other = other_x * counts[1] + other_y
            for k, (x, y) in enumerate((x, y) for x in xs for y in ys):
                rows = [slots_ref[other, 3 * k + m] for m in range(3)] + [jnp.zeros((1, LANES), F32)]
                image[x, y] = image[x, y] + place.keep(jnp.concatenate(rows, axis=0), dx, dy, 1)
    for x, y in INNER:
        w = w_ref[x + 2, y + 2]
        z1 = z1_ref[x, y]
        solution = step1 * z1 + step2 * (z2_ref[x, y] + ratio * z1)
        residual = r_ref[x + 2, y + 2] - step1 * w - step2 * (image[x, y] + ratio * w)
        for m in range(3):
            solution_ref[m, x, y : y + 1, :] = solution[m : m + 1]
            residual_ref[m, x, y : y + 1, :] = residual[m : m + 1]


def call(kernel, counts, shapes, *args, scratch=(), far=0):
    near = len(args) - far
    return pl.pallas_call(
        functools.partial(kernel, counts),
        out_shape=[jax.ShapeDtypeStruct(s, F32) for s in shapes],
        in_specs=[pl.BlockSpec(memory_space=pltpu.VMEM)] * near + [pl.BlockSpec(memory_space=pltpu.HBM)] * far,
        scratch_shapes=scratch,
        compiler_params=pltpu.CompilerParams(vmem_limit_bytes=VMEM_BYTES),
    )(*args)


def per_device(counts, right_side, node_mass, gradients, stiffness, valid, node_base):
    bricks = counts[0] * counts[1]
    blocks = gradients.shape[2]
    particles = (node_base[0, 0], stiffness[0, 0], valid[0, 0], gradients[0, 0].transpose(1, 2, 0, 3))
    tiles = 9 * (BRICK + 2) * 8
    depth = BRICK * LANES
    width = blocks * LANES
    scratch = (
        *(pltpu.VMEM(p.shape, p.dtype) for p in particles),
        pltpu.SemaphoreType.DMA((4,)),
        pltpu.VMEM((bricks + 2 * (8 + counts[1]), LANES), F32),
        pltpu.VMEM((depth, width), jnp.bfloat16),
        pltpu.VMEM((tiles, depth), jnp.bfloat16),
        pltpu.VMEM((tiles, width), jnp.bfloat16),
        pltpu.VMEM((tiles, width), F32),
        pltpu.VMEM((tiles, depth), F32),
    )
    rows = lambda columns, more=0: (-(-(3 * len(columns) + more + 1) // 8) * 8, LANES)

    fields = (right_side, node_mass)
    (own,) = call(
        pack_kernel, counts, [(4, 4, 4, LANES)], *fields, far=2,
        scratch=(*(pltpu.VMEM(p.shape, p.dtype) for p in fields), pltpu.SemaphoreType.DMA((2,))),
    )
    even, odd = exchange(own, own, "gx", counts)
    side = rows(SIDE, len(SIDE_MASS))
    wide, to_even, to_odd = call(widen_kernel, counts, [(12, 4, 4, LANES), side, side], own, even, odd)
    even, odd = exchange(to_even, to_odd, "gy", counts)
    r, *fields, slot = call(
        start_kernel, counts,
        [(8, 8, 4, LANES), (10, 10, 4, LANES), (10, 10, 4, LANES), (6, 6, 4, LANES), (6, 6, 4, LANES), (8, LANES)],
        wide, even, odd,
    )

    def share(slot):
        sent = jnp.broadcast_to(slot[None], (bricks, 8, LANES))
        return lax.all_to_all(sent, AXES, 0, 0).reshape(bricks * 8, LANES)

    level = share(slot)
    z1, image, to_even, to_odd, dots = call(
        first_kernel, counts,
        [(4, 4, 4, LANES), (6, 6, 4, LANES), rows(SIDE_X), rows(SIDE_X), (1, LANES)],
        level, r, *fields, *particles, scratch=scratch, far=4,
    )
    even, odd = exchange(to_even, to_odd, "gx", counts)
    wide, to_even, to_odd = call(
        along_x_kernel, counts, [(10, 6, 4, LANES), rows(SIDE_IMAGE), rows(SIDE_IMAGE)], image, even, odd
    )
    even, odd = exchange(to_even, to_odd, "gy", counts)
    w, slot = call(middle_kernel, counts, [(8, 8, 4, LANES), (8, LANES)], wide, even, odd, *fields, dots)
    change = share(slot)
    z2, image, slots = call(
        second_kernel, counts, [(4, 4, 4, LANES), (4, 4, 4, LANES), (bricks, 13, 1, LANES)],
        level, change, r, w, *fields, *particles, scratch=scratch, far=4,
    )
    slots = lax.all_to_all(slots, AXES, 0, 0)
    return tuple(
        call(last_kernel, counts, [right_side.shape, right_side.shape], slots, change, z1, z2, r, w, image)
    )


def solution(mesh):
    counts = (mesh.shape["gx"], mesh.shape["gy"])
    return jax.shard_map(
        functools.partial(per_device, counts),
        mesh=mesh,
        in_specs=(
            P(None, "gx", "gy", None),
            P("gx", "gy", None),
            P("gx", "gy", None, None, None, None),
            P("gx", "gy", None, None),
            P("gx", "gy", None, None),
            P("gx", "gy", None, None),
        ),
        out_specs=(P(None, "gx", "gy", None), P(None, "gx", "gy", None)),
        check_vma=False,
    )
```

```python
import functools

import jax
import jax.numpy as jnp
from jax import lax
from jax.experimental import pallas as pl
from jax.experimental.pallas import tpu as pltpu
from jax.sharding import PartitionSpec as P

POISSON = 0.3
DAMPING = 0.7
SWEEPS = 4
LANES = 128
BRICK = 4
AXES = ("gx", "gy")
VMEM_BYTES = 24 * 1024 * 1024
F32 = jnp.float32


def pairings(axis, counts):
    count_x, count_y = counts
    even, odd = [], []
    for x in range(count_x):
        for y in range(count_y):
            k, count = (x, count_x) if axis == "gx" else (y, count_y)
            move = lambda to: (to, y) if axis == "gx" else (x, to)
            even.append(((x, y), move(k ^ 1)))
            if 0 < k < count - 1:
                odd.append(((x, y), move(k + 1 if k % 2 else k - 1)))
            else:
                odd.append(((x, y), (x, y ^ 1) if axis == "gx" else (x ^ 1, y)))
    flat = lambda pairs: [(a * count_y + b, c * count_y + d) for (a, b), (c, d) in pairs]
    return flat(even), flat(odd)


def exchange(first, second, axis, counts):
    even, odd = pairings(axis, counts)
    return lax.ppermute(first, AXES, even), lax.ppermute(second, AXES, odd)


SIDE = [(x, -1) for x in range(-2, 6)] + [(x, -2) for x in range(-1, 5)]
SIDE_IMAGE = [(x, 0) for x in range(-2, 6)] + SIDE
SIDE_X = [(x, y) for x in (-2, -1) for y in range(BRICK)]
SIDE_X_IMAGE = [(x, y) for x in (-2, -1, 0) for y in range(-1, 5)]


def mirror(x, y):
    return x, BRICK - 1 - y


def mirror_x(x, y):
    return BRICK - 1 - x, y


def lane_index():
    return lax.broadcasted_iota(jnp.int32, (1, LANES), 1)


def as_f32(cond):
    return jnp.where(cond, 1.0, 0.0).astype(F32)


def turn(x, shift):
    return pltpu.roll(x, shift % LANES, x.ndim - 1)


class Place:
    def __init__(self, count_x, count_y):
        self.gx = lax.axis_index("gx")
        self.gy = lax.axis_index("gy")
        self.count_x, self.count_y = count_x, count_y
        flag = lambda cond: jnp.where(cond, 1.0, 0.0).astype(F32)
        self.even_x = flag(self.gx % 2 == 0)
        self.even_y = flag(self.gy % 2 == 0)
        self.in_x = {-1: flag(self.gx > 0), 0: None, 1: flag(self.gx < count_x - 1)}
        self.in_y = {-1: flag(self.gy > 0), 0: None, 1: flag(self.gy < count_y - 1)}

    def keep(self, value, x, y, size):
        side_x = -1 if x < 0 else 1 if x >= size else 0
        side_y = -1 if y < 0 else 1 if y >= size else 0
        if side_x:
            value = value * self.in_x[side_x]
        if side_y:
            value = value * self.in_y[side_y]
        return value


class Shifts:
    def __init__(self):
        lane = lane_index()
        self.low = {d: as_f32(lane >= d) for d in (1, 2, 4)}
        self.high = {d: as_f32(lane < LANES - d) for d in (1, 2, 4)}
        self.even = as_f32(lane % 2 == 0)
        self.odd = 1.0 - self.even
        self.half = as_f32(lane % 4 < 2)

    def beside(self, x, d):
        return turn(x, d) * self.low[d] + turn(x, -d) * self.high[d]

    def pair_sum(self, x):
        t = (x + turn(x, -1)) * self.even
        return t + turn(t, 1)

    def quad_sum(self, x):
        t = (x + turn(x, -2)) * self.half
        return t + turn(t, 2)


def memo(fn):
    kept = {}

    def wrapped(x, y):
        if (x, y) not in kept:
            kept[(x, y)] = fn(x, y)
        return kept[(x, y)]

    return wrapped


def grid_apply(e, mass, coupling, shifts, step):
    def at(x, y):
        c = e(x, y)
        beside = e(x + 1, y) + e(x - 1, y) + e(x, y + 1) + e(x, y - 1) + shifts.beside(c, step)
        return mass(x, y) * c + coupling * (6.0 * c - beside)

    return at


def contribution(w, mass0, weight0, columns, cells, shifts):
    inside = set(columns)
    e0 = memo(lambda x, y: weight0(x, y) * w(x, y) if (x, y) in inside else None)

    def rest(x, y):
        beside = [v for v in (e0(x + 1, y), e0(x - 1, y), e0(x, y + 1), e0(x, y - 1)) if v is not None]
        total = sum(beside) if beside else None
        c = e0(x, y)
        if c is None:
            return total
        near = shifts.beside(c, 1) if total is None else total + shifts.beside(c, 1)
        return w(x, y) - (mass0(x, y) * c + (6.0 * c - near))

    out = {}
    for x, y in cells:
        parts = [rest(2 * x + i, 2 * y + j) for i in range(2) for j in range(2)]
        out[x, y] = shifts.pair_sum(sum(v for v in parts if v is not None))
    return out


class Levels:
    def __init__(self, count_x, count_y, shifts):
        rows = count_x * count_y
        lane = lax.broadcasted_iota(jnp.int32, (rows, LANES), 1)
        row = lax.broadcasted_iota(jnp.int32, (rows, LANES), 0)
        column = row % count_y
        self.rows, self.count_y, self.shifts = rows, count_y, shifts
        self.x_low, self.x_high = as_f32(row >= count_y), as_f32(row < rows - count_y)
        self.y_low, self.y_high = as_f32(column > 0), as_f32(column < count_y - 1)
        self.even = as_f32(lane % 2 == 0)
        self.odd = 1.0 - self.even
        self.from_low = self.y_low * self.even
        self.from_high = self.y_high * self.odd

    def below_x(self, v):
        return pltpu.roll(v, self.count_y, 0) * self.x_low

    def above_x(self, v):
        return pltpu.roll(v, self.rows - self.count_y, 0) * self.x_high

    def row(self, v, k):
        return pltpu.roll(v, k % self.rows, 0)

    def gather_y(self, first, second):
        return (first + self.row(second, 1) * self.y_low) * self.even + (
            second + self.row(first, -1) * self.y_high
        ) * self.odd

    def apply_1(self, v, mass):
        out = []
        for x in range(2):
            c, other = v[x], v[1 - x]
            swapped = turn(c, -1) * self.even + turn(c, 1) * self.odd
            near = other + (self.below_x(other) if x == 0 else self.above_x(other))
            near = near + swapped + self.row(swapped, 1) * self.from_low + self.row(swapped, -1) * self.from_high
            near = near + self.shifts.beside(c, 2)
            out.append(mass[x] * c + 2.0 * (6.0 * c - near))
        return out

    def solve_2(self, r2, mass, weight):
        e = weight * r2
        for _ in range(SWEEPS - 1):
            near = self.shifts.beside(e, 4) + self.below_x(e) + self.above_x(e)
            near = near + self.row(e, 1) * self.y_low + self.row(e, -1) * self.y_high
            e = e + weight * (r2 - (mass * e + 4.0 * (6.0 * e - near)))
        return e

    def sum_2(self, v):
        return self.shifts.quad_sum(self.shifts.pair_sum(v[0] + v[1]))

    def solve(self, r1, mass1):
        weight1 = [DAMPING / (m + 12.0) for m in mass1]
        mass2 = self.sum_2(mass1)
        weight2 = DAMPING / (mass2 + 24.0)
        out = []
        for r in r1:
            e = [weight1[x] * r[x] for x in range(2)]
            g = self.apply_1(e, mass1)
            e2 = self.solve_2(self.sum_2([r[x] - g[x] for x in range(2)]), mass2, weight2)
            e = [e[x] + e2 for x in range(2)]
            g = self.apply_1(e, mass1)
            out.append([e[x] + weight1[x] * (r[x] - g[x]) for x in range(2)])
        return out


def pack_y(cells, x, shifts):
    return (
        cells[x, 0] * shifts.even + cells[x, -1] * shifts.odd,
        cells[x, 1] * shifts.odd + cells[x, 2] * shifts.even,
    )


def put_rows(slot_ref, row, column):
    for m in range(3):
        slot_ref[row + m] = column[m : m + 1]


def fine_level(r, f1, mass0, weight0, place, shifts):
    e0 = memo(lambda x, y: weight0(x, y) * r(x, y) + f1(x // 2, y // 2))
    g0 = grid_apply(e0, mass0, 1.0, shifts, 1)
    return memo(lambda x, y: place.keep(e0(x, y) + weight0(x, y) * (r(x, y) - g0(x, y)), x, y, BRICK))


def stiffness_apply(z, fetched, base_ref, stiff_ref, valid_ref, grad_ref, hot, nodes, forces, picked, spread_sums, shifts):
    blocks = grad_ref.shape[2]
    turns = [(b, c) for b in range(3) for c in range(3)]
    span = BRICK + 2

    def halves(x):
        high = x.astype(jnp.bfloat16).astype(F32)
        return jnp.concatenate([high, x - high], axis=0)

    split = {}
    for x in range(span):
        for y in range(span):
            whole = halves(z(x - 1, y - 1))
            split[x, y, 1] = whole
            split[x, y, 0] = turn(whole, 1) * shifts.low[1]
            split[x, y, 2] = turn(whole, -1) * shifts.high[1]
    for u, (b, c) in enumerate(turns):
        for j in range(BRICK):
            for x in range(0, span, 2):
                pair = jnp.concatenate([split[x, j + b, c], split[x + 1, j + b, c]], axis=0).astype(jnp.bfloat16)
                row = (u * span + x) * 8
                nodes[row : row + 16, j * LANES : (j + 1) * LANES] = pair

    fetched()
    base = base_ref[...]
    plane = base // (LANES + 2)
    depth = base - plane * (LANES + 2)
    node_x = plane // span
    node_y = plane - node_x * span
    sub = lax.broadcasted_iota(jnp.int32, (LANES, LANES), 0)
    for s in range(blocks):
        for j in range(BRICK):
            wanted = jnp.where(node_y[s : s + 1] == j, depth[s : s + 1], -1)
            hot[j * LANES : (j + 1) * LANES, s * LANES : (s + 1) * LANES] = as_f32(sub == wanted).astype(jnp.bfloat16)
    picked[...] = jnp.dot(nodes[...], hot[...], preferred_element_type=F32)

    first = POISSON / ((1.0 + POISSON) * (1.0 - 2.0 * POISSON))
    shear_of = 0.5 / (1.0 + POISSON)
    row8 = lax.broadcasted_iota(jnp.int32, (8, LANES), 0)
    row_is = [as_f32(row8 % 4 == m) for m in range(3)]
    is_high = row8 < 4
    zero = jnp.zeros((8, LANES), F32)
    wide = lambda row: jnp.broadcast_to(row, (8, LANES))
    for s in range(blocks):
        lanes = slice(s * LANES, (s + 1) * LANES)
        grad = lambda l, a, b, c: wide(grad_ref[l, 9 * a + 3 * b + c, s : s + 1, :])
        at_x = [wide(node_x[s : s + 1]) == i for i in range(BRICK)]
        h = [None] * 3
        for u, (b, c) in enumerate(turns):
            tiles = [picked[(u * span + x) * 8 : (u * span + x) * 8 + 8, lanes] for x in range(span)]
            for a in range(3):
                value = tiles[3 + a]
                for i in (2, 1, 0):
                    value = jnp.where(at_x[i], tiles[i + a], value)
                for l in range(3):
                    term = value * grad(l, a, b, c)
                    h[l] = term if h[l] is None else h[l] + term
        h = [x[0:4] + x[4:8] for x in h]
        h = [[h[l][m : m + 1] for l in range(3)] for m in range(3)]
        effective = stiff_ref[s : s + 1] * valid_ref[s : s + 1].astype(F32)
        shear = effective * shear_of
        bulk = effective * first * (h[0][0] + h[1][1] + h[2][2])
        stress = []
        for l in range(3):
            column = 0.0
            for m in range(3):
                entry = shear * (h[m][l] + h[l][m])
                if l == m:
                    entry = entry + bulk
                column = column + wide(entry) * row_is[m]
            stress.append(column)
        for u, (b, c) in enumerate(turns):
            parts = []
            for a in range(3):
                f = stress[0] * grad(0, a, b, c) + stress[1] * grad(1, a, b, c) + stress[2] * grad(2, a, b, c)
                high = f.astype(jnp.bfloat16).astype(F32)
                parts.append(jnp.where(is_high, high, f - high))
            tiles = []
            for x in range(span):
                tile = zero
                for a in range(3):
                    if 0 <= x - a < BRICK:
                        tile = jnp.where(at_x[x - a], parts[a], tile)
                tiles.append(tile)
            for x in range(0, span, 2):
                row = (u * span + x) * 8
                pair = jnp.concatenate([tiles[x], tiles[x + 1]], axis=0).astype(jnp.bfloat16)
                forces[row : row + 16, lanes] = pair
    spread_sums[...] = lax.dot_general(
        forces[...], hot[...], (((1,), (1,)), ((), ())), preferred_element_type=F32
    )
    out = {}
    for x in range(span):
        for y in range(span):
            sums = [0.0, 0.0, 0.0]
            for u, (b, c) in enumerate(turns):
                j = y - b
                if 0 <= j < BRICK:
                    row = (u * span + x) * 8
                    sums[c] = sums[c] + spread_sums[row : row + 8, j * LANES : (j + 1) * LANES]
            total = sums[1] + turn(sums[0], -1) * shifts.high[1] + turn(sums[2], 1) * shifts.low[1]
            out[x - 1, y - 1] = total[0:4] + total[4:8]
    return out


def fetch(sources, targets, semaphores):
    copies = [pltpu.make_async_copy(a, b, semaphores.at[k]) for k, (a, b) in enumerate(zip(sources, targets))]
    for copy in copies:
        copy.start()

    def wait():
        for copy in copies:
            copy.wait()

    return wait


def side_parts(even_ref, odd_ref, is_even, inside_low, inside_high):
    odd = 1.0 - is_even
    below_odd, below_even = inside_low * is_even, inside_low * odd
    above_odd, above_even = inside_high * odd, inside_high * is_even

    def below(row, size):
        return odd_ref[row : row + size, :] * below_odd + even_ref[row : row + size, :] * below_even

    def above(row, size):
        return odd_ref[row : row + size, :] * above_odd + even_ref[row : row + size, :] * above_even

    return below, above


def put_sides(to_even_ref, to_odd_ref, row, size, up, down, is_even):
    odd = 1.0 - is_even
    to_even_ref[row : row + size, :] = (up * is_even + down * odd)[0:size]
    to_odd_ref[row : row + size, :] = (down * is_even + up * odd)[0:size]


def clear_tail(*refs):
    for ref in refs:
        ref[ref.shape[0] - 8 :, :] = jnp.zeros((8, LANES), F32)


def weight_of(mass):
    return DAMPING / (mass + 6.0)


def spread_mass(column):
    return jnp.broadcast_to(column[3:4], (4, LANES))


def live_rows():
    return as_f32(lax.broadcasted_iota(jnp.int32, (4, LANES), 0) < 3)


FIRST_ROWS = 20
SECOND_ROWS = 13


def pack_kernel(counts, right_in, mass_in, own_ref, even_ref, odd_ref, slot_ref, right_ref, mass_ref, semaphores):
    fetch((right_in, mass_in), (right_ref, mass_ref), semaphores)()
    place, shifts = Place(*counts), Shifts()
    own = {}
    for x in range(BRICK):
        for y in range(BRICK):
            rows = [right_ref[m, x, y : y + 1, :] for m in range(3)] + [mass_ref[x, y : y + 1, :]]
            own[x, y] = jnp.concatenate(rows, axis=0)
            own_ref[x, y] = own[x, y]
    odd_x = 1.0 - place.even_x
    for k, (x, y) in enumerate(SIDE_X):
        up, down = own[x + 4, y], own[-1 - x, y]
        even_ref[k] = up * place.even_x + down * odd_x
        odd_ref[k] = down * place.even_x + up * odd_x
    live = live_rows()
    mass0 = memo(lambda x, y: spread_mass(own[x, y]))
    weight0 = memo(lambda x, y: weight_of(mass0(x, y)))
    r = memo(lambda x, y: own[x, y] * live)
    cells = [(x, y) for x in (0, 1) for y in range(-1, 3)] + [(x, y) for x in (-1, 2) for y in (0, 1)]
    part = contribution(r, mass0, weight0, INNER, cells, shifts)
    for x in (0, 1):
        for k, column in enumerate(pack_y(part, x, shifts)):
            put_rows(slot_ref, 6 * x + 3 * k, column)
    for k, x in enumerate((-1, 2)):
        put_rows(slot_ref, 12 + 3 * k, part[x, 0] * shifts.even + part[x, 1] * shifts.odd)
    for x in (0, 1):
        mass1 = [
            shifts.pair_sum(sum(own[2 * x + i, 2 * y + j][3:4] for i in range(2) for j in range(2))) for y in (0, 1)
        ]
        slot_ref[18 + x] = mass1[0] * shifts.even + mass1[1] * shifts.odd


def widen_kernel(counts, own_ref, even_ref, odd_ref, wide_ref, to_even_ref, to_odd_ref):
    place = Place(*counts)
    odd_x = 1.0 - place.even_x
    left = (place.in_x[-1] * place.even_x, place.in_x[-1] * odd_x)
    right = (place.in_x[1] * odd_x, place.in_x[1] * place.even_x)

    def value(x, y):
        if 0 <= x < BRICK:
            return own_ref[x, y]
        odd, even = left if x < 0 else right
        k = SIDE_X.index((x, y) if x < 0 else mirror_x(x, y))
        return odd_ref[k] * odd + even_ref[k] * even

    value = memo(value)
    for x in range(-2, 6):
        for y in range(BRICK):
            wide_ref[x + 2, y] = value(x, y)
    odd_y = 1.0 - place.even_y
    for k, (x, y) in enumerate(SIDE):
        up, down = value(x, y + 4), value(x, -1 - y)
        to_even_ref[k] = up * place.even_y + down * odd_y
        to_odd_ref[k] = down * place.even_y + up * odd_y


def start_kernel(counts, wide_ref, even_ref, odd_ref, r_ref, mass0_ref, weight0_ref):
    place = Place(*counts)
    live = live_rows()
    odd_y = 1.0 - place.even_y
    below = (place.in_y[-1] * place.even_y, place.in_y[-1] * odd_y)
    above = (place.in_y[1] * odd_y, place.in_y[1] * place.even_y)
    for x in range(-2, 6):
        for y in range(-2, 6):
            if 0 <= y < BRICK:
                value = wide_ref[x + 2, y]
            else:
                key = (x, y) if y < 0 else mirror(x, y)
                odd, even = below if y < 0 else above
                if key in SIDE:
                    k = SIDE.index(key)
                    value = odd_ref[k] * odd + even_ref[k] * even
                else:
                    value = jnp.zeros((4, LANES), F32)
            r_ref[x + 2, y + 2] = value * live
            mass = spread_mass(value)
            mass0_ref[x + 2, y + 2] = mass
            weight0_ref[x + 2, y + 2] = weight_of(mass)


def reader(ref, offset):
    return memo(lambda x, y: ref[x + offset, y + offset])


def cycle_and_apply(place, shifts, levels, r, r1, mass1, fields, fetched, particles, scratch):
    mass0, weight0 = fields
    coarse, *work = scratch
    margin = 8 * (place.count_y + 1)
    coarse[...] = jnp.zeros_like(coarse)
    for m, pair in enumerate(levels.solve(r1, mass1)):
        for x in range(2):
            coarse[pl.ds(margin + 4 * x + m, levels.rows, stride=8), :] = pair[x]

    def neighbour(x, y):
        brick = (place.gx + x) * place.count_y + place.gy + y
        rows = coarse[pl.ds(pl.multiple_of(margin + brick * 8, 8), 8), :]
        first, second = rows * shifts.even, rows * shifts.odd
        return first + turn(first, 1), second + turn(second, -1)

    neighbour = memo(neighbour)

    def f1_at(x, y):
        both = neighbour(x // 2, y // 2)[y % 2]
        return place.keep(both[4 * (x % 2) : 4 * (x % 2) + 4], x, y, 2)

    z = fine_level(r, memo(f1_at), mass0, weight0, place, shifts)
    image = stiffness_apply(z, fetched, *particles, *work, shifts)
    for x, y in INNER:
        image[x, y] = image[x, y] + mass0(x, y) * z(x, y)
    return z, image


def total_of(pairs):
    acc = 0.0
    for a, b in pairs:
        acc = acc + a * b
    return jnp.sum(jnp.sum(acc, axis=0, keepdims=True), axis=1, keepdims=True)


def dots_row(*values):
    lane = lane_index()
    row = 0.0
    for k, v in enumerate(values):
        row = row + as_f32(lane == k) * v
    return row


INNER = [(x, y) for x in range(BRICK) for y in range(BRICK)]
RIMMED = [(x, y) for x in range(-1, BRICK + 1) for y in range(-1, BRICK + 1)]


def first_kernel(counts, level_ref, r_ref, mass0_ref, weight0_ref,
                 base_in, stiff_in, valid_in, grad_in, z_ref, image_ref, even_ref, odd_ref, dots_ref, r1_ref, mass1_ref,
                 base_ref, stiff_ref, valid_ref, grad_ref, semaphores, *scratch):
    particles = (base_ref, stiff_ref, valid_ref, grad_ref)
    fetched = fetch((base_in, stiff_in, valid_in, grad_in), particles, semaphores)
    place, shifts = Place(*counts), Shifts()
    levels = Levels(*counts, shifts)
    rows = lambda q: level_ref[pl.ds(q, levels.rows, stride=FIRST_ROWS), :]
    r1 = []
    for m in range(3):
        pair = [levels.gather_y(rows(6 * x + m), rows(6 * x + 3 + m)) for x in range(2)]
        pair[1] = pair[1] + levels.above_x(rows(12 + m))
        pair[0] = pair[0] + levels.below_x(rows(15 + m))
        r1.append(pair)
    mass1 = [rows(18), rows(19)]
    for x in range(2):
        mass1_ref[x] = mass1[x]
        for m in range(3):
            r1_ref[m, x] = r1[m][x]
    r = reader(r_ref, 2)
    fields = (reader(mass0_ref, 2), reader(weight0_ref, 2))
    z, image = cycle_and_apply(place, shifts, levels, r, r1, mass1, fields, fetched, particles, scratch)
    for x, y in INNER:
        z_ref[x, y] = z(x, y)
    for x, y in RIMMED:
        image_ref[x + 1, y + 1] = image[x, y]
    clear_tail(even_ref, odd_ref)
    for k, (x, y) in enumerate(SIDE_X_IMAGE):
        put_sides(even_ref, odd_ref, 3 * k, 3, image[x + 4, y], image[-1 - x, y], place.even_x)
    rz = total_of((r(x, y), z(x, y)) for x, y in INNER)
    zaz = total_of((image[x, y], z(x, y)) for x, y in RIMMED)
    dots_ref[...] = dots_row(rz, zaz)


def along_x_kernel(counts, image_ref, even_ref, odd_ref, mass0_ref, weight0_ref, dots_ref,
                   wide_ref, to_even_ref, to_odd_ref, slot_ref):
    place, shifts = Place(*counts), Shifts()
    left, right = side_parts(even_ref, odd_ref, place.even_x, place.in_x[-1], place.in_x[1])

    def value(x, y):
        total = None
        if -1 <= x <= 4:
            total = place.keep(image_ref[x + 1, y + 1], x, y, BRICK)
        for part, key in ((left, (x, y)), (right, mirror_x(x, y))):
            if key in SIDE_X_IMAGE:
                more = place.keep(part(3 * SIDE_X_IMAGE.index(key), 4), 0, y, BRICK)
                total = more if total is None else total + more
        return total

    value = memo(value)
    clear_tail(to_even_ref, to_odd_ref)
    for k, (x, y) in enumerate(SIDE_IMAGE):
        put_sides(to_even_ref, to_odd_ref, 3 * k, 3, value(x, y + 4), value(x, -1 - y), place.even_y)
    for x in range(-2, 6):
        for y in range(-1, BRICK + 1):
            wide_ref[x + 2, y + 1] = value(x, y)
    cells = [(x, y) for x in (0, 1) for y in range(-1, 3)]
    part = contribution(value, reader(mass0_ref, 2), reader(weight0_ref, 2), RIMMED, cells, shifts)
    for x in (0, 1):
        for k, column in enumerate(pack_y(part, x, shifts)):
            put_rows(slot_ref, 6 * x + 3 * k, column)
    slot_ref[12] = dots_ref[...]


def middle_kernel(counts, wide_ref, even_ref, odd_ref, w_ref):
    place = Place(*counts)
    below, above = side_parts(even_ref, odd_ref, place.even_y, place.in_y[-1], place.in_y[1])
    live = live_rows()
    for x in range(-2, 6):
        for y in range(-2, 6):
            total = jnp.zeros((4, LANES), F32)
            if -1 <= y <= 4:
                total = total + wide_ref[x + 2, y + 1]
            for part, key in ((below, (x, y)), (above, mirror(x, y))):
                if key in SIDE_IMAGE:
                    total = total + part(3 * SIDE_IMAGE.index(key), 4)
            w_ref[x + 2, y + 2] = total * live


def sums_of(ref, count, first, stride):
    return jnp.sum(ref[pl.ds(first, count, stride=stride), :], axis=0, keepdims=True)


def second_kernel(counts, change_ref, r1_ref, mass1_ref, r_ref, w_ref, mass0_ref, weight0_ref,
                  base_in, stiff_in, valid_in, grad_in, z_ref, image_ref, slots_ref,
                  base_ref, stiff_ref, valid_ref, grad_ref, semaphores, *scratch):
    particles = (base_ref, stiff_ref, valid_ref, grad_ref)
    fetched = fetch((base_in, stiff_in, valid_in, grad_in), particles, semaphores)
    place, shifts = Place(*counts), Shifts()
    bricks = counts[0] * counts[1]
    levels = Levels(*counts, shifts)
    sums = sums_of(change_ref, bricks, 12, SECOND_ROWS)
    step = sums[:, 0:1] / sums[:, 1:2]
    r = memo(lambda x, y: r_ref[x + 2, y + 2] - step * w_ref[x + 2, y + 2])
    rows = lambda q: change_ref[pl.ds(q, bricks, stride=SECOND_ROWS), :]
    r1 = [
        [r1_ref[m, x] - step * levels.gather_y(rows(6 * x + m), rows(6 * x + 3 + m)) for x in range(2)] for m in range(3)
    ]
    fields = (reader(mass0_ref, 2), reader(weight0_ref, 2))
    mass1 = [mass1_ref[0], mass1_ref[1]]
    z, image = cycle_and_apply(place, shifts, levels, r, r1, mass1, fields, fetched, particles, scratch)
    for x, y in INNER:
        z_ref[x, y] = z(x, y)
        image_ref[x, y] = image[x, y]
    rz = total_of((r(x, y), z(x, y)) for x, y in INNER)
    zaz = total_of((image[x, y], z(x, y)) for x, y in RIMMED)
    zw = total_of((w_ref[x + 2, y + 2], z(x, y)) for x, y in INNER)
    row = dots_row(rz, zaz, zw)
    none = jnp.zeros((12, 1, LANES), F32)

    def fill(k, carry):
        slots_ref[k, 0:12] = none
        slots_ref[k, 12] = row
        return carry

    lax.fori_loop(0, bricks, fill, 0)
    for dx in (-1, 0, 1):
        for dy in (-1, 0, 1):
            if dx == 0 and dy == 0:
                continue
            xs = [-1] if dx < 0 else [BRICK] if dx > 0 else range(BRICK)
            ys = [-1] if dy < 0 else [BRICK] if dy > 0 else range(BRICK)
            columns = [image[x, y] for x in xs for y in ys]
            there_x = (place.gx + dx >= 0) & (place.gx + dx < counts[0])
            there_y = (place.gy + dy >= 0) & (place.gy + dy < counts[1])

            @pl.when(there_x & there_y)
            def _(columns=columns, dx=dx, dy=dy):
                other = (place.gx + dx) * counts[1] + place.gy + dy
                for k, column in enumerate(columns):
                    for m in range(3):
                        slots_ref[other, 3 * k + m] = column[m : m + 1]


def last_kernel(counts, slots_ref, change_ref, z1_ref, z2_ref, r_ref, w_ref, image_ref, solution_ref, residual_ref):
    place = Place(*counts)
    bricks = counts[0] * counts[1]
    sums1 = sums_of(change_ref, bricks, 12, SECOND_ROWS)
    sums2 = jnp.sum(slots_ref[:, 12], axis=0)
    rz1, zaz1 = sums1[:, 0:1], sums1[:, 1:2]
    rz2, zaz2, zw = sums2[:, 0:1], sums2[:, 1:2], sums2[:, 2:3]
    step1 = rz1 / zaz1
    ratio = rz2 / rz1
    step2 = rz2 / (zaz2 + 2.0 * ratio * zw + ratio * ratio * zaz1)
    image = {(x, y): image_ref[x, y] for x, y in INNER}
    for dx in (-1, 0, 1):
        for dy in (-1, 0, 1):
            if dx == 0 and dy == 0:
                continue
            xs = [0] if dx < 0 else [BRICK - 1] if dx > 0 else range(BRICK)
            ys = [0] if dy < 0 else [BRICK - 1] if dy > 0 else range(BRICK)
            other_x = jnp.clip(place.gx + dx, 0, counts[0] - 1)
            other_y = jnp.clip(place.gy + dy, 0, counts[1] - 1)
            other = other_x * counts[1] + other_y
            for k, (x, y) in enumerate((x, y) for x in xs for y in ys):
                rows = [slots_ref[other, 3 * k + m] for m in range(3)] + [jnp.zeros((1, LANES), F32)]
                image[x, y] = image[x, y] + place.keep(jnp.concatenate(rows, axis=0), dx, dy, 1)
    for x, y in INNER:
        w = w_ref[x + 2, y + 2]
        z1 = z1_ref[x, y]
        solution = step1 * z1 + step2 * (z2_ref[x, y] + ratio * z1)
        residual = r_ref[x + 2, y + 2] - step1 * w - step2 * (image[x, y] + ratio * w)
        for m in range(3):
            solution_ref[m, x, y : y + 1, :] = solution[m : m + 1]
            residual_ref[m, x, y : y + 1, :] = residual[m : m + 1]


def call(kernel, counts, shapes, *args, scratch=(), far=0):
    near = len(args) - far
    return pl.pallas_call(
        functools.partial(kernel, counts),
        out_shape=[jax.ShapeDtypeStruct(s, F32) for s in shapes],
        in_specs=[pl.BlockSpec(memory_space=pltpu.VMEM)] * near + [pl.BlockSpec(memory_space=pltpu.HBM)] * far,
        scratch_shapes=scratch,
        compiler_params=pltpu.CompilerParams(vmem_limit_bytes=VMEM_BYTES),
    )(*args)


def per_device(counts, right_side, node_mass, gradients, stiffness, valid, node_base):
    bricks = counts[0] * counts[1]
    blocks = gradients.shape[2]
    particles = (node_base[0, 0], stiffness[0, 0], valid[0, 0], gradients[0, 0].transpose(1, 2, 0, 3))
    tiles = 9 * (BRICK + 2) * 8
    depth = BRICK * LANES
    width = blocks * LANES
    scratch = (
        *(pltpu.VMEM(p.shape, p.dtype) for p in particles),
        pltpu.SemaphoreType.DMA((4,)),
        pltpu.VMEM((8 * (bricks + 2 * (counts[1] + 1)), LANES), F32),
        pltpu.VMEM((depth, width), jnp.bfloat16),
        pltpu.VMEM((tiles, depth), jnp.bfloat16),
        pltpu.VMEM((tiles, width), jnp.bfloat16),
        pltpu.VMEM((tiles, width), F32),
        pltpu.VMEM((tiles, depth), F32),
    )
    rows = lambda columns: (-(-(3 * len(columns) + 1) // 8) * 8, LANES)
    block = lambda *dims: (*dims, 4, LANES)

    def share(slot):
        sent = jnp.broadcast_to(slot[None], (bricks, *slot.shape))
        return lax.all_to_all(sent, AXES, 0, 0).reshape(bricks * slot.shape[0], LANES)

    fields = (right_side, node_mass)
    own, to_even, to_odd, slot = call(
        pack_kernel, counts, [block(4, 4), block(8), block(8), (FIRST_ROWS, 1, LANES)], *fields, far=2,
        scratch=(*(pltpu.VMEM(p.shape, p.dtype) for p in fields), pltpu.SemaphoreType.DMA((2,))),
    )
    level = share(slot)
    even, odd = exchange(to_even, to_odd, "gx", counts)
    side = block(len(SIDE))
    wide, to_even, to_odd = call(widen_kernel, counts, [block(8, 4), side, side], own, even, odd)
    even, odd = exchange(to_even, to_odd, "gy", counts)
    r, *fields = call(start_kernel, counts, [block(8, 8)] * 3, wide, even, odd)

    side = rows(SIDE_X_IMAGE)
    z1, image, to_even, to_odd, dots, r1, mass1 = call(
        first_kernel, counts,
        [block(4, 4), block(6, 6), side, side, (1, LANES), (3, 2, bricks, LANES), (2, bricks, LANES)],
        level, r, *fields, *particles, scratch=scratch, far=4,
    )
    even, odd = exchange(to_even, to_odd, "gx", counts)
    side = rows(SIDE_IMAGE)
    wide, to_even, to_odd, slot = call(
        along_x_kernel, counts, [block(8, 6), side, side, (SECOND_ROWS, 1, LANES)], image, even, odd, *fields, dots
    )
    change = share(slot)
    even, odd = exchange(to_even, to_odd, "gy", counts)
    (w,) = call(middle_kernel, counts, [block(8, 8)], wide, even, odd)
    z2, image, slots = call(
        second_kernel, counts, [block(4, 4), block(4, 4), (bricks, 13, 1, LANES)],
        change, r1, mass1, r, w, *fields, *particles, scratch=scratch, far=4,
    )
    slots = lax.all_to_all(slots, AXES, 0, 0)
    return tuple(
        call(last_kernel, counts, [right_side.shape, right_side.shape], slots, change, z1, z2, r, w, image)
    )


def solution(mesh):
    counts = (mesh.shape["gx"], mesh.shape["gy"])
    return jax.shard_map(
        functools.partial(per_device, counts),
        mesh=mesh,
        in_specs=(
            P(None, "gx", "gy", None),
            P("gx", "gy", None),
            P("gx", "gy", None, None, None, None),
            P("gx", "gy", None, None),
            P("gx", "gy", None, None),
            P("gx", "gy", None, None),
        ),
        out_specs=(P(None, "gx", "gy", None), P(None, "gx", "gy", None)),
        check_vma=False,
    )
```

```python
import functools

import jax
import jax.numpy as jnp
from jax import lax
from jax.experimental import pallas as pl
from jax.experimental.pallas import tpu as pltpu
from jax.sharding import PartitionSpec as P

POISSON = 0.3
DAMPING = 0.7
SWEEPS = 4
LANES = 128
BRICK = 4
AXES = ("gx", "gy")
VMEM_BYTES = 24 * 1024 * 1024
F32 = jnp.float32


def pairings(axis, counts):
    count_x, count_y = counts
    even, odd = [], []
    for x in range(count_x):
        for y in range(count_y):
            k, count = (x, count_x) if axis == "gx" else (y, count_y)
            move = lambda to: (to, y) if axis == "gx" else (x, to)
            even.append(((x, y), move(k ^ 1)))
            if 0 < k < count - 1:
                odd.append(((x, y), move(k + 1 if k % 2 else k - 1)))
            else:
                odd.append(((x, y), (x, y ^ 1) if axis == "gx" else (x ^ 1, y)))
    flat = lambda pairs: [(a * count_y + b, c * count_y + d) for (a, b), (c, d) in pairs]
    return flat(even), flat(odd)


def exchange(first, second, axis, counts):
    even, odd = pairings(axis, counts)
    return lax.ppermute(first, AXES, even), lax.ppermute(second, AXES, odd)


SIDE = [(x, -1) for x in range(-2, 6)] + [(x, -2) for x in range(-1, 5)]
SIDE_IMAGE = [(x, 0) for x in range(-2, 6)] + SIDE
SIDE_X = [(x, y) for x in (-2, -1) for y in range(BRICK)]
SIDE_X_IMAGE = [(x, y) for x in (-2, -1, 0) for y in range(-1, 5)]


def mirror(x, y):
    return x, BRICK - 1 - y


def mirror_x(x, y):
    return BRICK - 1 - x, y


def lane_index():
    return lax.broadcasted_iota(jnp.int32, (1, LANES), 1)


def as_f32(cond):
    return jnp.where(cond, 1.0, 0.0).astype(F32)


def turn(x, shift):
    return pltpu.roll(x, shift % LANES, x.ndim - 1)


class Place:
    def __init__(self, count_x, count_y):
        self.gx = lax.axis_index("gx")
        self.gy = lax.axis_index("gy")
        self.count_x, self.count_y = count_x, count_y
        flag = lambda cond: jnp.where(cond, 1.0, 0.0).astype(F32)
        self.even_x = flag(self.gx % 2 == 0)
        self.even_y = flag(self.gy % 2 == 0)
        self.in_x = {-1: flag(self.gx > 0), 0: None, 1: flag(self.gx < count_x - 1)}
        self.in_y = {-1: flag(self.gy > 0), 0: None, 1: flag(self.gy < count_y - 1)}

    def keep(self, value, x, y, size):
        side_x = -1 if x < 0 else 1 if x >= size else 0
        side_y = -1 if y < 0 else 1 if y >= size else 0
        if side_x:
            value = value * self.in_x[side_x]
        if side_y:
            value = value * self.in_y[side_y]
        return value


class Shifts:
    def __init__(self):
        lane = lane_index()
        self.low = {d: as_f32(lane >= d) for d in (1, 2, 4)}
        self.high = {d: as_f32(lane < LANES - d) for d in (1, 2, 4)}
        self.even = as_f32(lane % 2 == 0)
        self.odd = 1.0 - self.even
        self.half = as_f32(lane % 4 < 2)

    def beside(self, x, d):
        return turn(x, d) * self.low[d] + turn(x, -d) * self.high[d]

    def pair_sum(self, x):
        t = (x + turn(x, -1)) * self.even
        return t + turn(t, 1)

    def quad_sum(self, x):
        t = (x + turn(x, -2)) * self.half
        return t + turn(t, 2)


def memo(fn):
    kept = {}

    def wrapped(x, y):
        if (x, y) not in kept:
            kept[(x, y)] = fn(x, y)
        return kept[(x, y)]

    return wrapped


def grid_apply(e, mass, coupling, shifts, step):
    def at(x, y):
        c = e(x, y)
        beside = e(x + 1, y) + e(x - 1, y) + e(x, y + 1) + e(x, y - 1) + shifts.beside(c, step)
        return mass(x, y) * c + coupling * (6.0 * c - beside)

    return at


def contribution(w, mass0, weight0, columns, cells, shifts):
    inside = set(columns)
    e0 = memo(lambda x, y: weight0(x, y) * w(x, y) if (x, y) in inside else None)

    def rest(x, y):
        beside = [v for v in (e0(x + 1, y), e0(x - 1, y), e0(x, y + 1), e0(x, y - 1)) if v is not None]
        total = sum(beside) if beside else None
        c = e0(x, y)
        if c is None:
            return total
        near = shifts.beside(c, 1) if total is None else total + shifts.beside(c, 1)
        return w(x, y) - (mass0(x, y) * c + (6.0 * c - near))

    out = {}
    for x, y in cells:
        parts = [rest(2 * x + i, 2 * y + j) for i in range(2) for j in range(2)]
        out[x, y] = shifts.pair_sum(sum(v for v in parts if v is not None))
    return out


class Levels:
    def __init__(self, count_x, count_y, shifts):
        rows = count_x * count_y
        lane = lax.broadcasted_iota(jnp.int32, (rows, LANES), 1)
        row = lax.broadcasted_iota(jnp.int32, (rows, LANES), 0)
        column = row % count_y
        self.rows, self.count_y, self.shifts = rows, count_y, shifts
        self.x_low, self.x_high = as_f32(row >= count_y), as_f32(row < rows - count_y)
        self.y_low, self.y_high = as_f32(column > 0), as_f32(column < count_y - 1)
        self.even = as_f32(lane % 2 == 0)
        self.odd = 1.0 - self.even
        self.from_low = self.y_low * self.even
        self.from_high = self.y_high * self.odd

    def below_x(self, v):
        return pltpu.roll(v, self.count_y, 0) * self.x_low

    def above_x(self, v):
        return pltpu.roll(v, self.rows - self.count_y, 0) * self.x_high

    def row(self, v, k):
        return pltpu.roll(v, k % self.rows, 0)

    def gather_y(self, first, second):
        return (first + self.row(second, 1) * self.y_low) * self.even + (
            second + self.row(first, -1) * self.y_high
        ) * self.odd

    def apply_1(self, v, mass):
        out = []
        for x in range(2):
            c, other = v[x], v[1 - x]
            swapped = turn(c, -1) * self.even + turn(c, 1) * self.odd
            near = other + (self.below_x(other) if x == 0 else self.above_x(other))
            near = near + swapped + self.row(swapped, 1) * self.from_low + self.row(swapped, -1) * self.from_high
            near = near + self.shifts.beside(c, 2)
            out.append(mass[x] * c + 2.0 * (6.0 * c - near))
        return out

    def solve_2(self, r2, mass, weight):
        e = weight * r2
        for _ in range(SWEEPS - 1):
            near = self.shifts.beside(e, 4) + self.below_x(e) + self.above_x(e)
            near = near + self.row(e, 1) * self.y_low + self.row(e, -1) * self.y_high
            e = e + weight * (r2 - (mass * e + 4.0 * (6.0 * e - near)))
        return e

    def sum_2(self, v):
        return self.shifts.quad_sum(self.shifts.pair_sum(v[0] + v[1]))

    def solve(self, r1, mass1):
        weight1 = [DAMPING / (m + 12.0) for m in mass1]
        mass2 = self.sum_2(mass1)
        weight2 = DAMPING / (mass2 + 24.0)
        out = []
        for r in r1:
            e = [weight1[x] * r[x] for x in range(2)]
            g = self.apply_1(e, mass1)
            e2 = self.solve_2(self.sum_2([r[x] - g[x] for x in range(2)]), mass2, weight2)
            e = [e[x] + e2 for x in range(2)]
            g = self.apply_1(e, mass1)
            out.append([e[x] + weight1[x] * (r[x] - g[x]) for x in range(2)])
        return out


def pack_y(cells, x, shifts):
    return (
        cells[x, 0] * shifts.even + cells[x, -1] * shifts.odd,
        cells[x, 1] * shifts.odd + cells[x, 2] * shifts.even,
    )


def put_rows(slot_ref, row, column):
    for m in range(3):
        slot_ref[row + m] = column[m : m + 1]


def fine_level(r, f1, mass0, weight0, place, shifts):
    e0 = memo(lambda x, y: weight0(x, y) * r(x, y) + f1(x // 2, y // 2))
    g0 = grid_apply(e0, mass0, 1.0, shifts, 1)
    return memo(lambda x, y: place.keep(e0(x, y) + weight0(x, y) * (r(x, y) - g0(x, y)), x, y, BRICK))


def stiffness_apply(z, hot, x_ref, effective_ref, grad_ref, nodes, forces, picked, spread_sums, shifts):
    blocks = grad_ref.shape[2]
    turns = [(b, c) for b in range(3) for c in range(3)]
    span = BRICK + 2

    def halves(x):
        high = x.astype(jnp.bfloat16).astype(F32)
        return jnp.concatenate([high, x - high], axis=0)

    split = {}
    for x in range(span):
        for y in range(span):
            whole = halves(z(x - 1, y - 1))
            split[x, y, 1] = whole
            split[x, y, 0] = turn(whole, 1) * shifts.low[1]
            split[x, y, 2] = turn(whole, -1) * shifts.high[1]
    for u, (b, c) in enumerate(turns):
        for j in range(BRICK):
            for x in range(0, span, 2):
                pair = jnp.concatenate([split[x, j + b, c], split[x + 1, j + b, c]], axis=0).astype(jnp.bfloat16)
                row = (u * span + x) * 8
                nodes[row : row + 16, j * LANES : (j + 1) * LANES] = pair

    node_x = x_ref[...]
    picked[...] = jnp.dot(nodes[...], hot[...], preferred_element_type=F32)

    first = POISSON / ((1.0 + POISSON) * (1.0 - 2.0 * POISSON))
    shear_of = 0.5 / (1.0 + POISSON)
    row8 = lax.broadcasted_iota(jnp.int32, (8, LANES), 0)
    row_is = [as_f32(row8 % 4 == m) for m in range(3)]
    is_high = row8 < 4
    zero = jnp.zeros((8, LANES), F32)
    wide = lambda row: jnp.broadcast_to(row, (8, LANES))
    for s in range(blocks):
        lanes = slice(s * LANES, (s + 1) * LANES)
        grad = lambda l, a, b, c: wide(grad_ref[l, 9 * a + 3 * b + c, s : s + 1, :])
        at_x = [wide(node_x[s : s + 1]) == i for i in range(BRICK)]
        h = [None] * 3
        for u, (b, c) in enumerate(turns):
            tiles = [picked[(u * span + x) * 8 : (u * span + x) * 8 + 8, lanes] for x in range(span)]
            for a in range(3):
                value = tiles[3 + a]
                for i in (2, 1, 0):
                    value = jnp.where(at_x[i], tiles[i + a], value)
                for l in range(3):
                    term = value * grad(l, a, b, c)
                    h[l] = term if h[l] is None else h[l] + term
        h = [x[0:4] + x[4:8] for x in h]
        h = [[h[l][m : m + 1] for l in range(3)] for m in range(3)]
        effective = effective_ref[s : s + 1]
        shear = effective * shear_of
        bulk = effective * first * (h[0][0] + h[1][1] + h[2][2])
        stress = []
        for l in range(3):
            column = 0.0
            for m in range(3):
                entry = shear * (h[m][l] + h[l][m])
                if l == m:
                    entry = entry + bulk
                column = column + wide(entry) * row_is[m]
            stress.append(column)
        for u, (b, c) in enumerate(turns):
            parts = []
            for a in range(3):
                f = stress[0] * grad(0, a, b, c) + stress[1] * grad(1, a, b, c) + stress[2] * grad(2, a, b, c)
                high = f.astype(jnp.bfloat16).astype(F32)
                parts.append(jnp.where(is_high, high, f - high))
            tiles = []
            for x in range(span):
                tile = zero
                for a in range(3):
                    if 0 <= x - a < BRICK:
                        tile = jnp.where(at_x[x - a], parts[a], tile)
                tiles.append(tile)
            for x in range(0, span, 2):
                row = (u * span + x) * 8
                pair = jnp.concatenate([tiles[x], tiles[x + 1]], axis=0).astype(jnp.bfloat16)
                forces[row : row + 16, lanes] = pair
    spread_sums[...] = lax.dot_general(
        forces[...], hot[...], (((1,), (1,)), ((), ())), preferred_element_type=F32
    )
    out = {}
    for x in range(span):
        for y in range(span):
            sums = [0.0, 0.0, 0.0]
            for u, (b, c) in enumerate(turns):
                j = y - b
                if 0 <= j < BRICK:
                    row = (u * span + x) * 8
                    sums[c] = sums[c] + spread_sums[row : row + 8, j * LANES : (j + 1) * LANES]
            total = sums[1] + turn(sums[0], -1) * shifts.high[1] + turn(sums[2], 1) * shifts.low[1]
            out[x - 1, y - 1] = total[0:4] + total[4:8]
    return out


def particle_kernel(counts, base_ref, stiff_ref, valid_ref, hot_ref, x_ref, effective_ref):
    span = BRICK + 2
    base = base_ref[...]
    plane = base // (LANES + 2)
    depth = base - plane * (LANES + 2)
    node_x = plane // span
    node_y = plane - node_x * span
    x_ref[...] = node_x
    effective_ref[...] = stiff_ref[...] * valid_ref[...].astype(F32)
    sub = lax.broadcasted_iota(jnp.int32, (LANES, LANES), 0)
    for s in range(base_ref.shape[0]):
        for j in range(BRICK):
            wanted = jnp.where(node_y[s : s + 1] == j, depth[s : s + 1], -1)
            hot_ref[j * LANES : (j + 1) * LANES, s * LANES : (s + 1) * LANES] = as_f32(sub == wanted).astype(jnp.bfloat16)


def side_parts(even_ref, odd_ref, is_even, inside_low, inside_high):
    odd = 1.0 - is_even
    below_odd, below_even = inside_low * is_even, inside_low * odd
    above_odd, above_even = inside_high * odd, inside_high * is_even

    def below(row, size):
        return odd_ref[row : row + size, :] * below_odd + even_ref[row : row + size, :] * below_even

    def above(row, size):
        return odd_ref[row : row + size, :] * above_odd + even_ref[row : row + size, :] * above_even

    return below, above


def put_sides(to_even_ref, to_odd_ref, row, size, up, down, is_even):
    odd = 1.0 - is_even
    to_even_ref[row : row + size, :] = (up * is_even + down * odd)[0:size]
    to_odd_ref[row : row + size, :] = (down * is_even + up * odd)[0:size]


def clear_tail(*refs):
    for ref in refs:
        ref[ref.shape[0] - 8 :, :] = jnp.zeros((8, LANES), F32)


def weight_of(mass):
    return DAMPING / (mass + 6.0)


def spread_mass(column):
    return jnp.broadcast_to(column[3:4], (4, LANES))


def live_rows():
    return as_f32(lax.broadcasted_iota(jnp.int32, (4, LANES), 0) < 3)


FIRST_ROWS = 20
SECOND_ROWS = 13


def pack_kernel(counts, fields_ref, own_ref, even_ref, odd_ref, slot_ref):
    place, shifts = Place(*counts), Shifts()
    own = {}
    for x in range(BRICK):
        for y in range(BRICK):
            own[x, y] = jnp.concatenate([fields_ref[m, x, y : y + 1, :] for m in range(4)], axis=0)
            own_ref[x, y] = own[x, y]
    odd_x = 1.0 - place.even_x
    for k, (x, y) in enumerate(SIDE_X):
        up, down = own[x + 4, y], own[-1 - x, y]
        even_ref[k] = up * place.even_x + down * odd_x
        odd_ref[k] = down * place.even_x + up * odd_x
    live = live_rows()
    mass0 = memo(lambda x, y: spread_mass(own[x, y]))
    weight0 = memo(lambda x, y: weight_of(mass0(x, y)))
    r = memo(lambda x, y: own[x, y] * live)
    cells = [(x, y) for x in (0, 1) for y in range(-1, 3)] + [(x, y) for x in (-1, 2) for y in (0, 1)]
    part = contribution(r, mass0, weight0, INNER, cells, shifts)
    for x in (0, 1):
        for k, column in enumerate(pack_y(part, x, shifts)):
            put_rows(slot_ref, 6 * x + 3 * k, column)
    for k, x in enumerate((-1, 2)):
        put_rows(slot_ref, 12 + 3 * k, part[x, 0] * shifts.even + part[x, 1] * shifts.odd)
    for x in (0, 1):
        mass1 = [
            shifts.pair_sum(sum(own[2 * x + i, 2 * y + j][3:4] for i in range(2) for j in range(2))) for y in (0, 1)
        ]
        slot_ref[18 + x] = mass1[0] * shifts.even + mass1[1] * shifts.odd


def widen_kernel(counts, own_ref, even_ref, odd_ref, wide_ref, to_even_ref, to_odd_ref):
    place = Place(*counts)
    odd_x = 1.0 - place.even_x
    left = (place.in_x[-1] * place.even_x, place.in_x[-1] * odd_x)
    right = (place.in_x[1] * odd_x, place.in_x[1] * place.even_x)

    def value(x, y):
        if 0 <= x < BRICK:
            return own_ref[x, y]
        odd, even = left if x < 0 else right
        k = SIDE_X.index((x, y) if x < 0 else mirror_x(x, y))
        return odd_ref[k] * odd + even_ref[k] * even

    value = memo(value)
    for x in range(-2, 6):
        for y in range(BRICK):
            wide_ref[x + 2, y] = value(x, y)
    odd_y = 1.0 - place.even_y
    for k, (x, y) in enumerate(SIDE):
        up, down = value(x, y + 4), value(x, -1 - y)
        to_even_ref[k] = up * place.even_y + down * odd_y
        to_odd_ref[k] = down * place.even_y + up * odd_y


def start_kernel(counts, wide_ref, even_ref, odd_ref, r_ref, mass0_ref, weight0_ref):
    place = Place(*counts)
    live = live_rows()
    odd_y = 1.0 - place.even_y
    below = (place.in_y[-1] * place.even_y, place.in_y[-1] * odd_y)
    above = (place.in_y[1] * odd_y, place.in_y[1] * place.even_y)
    for x in range(-2, 6):
        for y in range(-2, 6):
            if 0 <= y < BRICK:
                value = wide_ref[x + 2, y]
            else:
                key = (x, y) if y < 0 else mirror(x, y)
                odd, even = below if y < 0 else above
                if key in SIDE:
                    k = SIDE.index(key)
                    value = odd_ref[k] * odd + even_ref[k] * even
                else:
                    value = jnp.zeros((4, LANES), F32)
            r_ref[x + 2, y + 2] = value * live
            mass = spread_mass(value)
            mass0_ref[x + 2, y + 2] = mass
            weight0_ref[x + 2, y + 2] = weight_of(mass)


def reader(ref, offset):
    return memo(lambda x, y: ref[x + offset, y + offset])


def cycle_and_apply(place, shifts, levels, r, r1, mass1, fields, particles, scratch):
    mass0, weight0 = fields
    coarse, *work = scratch
    margin = 8 * (place.count_y + 1)
    coarse[...] = jnp.zeros_like(coarse)
    for m, pair in enumerate(levels.solve(r1, mass1)):
        for x in range(2):
            coarse[pl.ds(margin + 4 * x + m, levels.rows, stride=8), :] = pair[x]

    def neighbour(x, y):
        brick = (place.gx + x) * place.count_y + place.gy + y
        rows = coarse[pl.ds(pl.multiple_of(margin + brick * 8, 8), 8), :]
        first, second = rows * shifts.even, rows * shifts.odd
        return first + turn(first, 1), second + turn(second, -1)

    neighbour = memo(neighbour)

    def f1_at(x, y):
        both = neighbour(x // 2, y // 2)[y % 2]
        return place.keep(both[4 * (x % 2) : 4 * (x % 2) + 4], x, y, 2)

    z = fine_level(r, memo(f1_at), mass0, weight0, place, shifts)
    image = stiffness_apply(z, *particles, *work, shifts)
    for x, y in INNER:
        image[x, y] = image[x, y] + mass0(x, y) * z(x, y)
    return z, image


def total_of(pairs):
    acc = 0.0
    for a, b in pairs:
        acc = acc + a * b
    return jnp.sum(jnp.sum(acc, axis=0, keepdims=True), axis=1, keepdims=True)


def dots_row(*values):
    lane = lane_index()
    row = 0.0
    for k, v in enumerate(values):
        row = row + as_f32(lane == k) * v
    return row


INNER = [(x, y) for x in range(BRICK) for y in range(BRICK)]
RIMMED = [(x, y) for x in range(-1, BRICK + 1) for y in range(-1, BRICK + 1)]


def first_kernel(counts, level_ref, r_ref, mass0_ref, weight0_ref,
                 hot_ref, x_ref, effective_ref, grad_ref, z_ref, image_ref, even_ref, odd_ref, dots_ref, r1_ref, mass1_ref,
                 *scratch):
    particles = (hot_ref, x_ref, effective_ref, grad_ref)
    place, shifts = Place(*counts), Shifts()
    levels = Levels(*counts, shifts)
    rows = lambda q: level_ref[pl.ds(q, levels.rows, stride=FIRST_ROWS), :]
    r1 = []
    for m in range(3):
        pair = [levels.gather_y(rows(6 * x + m), rows(6 * x + 3 + m)) for x in range(2)]
        pair[1] = pair[1] + levels.above_x(rows(12 + m))
        pair[0] = pair[0] + levels.below_x(rows(15 + m))
        r1.append(pair)
    mass1 = [rows(18), rows(19)]
    for x in range(2):
        mass1_ref[x] = mass1[x]
        for m in range(3):
            r1_ref[m, x] = r1[m][x]
    r = reader(r_ref, 2)
    fields = (reader(mass0_ref, 2), reader(weight0_ref, 2))
    z, image = cycle_and_apply(place, shifts, levels, r, r1, mass1, fields, particles, scratch)
    for x, y in INNER:
        z_ref[x, y] = z(x, y)
    for x, y in RIMMED:
        image_ref[x + 1, y + 1] = image[x, y]
    clear_tail(even_ref, odd_ref)
    for k, (x, y) in enumerate(SIDE_X_IMAGE):
        put_sides(even_ref, odd_ref, 3 * k, 3, image[x + 4, y], image[-1 - x, y], place.even_x)
    rz = total_of((r(x, y), z(x, y)) for x, y in INNER)
    zaz = total_of((image[x, y], z(x, y)) for x, y in RIMMED)
    dots_ref[...] = dots_row(rz, zaz)


def along_x_kernel(counts, image_ref, even_ref, odd_ref, mass0_ref, weight0_ref, dots_ref,
                   wide_ref, to_even_ref, to_odd_ref, slot_ref):
    place, shifts = Place(*counts), Shifts()
    left, right = side_parts(even_ref, odd_ref, place.even_x, place.in_x[-1], place.in_x[1])

    def value(x, y):
        total = None
        if -1 <= x <= 4:
            total = place.keep(image_ref[x + 1, y + 1], x, y, BRICK)
        for part, key in ((left, (x, y)), (right, mirror_x(x, y))):
            if key in SIDE_X_IMAGE:
                more = place.keep(part(3 * SIDE_X_IMAGE.index(key), 4), 0, y, BRICK)
                total = more if total is None else total + more
        return total

    value = memo(value)
    clear_tail(to_even_ref, to_odd_ref)
    for k, (x, y) in enumerate(SIDE_IMAGE):
        put_sides(to_even_ref, to_odd_ref, 3 * k, 3, value(x, y + 4), value(x, -1 - y), place.even_y)
    for x in range(-2, 6):
        for y in range(-1, BRICK + 1):
            wide_ref[x + 2, y + 1] = value(x, y)
    cells = [(x, y) for x in (0, 1) for y in range(-1, 3)]
    part = contribution(value, reader(mass0_ref, 2), reader(weight0_ref, 2), RIMMED, cells, shifts)
    for x in (0, 1):
        for k, column in enumerate(pack_y(part, x, shifts)):
            put_rows(slot_ref, 6 * x + 3 * k, column)
    slot_ref[12] = dots_ref[...]


def middle_kernel(counts, wide_ref, even_ref, odd_ref, w_ref):
    place = Place(*counts)
    below, above = side_parts(even_ref, odd_ref, place.even_y, place.in_y[-1], place.in_y[1])
    live = live_rows()
    for x in range(-2, 6):
        for y in range(-2, 6):
            total = jnp.zeros((4, LANES), F32)
            if -1 <= y <= 4:
                total = total + wide_ref[x + 2, y + 1]
            for part, key in ((below, (x, y)), (above, mirror(x, y))):
                if key in SIDE_IMAGE:
                    total = total + part(3 * SIDE_IMAGE.index(key), 4)
            w_ref[x + 2, y + 2] = total * live


def sums_of(ref, count, first, stride):
    return jnp.sum(ref[pl.ds(first, count, stride=stride), :], axis=0, keepdims=True)


def second_kernel(counts, change_ref, r1_ref, mass1_ref, r_ref, w_ref, mass0_ref, weight0_ref,
                  hot_ref, x_ref, effective_ref, grad_ref, z_ref, image_ref, x_even_ref, x_odd_ref, y_even_ref, y_odd_ref,
                  slots_ref, *scratch):
    particles = (hot_ref, x_ref, effective_ref, grad_ref)
    place, shifts = Place(*counts), Shifts()
    bricks = counts[0] * counts[1]
    levels = Levels(*counts, shifts)
    sums = sums_of(change_ref, bricks, 12, SECOND_ROWS)
    step = sums[:, 0:1] / sums[:, 1:2]
    r = memo(lambda x, y: r_ref[x + 2, y + 2] - step * w_ref[x + 2, y + 2])
    rows = lambda q: change_ref[pl.ds(q, bricks, stride=SECOND_ROWS), :]
    r1 = [
        [r1_ref[m, x] - step * levels.gather_y(rows(6 * x + m), rows(6 * x + 3 + m)) for x in range(2)] for m in range(3)
    ]
    fields = (reader(mass0_ref, 2), reader(weight0_ref, 2))
    mass1 = [mass1_ref[0], mass1_ref[1]]
    z, image = cycle_and_apply(place, shifts, levels, r, r1, mass1, fields, particles, scratch)
    for x, y in INNER:
        z_ref[x, y] = z(x, y)
        image_ref[x, y] = image[x, y]
    rz = total_of((r(x, y), z(x, y)) for x, y in INNER)
    zaz = total_of((image[x, y], z(x, y)) for x, y in RIMMED)
    zw = total_of((w_ref[x + 2, y + 2], z(x, y)) for x, y in INNER)
    row = dots_row(rz, zaz, zw)
    none = jnp.zeros((3, 1, LANES), F32)

    def fill(k, carry):
        slots_ref[k, 0:3] = none
        slots_ref[k, 3] = row
        return carry

    lax.fori_loop(0, bricks, fill, 0)
    for dx in (-1, 1):
        for dy in (-1, 1):
            there_x = (place.gx + dx >= 0) & (place.gx + dx < counts[0])
            there_y = (place.gy + dy >= 0) & (place.gy + dy < counts[1])
            column = image[BRICK if dx > 0 else -1, BRICK if dy > 0 else -1]

            @pl.when(there_x & there_y)
            def _(column=column, dx=dx, dy=dy):
                other = (place.gx + dx) * counts[1] + place.gy + dy
                for m in range(3):
                    slots_ref[other, m] = column[m : m + 1]

    clear_tail(x_even_ref, x_odd_ref, y_even_ref, y_odd_ref)
    for k in range(BRICK):
        put_sides(x_even_ref, x_odd_ref, 3 * k, 3, image[BRICK, k], image[-1, k], place.even_x)
        put_sides(y_even_ref, y_odd_ref, 3 * k, 3, image[k, BRICK], image[k, -1], place.even_y)


def last_kernel(counts, slots_ref, x_even_ref, x_odd_ref, y_even_ref, y_odd_ref, change_ref, z1_ref, z2_ref, r_ref, w_ref, image_ref, solution_ref, residual_ref):
    place = Place(*counts)
    bricks = counts[0] * counts[1]
    sums1 = sums_of(change_ref, bricks, 12, SECOND_ROWS)
    sums2 = jnp.sum(slots_ref[:, 3], axis=0)
    rz1, zaz1 = sums1[:, 0:1], sums1[:, 1:2]
    rz2, zaz2, zw = sums2[:, 0:1], sums2[:, 1:2], sums2[:, 2:3]
    step1 = rz1 / zaz1
    ratio = rz2 / rz1
    step2 = rz2 / (zaz2 + 2.0 * ratio * zw + ratio * ratio * zaz1)
    image = {(x, y): image_ref[x, y] for x, y in INNER}
    left, right = side_parts(x_even_ref, x_odd_ref, place.even_x, place.in_x[-1], place.in_x[1])
    below, above = side_parts(y_even_ref, y_odd_ref, place.even_y, place.in_y[-1], place.in_y[1])
    end = BRICK - 1
    for k in range(BRICK):
        for at, part in (((0, k), left), ((end, k), right), ((k, 0), below), ((k, end), above)):
            image[at] = image[at] + part(3 * k, 4)
    for dx in (-1, 1):
        for dy in (-1, 1):
            other_x = jnp.clip(place.gx + dx, 0, counts[0] - 1)
            other_y = jnp.clip(place.gy + dy, 0, counts[1] - 1)
            other = other_x * counts[1] + other_y
            column = jnp.concatenate([slots_ref[other, m] for m in range(3)] + [jnp.zeros((1, LANES), F32)], axis=0)
            at = (end if dx > 0 else 0, end if dy > 0 else 0)
            image[at] = image[at] + place.keep(column, dx, dy, 1)
    for x, y in INNER:
        w = w_ref[x + 2, y + 2]
        z1 = z1_ref[x, y]
        solution = step1 * z1 + step2 * (z2_ref[x, y] + ratio * z1)
        residual = r_ref[x + 2, y + 2] - step1 * w - step2 * (image[x, y] + ratio * w)
        for m in range(3):
            solution_ref[m, x, y : y + 1, :] = solution[m : m + 1]
            residual_ref[m, x, y : y + 1, :] = residual[m : m + 1]


def call(kernel, counts, shapes, *args, scratch=()):
    shapes = [s if isinstance(s[0], tuple) else (s, F32) for s in shapes]
    return pl.pallas_call(
        functools.partial(kernel, counts),
        out_shape=[jax.ShapeDtypeStruct(*s) for s in shapes],
        scratch_shapes=scratch,
        compiler_params=pltpu.CompilerParams(vmem_limit_bytes=VMEM_BYTES),
    )(*args)


def per_device(counts, right_side, node_mass, gradients, stiffness, valid, node_base):
    bricks = counts[0] * counts[1]
    blocks = gradients.shape[2]
    tiles = 9 * (BRICK + 2) * 8
    depth = BRICK * LANES
    width = blocks * LANES
    scratch = (
        pltpu.VMEM((8 * (bricks + 2 * (counts[1] + 1)), LANES), F32),
        pltpu.VMEM((tiles, depth), jnp.bfloat16),
        pltpu.VMEM((tiles, width), jnp.bfloat16),
        pltpu.VMEM((tiles, width), F32),
        pltpu.VMEM((tiles, depth), F32),
    )
    rows = lambda columns: (-(-(3 * len(columns) + 1) // 8) * 8, LANES)
    block = lambda *dims: (*dims, 4, LANES)

    def share(slot):
        sent = jnp.broadcast_to(slot[None], (bricks, *slot.shape))
        return lax.all_to_all(sent, AXES, 0, 0).reshape(bricks * slot.shape[0], LANES)

    fields = jnp.concatenate([right_side, node_mass[None]], axis=0)
    own, to_even, to_odd, slot = call(
        pack_kernel, counts, [block(4, 4), block(8), block(8), (FIRST_ROWS, 1, LANES)], fields
    )
    level = share(slot)
    even, odd = exchange(to_even, to_odd, "gx", counts)
    side = block(len(SIDE))
    wide, to_even, to_odd = call(widen_kernel, counts, [block(8, 4), side, side], own, even, odd)
    even, odd = exchange(to_even, to_odd, "gy", counts)
    row = (blocks, LANES)
    prepared = call(
        particle_kernel, counts, [((depth, width), jnp.bfloat16), (row, jnp.int32), row],
        node_base[0, 0], stiffness[0, 0], valid[0, 0],
    )
    particles = (*prepared, gradients[0, 0].transpose(1, 2, 0, 3))
    r, *fields = call(start_kernel, counts, [block(8, 8)] * 3, wide, even, odd)

    side = rows(SIDE_X_IMAGE)
    z1, image, to_even, to_odd, dots, r1, mass1 = call(
        first_kernel, counts,
        [block(4, 4), block(6, 6), side, side, (1, LANES), (3, 2, bricks, LANES), (2, bricks, LANES)],
        level, r, *fields, *particles, scratch=scratch,
    )
    even, odd = exchange(to_even, to_odd, "gx", counts)
    side = rows(SIDE_IMAGE)
    wide, to_even, to_odd, slot = call(
        along_x_kernel, counts, [block(8, 6), side, side, (SECOND_ROWS, 1, LANES)], image, even, odd, *fields, dots
    )
    change = share(slot)
    even, odd = exchange(to_even, to_odd, "gy", counts)
    (w,) = call(middle_kernel, counts, [block(8, 8)], wide, even, odd)
    side = (2 * 8, LANES)
    z2, image, x_even, x_odd, y_even, y_odd, slots = call(
        second_kernel, counts, [block(4, 4), block(4, 4), side, side, side, side, (bricks, 4, 1, LANES)],
        change, r1, mass1, r, w, *fields, *particles, scratch=scratch,
    )
    sides = (*exchange(x_even, x_odd, "gx", counts), *exchange(y_even, y_odd, "gy", counts))
    slots = lax.all_to_all(slots, AXES, 0, 0)
    return tuple(
        call(last_kernel, counts, [right_side.shape, right_side.shape], slots, *sides, change, z1, z2, r, w, image)
    )


def solution(mesh):
    counts = (mesh.shape["gx"], mesh.shape["gy"])
    return jax.shard_map(
        functools.partial(per_device, counts),
        mesh=mesh,
        in_specs=(
            P(None, "gx", "gy", None),
            P("gx", "gy", None),
            P("gx", "gy", None, None, None, None),
            P("gx", "gy", None, None),
            P("gx", "gy", None, None),
            P("gx", "gy", None, None),
        ),
        out_specs=(P(None, "gx", "gy", None), P(None, "gx", "gy", None)),
        check_vma=False,
    )
```

```python
import functools

import jax
import jax.numpy as jnp
from jax import lax
from jax.experimental import pallas as pl
from jax.experimental.pallas import tpu as pltpu
from jax.sharding import PartitionSpec as P

POISSON = 0.3
DAMPING = 0.7
KEPT = 1.0 - DAMPING
SWEEPS = 4
LANES = 128
BRICK = 4
AXES = ("gx", "gy")
VMEM_BYTES = 24 * 1024 * 1024
F32 = jnp.float32


def pairings(axis, counts):
    count_x, count_y = counts
    even, odd = [], []
    for x in range(count_x):
        for y in range(count_y):
            k, count = (x, count_x) if axis == "gx" else (y, count_y)
            move = lambda to: (to, y) if axis == "gx" else (x, to)
            even.append(((x, y), move(k ^ 1)))
            if 0 < k < count - 1:
                odd.append(((x, y), move(k + 1 if k % 2 else k - 1)))
            else:
                odd.append(((x, y), (x, y ^ 1) if axis == "gx" else (x ^ 1, y)))
    flat = lambda pairs: [(a * count_y + b, c * count_y + d) for (a, b), (c, d) in pairs]
    return flat(even), flat(odd)


def exchange(first, second, axis, counts):
    even, odd = pairings(axis, counts)
    return lax.ppermute(first, AXES, even), lax.ppermute(second, AXES, odd)


SIDE = [(x, -1) for x in range(-2, 6)] + [(x, -2) for x in range(-1, 5)]
SIDE_X = [(x, y) for x in (-2, -1) for y in range(BRICK)]
SIDE_Y_IMAGE = [(x, y) for y in (-2, -1, 0) for x in range(-1, 5)]
SIDE_X_IMAGE = [(0, y) for y in range(-2, 6)] + [(y, x) for x, y in SIDE]


def mirror(x, y):
    return x, BRICK - 1 - y


def mirror_x(x, y):
    return BRICK - 1 - x, y


def lane_index():
    return lax.broadcasted_iota(jnp.int32, (1, LANES), 1)


def as_f32(cond):
    return jnp.where(cond, 1.0, 0.0).astype(F32)


def turn(x, shift):
    return pltpu.roll(x, shift % LANES, x.ndim - 1)


class Place:
    def __init__(self, count_x, count_y):
        self.gx = lax.axis_index("gx")
        self.gy = lax.axis_index("gy")
        self.count_x, self.count_y = count_x, count_y
        flag = lambda cond: jnp.where(cond, 1.0, 0.0).astype(F32)
        self.even_x = flag(self.gx % 2 == 0)
        self.even_y = flag(self.gy % 2 == 0)
        self.in_x = {-1: flag(self.gx > 0), 0: None, 1: flag(self.gx < count_x - 1)}
        self.in_y = {-1: flag(self.gy > 0), 0: None, 1: flag(self.gy < count_y - 1)}

    def keep(self, value, x, y, size):
        side_x = -1 if x < 0 else 1 if x >= size else 0
        side_y = -1 if y < 0 else 1 if y >= size else 0
        if side_x:
            value = value * self.in_x[side_x]
        if side_y:
            value = value * self.in_y[side_y]
        return value


class Shifts:
    def __init__(self):
        lane = lane_index()
        self.low = {d: as_f32(lane >= d) for d in (1, 2, 4)}
        self.high = {d: as_f32(lane < LANES - d) for d in (1, 2, 4)}
        self.even = as_f32(lane % 2 == 0)
        self.odd = 1.0 - self.even

    def beside(self, x, d):
        return turn(x, d) * self.low[d] + turn(x, -d) * self.high[d]

    def pair_sum(self, x):
        t = (x + turn(x, -1)) * self.even
        return t + turn(t, 1)


def memo(fn):
    kept = {}

    def wrapped(x, y):
        if (x, y) not in kept:
            kept[(x, y)] = fn(x, y)
        return kept[(x, y)]

    return wrapped


def beside_all(e, x, y, shifts, step):
    return e(x + 1, y) + e(x - 1, y) + e(x, y + 1) + e(x, y - 1) + shifts.beside(e(x, y), step)


def contribution(w, weight0, columns, cells, shifts):
    inside = set(columns)
    e0 = memo(lambda x, y: weight0(x, y) * w(x, y) if (x, y) in inside else None)

    def rest(x, y):
        beside = [v for v in (e0(x + 1, y), e0(x - 1, y), e0(x, y + 1), e0(x, y - 1)) if v is not None]
        total = sum(beside) if beside else None
        c = e0(x, y)
        if c is None:
            return total
        near = shifts.beside(c, 1) if total is None else total + shifts.beside(c, 1)
        return KEPT * w(x, y) + near

    out = {}
    for x, y in cells:
        parts = [rest(2 * x + i, 2 * y + j) for i in range(2) for j in range(2)]
        out[x, y] = shifts.pair_sum(sum(v for v in parts if v is not None))
    return out


class Levels:
    def __init__(self, count_x, count_y, shifts):
        self.count_x, self.count_y, self.shifts = count_x, count_y, shifts
        row = lax.broadcasted_iota(jnp.int32, (1, count_x, LANES), 1)
        lane = lax.broadcasted_iota(jnp.int32, (1, 1, LANES), 2)
        self.x_low, self.x_high = as_f32(row > 0), as_f32(row < count_x - 1)
        self.even = as_f32(lane % 2 == 0)
        self.odd = 1.0 - self.even
        self.first = as_f32(lane % 4 == 0)
        self.low, self.high = as_f32(lane >= 4), as_f32(lane < LANES - 4)
        self.z_low, self.z_high = self.low * as_f32(lane % 4 >= 2), self.high * as_f32(lane % 4 < 2)
        self.edge = jnp.zeros((1, count_x, LANES), F32)

    def load(self, ref, first, stride):
        pick = lambda y: ref[pl.ds(first + stride * y, self.count_x, stride=stride * self.count_y), :]
        return jnp.stack([pick(y) for y in range(self.count_y)])

    def below_x(self, v):
        return pltpu.roll(v, 1, 1) * self.x_low

    def above_x(self, v):
        return pltpu.roll(v, self.count_x - 1, 1) * self.x_high

    def below_y(self, v):
        return jnp.concatenate([self.edge, v[:-1]], axis=0)

    def above_y(self, v):
        return jnp.concatenate([v[1:], self.edge], axis=0)

    def beside(self, v, d):
        return turn(v, d) * self.low + turn(v, -d) * self.high

    def gather_y(self, first, second):
        return (first + self.below_y(second)) * self.even + (second + self.above_y(first)) * self.odd

    def quad_sum(self, v):
        v = (v + turn(v, -1) + turn(v, -2) + turn(v, -3)) * self.first
        return v + turn(v, 1) + turn(v, 2) + turn(v, 3)

    def restrict(self, r, e):
        t = e[0] + e[1]
        near = 3.0 * t + self.below_x(e[1]) + self.above_x(e[0]) + self.below_y(t) * self.odd
        near = near + self.above_y(t) * self.even + turn(t, 4) * self.z_low + turn(t, -4) * self.z_high
        return self.quad_sum(KEPT * (r[0] + r[1]) + 2.0 * near)

    def solve_2(self, r2, weight):
        start = weight * r2
        weight = 4.0 * weight
        e = start
        for _ in range(SWEEPS - 1):
            near = self.below_x(e) + self.above_x(e) + self.below_y(e) + self.above_y(e) + self.beside(e, 4)
            e = (KEPT * e + start) + weight * near
        return e


def pack_y(cells, x, shifts):
    return (
        cells[x, 0] * shifts.even + cells[x, -1] * shifts.odd,
        cells[x, 1] * shifts.odd + cells[x, 2] * shifts.even,
    )


def put_rows(slot_ref, row, column):
    for m in range(3):
        slot_ref[row + m] = column[m : m + 1]


def fine_level(r, f1, weight0, place, shifts):
    first = memo(lambda x, y: weight0(x, y) * r(x, y))
    e0 = memo(lambda x, y: first(x, y) + f1(x // 2, y // 2))

    def at(x, y):
        value = KEPT * e0(x, y) + first(x, y) + weight0(x, y) * beside_all(e0, x, y, shifts, 1)
        return place.keep(value, x, y, BRICK)

    return memo(at)


def stiffness_apply(z, hot, x_ref, effective_ref, grad_ref, nodes, forces, picked, spread_sums, shifts):
    blocks = grad_ref.shape[2]
    turns = [(b, c) for b in range(3) for c in range(3)]
    span = BRICK + 2

    def halves(x):
        high = x.astype(jnp.bfloat16).astype(F32)
        return jnp.concatenate([high, x - high], axis=0)

    split = {}
    for x in range(span):
        for y in range(span):
            whole = halves(z(x - 1, y - 1))
            split[x, y, 1] = whole
            split[x, y, 0] = turn(whole, 1) * shifts.low[1]
            split[x, y, 2] = turn(whole, -1) * shifts.high[1]
    for u, (b, c) in enumerate(turns):
        for j in range(BRICK):
            for x in range(0, span, 2):
                pair = jnp.concatenate([split[x, j + b, c], split[x + 1, j + b, c]], axis=0).astype(jnp.bfloat16)
                row = (u * span + x) * 8
                nodes[row : row + 16, j * LANES : (j + 1) * LANES] = pair

    node_x = x_ref[...]
    picked[...] = jnp.dot(nodes[...], hot[...], preferred_element_type=F32)

    first = POISSON / ((1.0 + POISSON) * (1.0 - 2.0 * POISSON))
    shear_of = 0.5 / (1.0 + POISSON)
    row8 = lax.broadcasted_iota(jnp.int32, (8, LANES), 0)
    row_is = [as_f32(row8 % 4 == m) for m in range(3)]
    is_high = row8 < 4
    zero = jnp.zeros((8, LANES), F32)
    wide = lambda row: jnp.broadcast_to(row, (8, LANES))
    for s in range(blocks):
        lanes = slice(s * LANES, (s + 1) * LANES)
        grad = lambda l, a, b, c: wide(grad_ref[l, 9 * a + 3 * b + c, s : s + 1, :])
        at_x = [wide(node_x[s : s + 1]) == i for i in range(BRICK)]
        h = [None] * 3
        for u, (b, c) in enumerate(turns):
            tiles = [picked[(u * span + x) * 8 : (u * span + x) * 8 + 8, lanes] for x in range(span)]
            for a in range(3):
                value = tiles[3 + a]
                for i in (2, 1, 0):
                    value = jnp.where(at_x[i], tiles[i + a], value)
                for l in range(3):
                    term = value * grad(l, a, b, c)
                    h[l] = term if h[l] is None else h[l] + term
        h = [x[0:4] + x[4:8] for x in h]
        h = [[h[l][m : m + 1] for l in range(3)] for m in range(3)]
        effective = effective_ref[s : s + 1]
        shear = effective * shear_of
        bulk = effective * first * (h[0][0] + h[1][1] + h[2][2])
        stress = []
        for l in range(3):
            column = 0.0
            for m in range(3):
                entry = shear * (h[m][l] + h[l][m])
                if l == m:
                    entry = entry + bulk
                column = column + wide(entry) * row_is[m]
            stress.append(column)
        for u, (b, c) in enumerate(turns):
            parts = []
            for a in range(3):
                f = stress[0] * grad(0, a, b, c) + stress[1] * grad(1, a, b, c) + stress[2] * grad(2, a, b, c)
                high = f.astype(jnp.bfloat16).astype(F32)
                parts.append(jnp.where(is_high, high, f - high))
            tiles = []
            for x in range(span):
                tile = zero
                for a in range(3):
                    if 0 <= x - a < BRICK:
                        tile = jnp.where(at_x[x - a], parts[a], tile)
                tiles.append(tile)
            for x in range(0, span, 2):
                row = (u * span + x) * 8
                pair = jnp.concatenate([tiles[x], tiles[x + 1]], axis=0).astype(jnp.bfloat16)
                forces[row : row + 16, lanes] = pair
    spread_sums[...] = lax.dot_general(
        forces[...], hot[...], (((1,), (1,)), ((), ())), preferred_element_type=F32
    )
    out = {}
    for x in range(span):
        for y in range(span):
            sums = [0.0, 0.0, 0.0]
            for u, (b, c) in enumerate(turns):
                j = y - b
                if 0 <= j < BRICK:
                    row = (u * span + x) * 8
                    sums[c] = sums[c] + spread_sums[row : row + 8, j * LANES : (j + 1) * LANES]
            total = sums[1] + turn(sums[0], -1) * shifts.high[1] + turn(sums[2], 1) * shifts.low[1]
            out[x - 1, y - 1] = total[0:4] + total[4:8]
    return out


def particle_kernel(counts, base_ref, stiff_ref, valid_ref, hot_ref, x_ref, effective_ref):
    span = BRICK + 2
    base = base_ref[...]
    plane = base // (LANES + 2)
    depth = base - plane * (LANES + 2)
    node_x = plane // span
    node_y = plane - node_x * span
    x_ref[...] = node_x
    effective_ref[...] = stiff_ref[...] * valid_ref[...].astype(F32)
    sub = lax.broadcasted_iota(jnp.int32, (LANES, LANES), 0)
    for s in range(base_ref.shape[0]):
        for j in range(BRICK):
            wanted = jnp.where(node_y[s : s + 1] == j, depth[s : s + 1], -1)
            hot_ref[j * LANES : (j + 1) * LANES, s * LANES : (s + 1) * LANES] = as_f32(sub == wanted).astype(jnp.bfloat16)


def side_parts(even_ref, odd_ref, is_even, inside_low, inside_high):
    odd = 1.0 - is_even
    below_odd, below_even = inside_low * is_even, inside_low * odd
    above_odd, above_even = inside_high * odd, inside_high * is_even

    def below(row, size):
        return odd_ref[row : row + size, :] * below_odd + even_ref[row : row + size, :] * below_even

    def above(row, size):
        return odd_ref[row : row + size, :] * above_odd + even_ref[row : row + size, :] * above_even

    return below, above


def put_sides(to_even_ref, to_odd_ref, row, size, up, down, is_even):
    odd = 1.0 - is_even
    to_even_ref[row : row + size, :] = (up * is_even + down * odd)[0:size]
    to_odd_ref[row : row + size, :] = (down * is_even + up * odd)[0:size]


def clear_tail(*refs):
    for ref in refs:
        ref[ref.shape[0] - 8 :, :] = jnp.zeros((8, LANES), F32)


def weight_of(mass):
    return DAMPING / (mass + 6.0)


def spread_mass(column):
    return jnp.broadcast_to(column[3:4], (4, LANES))


def live_rows():
    return as_f32(lax.broadcasted_iota(jnp.int32, (4, LANES), 0) < 3)


FIRST_ROWS = 20
SECOND_ROWS = 13


def pack_kernel(counts, fields_ref, own_ref, even_ref, odd_ref, slot_ref):
    place, shifts = Place(*counts), Shifts()
    own = {}
    for x in range(BRICK):
        for y in range(BRICK):
            own[x, y] = jnp.concatenate([fields_ref[m, x, y : y + 1, :] for m in range(4)], axis=0)
            own_ref[x, y] = own[x, y]
    odd_x = 1.0 - place.even_x
    for k, (x, y) in enumerate(SIDE_X):
        up, down = own[x + 4, y], own[-1 - x, y]
        even_ref[k] = up * place.even_x + down * odd_x
        odd_ref[k] = down * place.even_x + up * odd_x
    live = live_rows()
    mass0 = memo(lambda x, y: spread_mass(own[x, y]))
    weight0 = memo(lambda x, y: weight_of(mass0(x, y)))
    r = memo(lambda x, y: own[x, y] * live)
    cells = [(x, y) for x in (0, 1) for y in range(-1, 3)] + [(x, y) for x in (-1, 2) for y in (0, 1)]
    part = contribution(r, weight0, INNER, cells, shifts)
    for x in (0, 1):
        for k, column in enumerate(pack_y(part, x, shifts)):
            put_rows(slot_ref, 6 * x + 3 * k, column)
    for k, x in enumerate((-1, 2)):
        put_rows(slot_ref, 12 + 3 * k, part[x, 0] * shifts.even + part[x, 1] * shifts.odd)
    for x in (0, 1):
        mass1 = [
            shifts.pair_sum(sum(own[2 * x + i, 2 * y + j][3:4] for i in range(2) for j in range(2))) for y in (0, 1)
        ]
        slot_ref[18 + x] = mass1[0] * shifts.even + mass1[1] * shifts.odd


def widen_kernel(counts, own_ref, even_ref, odd_ref, wide_ref, to_even_ref, to_odd_ref):
    place = Place(*counts)
    odd_x = 1.0 - place.even_x
    left = (place.in_x[-1] * place.even_x, place.in_x[-1] * odd_x)
    right = (place.in_x[1] * odd_x, place.in_x[1] * place.even_x)

    def value(x, y):
        if 0 <= x < BRICK:
            return own_ref[x, y]
        odd, even = left if x < 0 else right
        k = SIDE_X.index((x, y) if x < 0 else mirror_x(x, y))
        return odd_ref[k] * odd + even_ref[k] * even

    value = memo(value)
    for x in range(-2, 6):
        for y in range(BRICK):
            wide_ref[x + 2, y] = value(x, y)
    odd_y = 1.0 - place.even_y
    for k, (x, y) in enumerate(SIDE):
        up, down = value(x, y + 4), value(x, -1 - y)
        to_even_ref[k] = up * place.even_y + down * odd_y
        to_odd_ref[k] = down * place.even_y + up * odd_y


def start_kernel(counts, wide_ref, even_ref, odd_ref, r_ref, mass0_ref, weight0_ref):
    place = Place(*counts)
    live = live_rows()
    odd_y = 1.0 - place.even_y
    below = (place.in_y[-1] * place.even_y, place.in_y[-1] * odd_y)
    above = (place.in_y[1] * odd_y, place.in_y[1] * place.even_y)
    for x in range(-2, 6):
        for y in range(-2, 6):
            if 0 <= y < BRICK:
                value = wide_ref[x + 2, y]
            else:
                key = (x, y) if y < 0 else mirror(x, y)
                odd, even = below if y < 0 else above
                if key in SIDE:
                    k = SIDE.index(key)
                    value = odd_ref[k] * odd + even_ref[k] * even
                else:
                    value = jnp.zeros((4, LANES), F32)
            r_ref[x + 2, y + 2] = value * live
            mass = spread_mass(value)
            mass0_ref[x + 2, y + 2] = mass
            weight0_ref[x + 2, y + 2] = weight_of(mass)


def reader(ref, offset):
    return memo(lambda x, y: ref[x + offset, y + offset])


def cycle_and_apply(place, shifts, levels, r, r1, mass1, fields, particles, scratch):
    mass0, weight0 = fields
    middle, coarse, *work = scratch
    width = place.count_x
    margin = 8 * (width + 1)

    def put(ref, row, value):
        for y in range(place.count_y):
            ref[pl.ds(margin + 8 * width * y + row, width, stride=8), :] = value[y]

    def get(ref, x, y):
        brick = (place.gy + y) * width + place.gx + x
        return ref[pl.ds(pl.multiple_of(margin + brick * 8, 8), 8), :]

    weight1 = [DAMPING / (m + 12.0) for m in mass1]
    weight2 = DAMPING / (levels.quad_sum(mass1[0] + mass1[1]) + 24.0)
    middle[...] = jnp.zeros_like(middle)
    coarse[...] = jnp.zeros_like(coarse)
    for x in range(2):
        put(middle, 4 * x + 3, weight1[x])
    for m in range(3):
        e = [weight1[x] * r1[m][x] for x in range(2)]
        for x in range(2):
            put(middle, 4 * x + m, e[x])
        put(coarse, m, levels.solve_2(levels.restrict(r1[m], e), weight2))

    def brick_at(x, y):
        rows = get(middle, x, y)
        first, second = rows * shifts.even, rows * shifts.odd
        return first + turn(first, 1), second + turn(second, -1)

    brick_at = memo(brick_at)

    def first_at(x, y):
        both = brick_at(x // 2, y // 2)[y % 2]
        return place.keep(both[4 * (x % 2) : 4 * (x % 2) + 4], x, y, 2)

    first = memo(first_at)
    e2 = memo(lambda x, y: place.keep(get(coarse, x, y)[0:4], x, y, 1))
    e1 = memo(lambda x, y: first(x, y) + e2(x // 2, y // 2))
    live = live_rows()

    def f1_at(x, y):
        weight = 2.0 * spread_mass(first(x, y))
        value = KEPT * e1(x, y) + first(x, y) + weight * beside_all(e1, x, y, shifts, 2)
        return place.keep(value * live, x, y, 2)

    z = fine_level(r, memo(f1_at), weight0, place, shifts)
    image = stiffness_apply(z, *particles, *work, shifts)
    for x, y in INNER:
        image[x, y] = image[x, y] + mass0(x, y) * z(x, y)
    return z, image


def total_of(pairs):
    acc = 0.0
    for a, b in pairs:
        acc = acc + a * b
    return jnp.sum(jnp.sum(acc, axis=0, keepdims=True), axis=1, keepdims=True)


def dots_row(*values):
    lane = lane_index()
    row = 0.0
    for k, v in enumerate(values):
        row = row + as_f32(lane == k) * v
    return row


INNER = [(x, y) for x in range(BRICK) for y in range(BRICK)]
RIMMED = [(x, y) for x in range(-1, BRICK + 1) for y in range(-1, BRICK + 1)]


def first_kernel(counts, level_ref, r_ref, mass0_ref, weight0_ref,
                 hot_ref, x_ref, effective_ref, grad_ref, z_ref, image_ref, even_ref, odd_ref, dots_ref, r1_ref, mass1_ref,
                 *scratch):
    particles = (hot_ref, x_ref, effective_ref, grad_ref)
    place, shifts = Place(*counts), Shifts()
    levels = Levels(*counts, shifts)
    rows = lambda q: levels.load(level_ref, q, FIRST_ROWS)
    r1 = []
    for m in range(3):
        pair = [levels.gather_y(rows(6 * x + m), rows(6 * x + 3 + m)) for x in range(2)]
        pair[1] = pair[1] + levels.above_x(rows(12 + m))
        pair[0] = pair[0] + levels.below_x(rows(15 + m))
        r1.append(pair)
    mass1 = [rows(18), rows(19)]
    for x in range(2):
        mass1_ref[x] = mass1[x]
        for m in range(3):
            r1_ref[m, x] = r1[m][x]
    r = reader(r_ref, 2)
    fields = (reader(mass0_ref, 2), reader(weight0_ref, 2))
    z, image = cycle_and_apply(place, shifts, levels, r, r1, mass1, fields, particles, scratch)
    for x, y in INNER:
        z_ref[x, y] = z(x, y)
    for x, y in RIMMED:
        image_ref[x + 1, y + 1] = image[x, y]
    clear_tail(even_ref, odd_ref)
    for k, (x, y) in enumerate(SIDE_Y_IMAGE):
        put_sides(even_ref, odd_ref, 3 * k, 3, image[x, y + 4], image[x, -1 - y], place.even_y)
    rz = total_of((r(x, y), z(x, y)) for x, y in INNER)
    zaz = total_of((image[x, y], z(x, y)) for x, y in RIMMED)
    dots_ref[...] = dots_row(rz, zaz)


def along_y_kernel(counts, image_ref, even_ref, odd_ref, weight0_ref, dots_ref,
                   long_ref, to_even_ref, to_odd_ref, slot_ref):
    place, shifts = Place(*counts), Shifts()
    below, above = side_parts(even_ref, odd_ref, place.even_y, place.in_y[-1], place.in_y[1])

    def value(x, y):
        total = None
        if -1 <= y <= 4:
            total = place.keep(image_ref[x + 1, y + 1], x, y, BRICK)
        for part, key in ((below, (x, y)), (above, mirror(x, y))):
            if key in SIDE_Y_IMAGE:
                more = place.keep(part(3 * SIDE_Y_IMAGE.index(key), 4), x, 0, BRICK)
                total = more if total is None else total + more
        return total

    value = memo(value)
    cells = [(x, y) for x in range(-1, 3) for y in (0, 1)]
    part = contribution(value, reader(weight0_ref, 2), RIMMED, cells, shifts)
    for x in range(-1, 3):
        put_rows(slot_ref, 3 * (x + 1), part[x, 0] * shifts.even + part[x, 1] * shifts.odd)
    slot_ref[12] = dots_ref[...]
    clear_tail(to_even_ref, to_odd_ref)
    for k, (x, y) in enumerate(SIDE_X_IMAGE):
        put_sides(to_even_ref, to_odd_ref, 3 * k, 3, value(x + 4, y), value(-1 - x, y), place.even_x)
    for x in range(-1, BRICK + 1):
        for y in range(-2, 6):
            long_ref[x + 1, y + 2] = value(x, y)


def middle_kernel(counts, long_ref, even_ref, odd_ref, w_ref):
    place = Place(*counts)
    left, right = side_parts(even_ref, odd_ref, place.even_x, place.in_x[-1], place.in_x[1])
    live = live_rows()
    for x in range(-2, 6):
        for y in range(-2, 6):
            total = jnp.zeros((4, LANES), F32)
            if -1 <= x <= 4:
                total = total + long_ref[x + 1, y + 2]
            for part, key in ((left, (x, y)), (right, mirror_x(x, y))):
                if key in SIDE_X_IMAGE:
                    total = total + part(3 * SIDE_X_IMAGE.index(key), 4)
            w_ref[x + 2, y + 2] = total * live


def sums_of(ref, count, first, stride):
    return jnp.sum(ref[pl.ds(first, count, stride=stride), :], axis=0, keepdims=True)


def second_kernel(counts, change_ref, r1_ref, mass1_ref, r_ref, w_ref, mass0_ref, weight0_ref,
                  hot_ref, x_ref, effective_ref, grad_ref, z_ref, image_ref, x_even_ref, x_odd_ref, y_even_ref, y_odd_ref,
                  slots_ref, *scratch):
    particles = (hot_ref, x_ref, effective_ref, grad_ref)
    place, shifts = Place(*counts), Shifts()
    bricks = counts[0] * counts[1]
    levels = Levels(*counts, shifts)
    sums = sums_of(change_ref, bricks, 12, SECOND_ROWS)
    step = sums[:, 0:1] / sums[:, 1:2]
    r = memo(lambda x, y: r_ref[x + 2, y + 2] - step * w_ref[x + 2, y + 2])
    rows = lambda q: levels.load(change_ref, q, SECOND_ROWS)
    r1 = []
    for m in range(3):
        low = rows(3 + m) + levels.below_x(rows(9 + m))
        high = rows(6 + m) + levels.above_x(rows(m))
        r1.append([r1_ref[m, 0] - step * low, r1_ref[m, 1] - step * high])
    fields = (reader(mass0_ref, 2), reader(weight0_ref, 2))
    mass1 = [mass1_ref[0], mass1_ref[1]]
    z, image = cycle_and_apply(place, shifts, levels, r, r1, mass1, fields, particles, scratch)
    for x, y in INNER:
        z_ref[x, y] = z(x, y)
        image_ref[x, y] = image[x, y]
    rz = total_of((r(x, y), z(x, y)) for x, y in INNER)
    zaz = total_of((image[x, y], z(x, y)) for x, y in RIMMED)
    zw = total_of((w_ref[x + 2, y + 2], z(x, y)) for x, y in INNER)
    row = dots_row(rz, zaz, zw)
    none = jnp.zeros((3, 1, LANES), F32)

    def fill(k, carry):
        slots_ref[k, 0:3] = none
        slots_ref[k, 3] = row
        return carry

    lax.fori_loop(0, bricks, fill, 0)
    for dx in (-1, 1):
        for dy in (-1, 1):
            there_x = (place.gx + dx >= 0) & (place.gx + dx < counts[0])
            there_y = (place.gy + dy >= 0) & (place.gy + dy < counts[1])
            column = image[BRICK if dx > 0 else -1, BRICK if dy > 0 else -1]

            @pl.when(there_x & there_y)
            def _(column=column, dx=dx, dy=dy):
                other = (place.gx + dx) * counts[1] + place.gy + dy
                for m in range(3):
                    slots_ref[other, m] = column[m : m + 1]

    clear_tail(x_even_ref, x_odd_ref, y_even_ref, y_odd_ref)
    for k in range(BRICK):
        put_sides(x_even_ref, x_odd_ref, 3 * k, 3, image[BRICK, k], image[-1, k], place.even_x)
        put_sides(y_even_ref, y_odd_ref, 3 * k, 3, image[k, BRICK], image[k, -1], place.even_y)


def last_kernel(counts, slots_ref, x_even_ref, x_odd_ref, y_even_ref, y_odd_ref, change_ref, z1_ref, z2_ref, r_ref, w_ref, image_ref, solution_ref, residual_ref):
    place = Place(*counts)
    bricks = counts[0] * counts[1]
    sums1 = sums_of(change_ref, bricks, 12, SECOND_ROWS)
    sums2 = jnp.sum(slots_ref[:, 3], axis=0)
    rz1, zaz1 = sums1[:, 0:1], sums1[:, 1:2]
    rz2, zaz2, zw = sums2[:, 0:1], sums2[:, 1:2], sums2[:, 2:3]
    step1 = rz1 / zaz1
    ratio = rz2 / rz1
    step2 = rz2 / (zaz2 + 2.0 * ratio * zw + ratio * ratio * zaz1)
    image = {(x, y): image_ref[x, y] for x, y in INNER}
    left, right = side_parts(x_even_ref, x_odd_ref, place.even_x, place.in_x[-1], place.in_x[1])
    below, above = side_parts(y_even_ref, y_odd_ref, place.even_y, place.in_y[-1], place.in_y[1])
    end = BRICK - 1
    for k in range(BRICK):
        for at, part in (((0, k), left), ((end, k), right), ((k, 0), below), ((k, end), above)):
            image[at] = image[at] + part(3 * k, 4)
    for dx in (-1, 1):
        for dy in (-1, 1):
            other_x = jnp.clip(place.gx + dx, 0, counts[0] - 1)
            other_y = jnp.clip(place.gy + dy, 0, counts[1] - 1)
            other = other_x * counts[1] + other_y
            column = jnp.concatenate([slots_ref[other, m] for m in range(3)] + [jnp.zeros((1, LANES), F32)], axis=0)
            at = (end if dx > 0 else 0, end if dy > 0 else 0)
            image[at] = image[at] + place.keep(column, dx, dy, 1)
    for x, y in INNER:
        w = w_ref[x + 2, y + 2]
        z1 = z1_ref[x, y]
        solution = step1 * z1 + step2 * (z2_ref[x, y] + ratio * z1)
        residual = r_ref[x + 2, y + 2] - step1 * w - step2 * (image[x, y] + ratio * w)
        for m in range(3):
            solution_ref[m, x, y : y + 1, :] = solution[m : m + 1]
            residual_ref[m, x, y : y + 1, :] = residual[m : m + 1]


def call(kernel, counts, shapes, *args, scratch=()):
    shapes = [s if isinstance(s[0], tuple) else (s, F32) for s in shapes]
    return pl.pallas_call(
        functools.partial(kernel, counts),
        out_shape=[jax.ShapeDtypeStruct(*s) for s in shapes],
        scratch_shapes=scratch,
        compiler_params=pltpu.CompilerParams(vmem_limit_bytes=VMEM_BYTES),
    )(*args)


def per_device(counts, right_side, node_mass, gradients, stiffness, valid, node_base):
    bricks = counts[0] * counts[1]
    blocks = gradients.shape[2]
    grid = (counts[1], counts[0], LANES)
    tiles = 9 * (BRICK + 2) * 8
    depth = BRICK * LANES
    width = blocks * LANES
    scratch = (
        *[pltpu.VMEM((8 * (bricks + 2 * (counts[0] + 1)), LANES), F32)] * 2,
        pltpu.VMEM((tiles, depth), jnp.bfloat16),
        pltpu.VMEM((tiles, width), jnp.bfloat16),
        pltpu.VMEM((tiles, width), F32),
        pltpu.VMEM((tiles, depth), F32),
    )
    rows = lambda columns: (-(-(3 * len(columns) + 1) // 8) * 8, LANES)
    block = lambda *dims: (*dims, 4, LANES)

    def share(slot):
        sent = jnp.broadcast_to(slot[None], (bricks, *slot.shape))
        return lax.all_to_all(sent, AXES, 0, 0).reshape(bricks * slot.shape[0], LANES)

    fields = jnp.concatenate([right_side, node_mass[None]], axis=0)
    own, to_even, to_odd, slot = call(
        pack_kernel, counts, [block(4, 4), block(8), block(8), (FIRST_ROWS, 1, LANES)], fields
    )
    level = share(slot)
    even, odd = exchange(to_even, to_odd, "gx", counts)
    side = block(len(SIDE))
    wide, to_even, to_odd = call(widen_kernel, counts, [block(8, 4), side, side], own, even, odd)
    even, odd = exchange(to_even, to_odd, "gy", counts)
    row = (blocks, LANES)
    prepared = call(
        particle_kernel, counts, [((depth, width), jnp.bfloat16), (row, jnp.int32), row],
        node_base[0, 0], stiffness[0, 0], valid[0, 0],
    )
    particles = (*prepared, gradients[0, 0].transpose(1, 2, 0, 3))
    r, *fields = call(start_kernel, counts, [block(8, 8)] * 3, wide, even, odd)

    side = rows(SIDE_Y_IMAGE)
    z1, image, to_even, to_odd, dots, r1, mass1 = call(
        first_kernel, counts,
        [block(4, 4), block(6, 6), side, side, (1, LANES), (3, 2, *grid), (2, *grid)],
        level, r, *fields, *particles, scratch=scratch,
    )
    even, odd = exchange(to_even, to_odd, "gy", counts)
    side = rows(SIDE_X_IMAGE)
    long, to_even, to_odd, slot = call(
        along_y_kernel, counts, [block(6, 8), side, side, (SECOND_ROWS, 1, LANES)], image, even, odd, fields[1], dots
    )
    change = share(slot)
    even, odd = exchange(to_even, to_odd, "gx", counts)
    (w,) = call(middle_kernel, counts, [block(8, 8)], long, even, odd)
    side = (2 * 8, LANES)
    z2, image, x_even, x_odd, y_even, y_odd, slots = call(
        second_kernel, counts, [block(4, 4), block(4, 4), side, side, side, side, (bricks, 4, 1, LANES)],
        change, r1, mass1, r, w, *fields, *particles, scratch=scratch,
    )
    sides = (*exchange(x_even, x_odd, "gx", counts), *exchange(y_even, y_odd, "gy", counts))
    slots = lax.all_to_all(slots, AXES, 0, 0)
    return tuple(
        call(last_kernel, counts, [right_side.shape, right_side.shape], slots, *sides, change, z1, z2, r, w, image)
    )


def solution(mesh):
    counts = (mesh.shape["gx"], mesh.shape["gy"])
    return jax.shard_map(
        functools.partial(per_device, counts),
        mesh=mesh,
        in_specs=(
            P(None, "gx", "gy", None),
            P("gx", "gy", None),
            P("gx", "gy", None, None, None, None),
            P("gx", "gy", None, None),
            P("gx", "gy", None, None),
            P("gx", "gy", None, None),
        ),
        out_specs=(P(None, "gx", "gy", None), P(None, "gx", "gy", None)),
        check_vma=False,
    )
```

```python
import functools

import jax
import jax.numpy as jnp
from jax import lax
from jax.experimental import pallas as pl
from jax.experimental.pallas import tpu as pltpu
from jax.sharding import PartitionSpec as P

POISSON = 0.3
DAMPING = 0.7
KEPT = 1.0 - DAMPING
SWEEPS = 4
LANES = 128
BRICK = 4
AXES = ("gx", "gy")
VMEM_BYTES = 24 * 1024 * 1024
F32 = jnp.float32


def pairings(axis, counts):
    count_x, count_y = counts
    even, odd = [], []
    for x in range(count_x):
        for y in range(count_y):
            k, count = (x, count_x) if axis == "gx" else (y, count_y)
            move = lambda to: (to, y) if axis == "gx" else (x, to)
            even.append(((x, y), move(k ^ 1)))
            if 0 < k < count - 1:
                odd.append(((x, y), move(k + 1 if k % 2 else k - 1)))
            else:
                odd.append(((x, y), (x, y ^ 1) if axis == "gx" else (x ^ 1, y)))
    flat = lambda pairs: [(a * count_y + b, c * count_y + d) for (a, b), (c, d) in pairs]
    return flat(even), flat(odd)


def exchange(first, second, axis, counts):
    even, odd = pairings(axis, counts)
    return lax.ppermute(first, AXES, even), lax.ppermute(second, AXES, odd)


SIDE = [(x, -1) for x in range(-2, 6)] + [(x, -2) for x in range(-1, 5)]
SIDE_X = [(x, y) for x in (-2, -1) for y in range(BRICK)]
SIDE_Y_IMAGE = [(x, y) for y in (-2, -1, 0) for x in range(-1, 5)]
SIDE_X_IMAGE = [(0, y) for y in range(-2, 6)] + [(y, x) for x, y in SIDE]


def mirror(x, y):
    return x, BRICK - 1 - y


def mirror_x(x, y):
    return BRICK - 1 - x, y


def lane_index():
    return lax.broadcasted_iota(jnp.int32, (1, LANES), 1)


def as_f32(cond):
    return jnp.where(cond, 1.0, 0.0).astype(F32)


def turn(x, shift):
    return pltpu.roll(x, shift % LANES, x.ndim - 1)


class Place:
    def __init__(self, count_x, count_y):
        self.gx = lax.axis_index("gx")
        self.gy = lax.axis_index("gy")
        self.count_x, self.count_y = count_x, count_y
        flag = lambda cond: jnp.where(cond, 1.0, 0.0).astype(F32)
        self.even_x = flag(self.gx % 2 == 0)
        self.even_y = flag(self.gy % 2 == 0)
        self.in_x = {-1: flag(self.gx > 0), 0: None, 1: flag(self.gx < count_x - 1)}
        self.in_y = {-1: flag(self.gy > 0), 0: None, 1: flag(self.gy < count_y - 1)}

    def keep(self, value, x, y, size):
        side_x = -1 if x < 0 else 1 if x >= size else 0
        side_y = -1 if y < 0 else 1 if y >= size else 0
        if side_x:
            value = value * self.in_x[side_x]
        if side_y:
            value = value * self.in_y[side_y]
        return value


class Shifts:
    def __init__(self):
        lane = lane_index()
        self.low = {d: as_f32(lane >= d) for d in (1, 2, 4)}
        self.high = {d: as_f32(lane < LANES - d) for d in (1, 2, 4)}
        self.even = as_f32(lane % 2 == 0)
        self.odd = 1.0 - self.even

    def beside(self, x, d):
        return turn(x, d) * self.low[d] + turn(x, -d) * self.high[d]

    def pair_sum(self, x):
        t = (x + turn(x, -1)) * self.even
        return t + turn(t, 1)


def memo(fn):
    kept = {}

    def wrapped(x, y):
        if (x, y) not in kept:
            kept[(x, y)] = fn(x, y)
        return kept[(x, y)]

    return wrapped


def beside_all(e, x, y, shifts, step):
    return e(x + 1, y) + e(x - 1, y) + e(x, y + 1) + e(x, y - 1) + shifts.beside(e(x, y), step)


def contribution(w, weight0, columns, cells, shifts):
    inside = set(columns)
    e0 = memo(lambda x, y: weight0(x, y) * w(x, y) if (x, y) in inside else None)

    def rest(x, y):
        beside = [v for v in (e0(x + 1, y), e0(x - 1, y), e0(x, y + 1), e0(x, y - 1)) if v is not None]
        total = sum(beside) if beside else None
        c = e0(x, y)
        if c is None:
            return total
        near = shifts.beside(c, 1) if total is None else total + shifts.beside(c, 1)
        return KEPT * w(x, y) + near

    out = {}
    for x, y in cells:
        parts = [rest(2 * x + i, 2 * y + j) for i in range(2) for j in range(2)]
        out[x, y] = shifts.pair_sum(sum(v for v in parts if v is not None))
    return out


class Levels:
    def __init__(self, count_x, count_y, shifts):
        self.count_x, self.count_y, self.shifts = count_x, count_y, shifts
        row = lax.broadcasted_iota(jnp.int32, (1, count_x, LANES), 1)
        lane = lax.broadcasted_iota(jnp.int32, (1, 1, LANES), 2)
        self.x_low, self.x_high = as_f32(row > 0), as_f32(row < count_x - 1)
        self.even = as_f32(lane % 2 == 0)
        self.odd = 1.0 - self.even
        self.first = as_f32(lane % 4 == 0)
        self.low, self.high = as_f32(lane >= 4), as_f32(lane < LANES - 4)
        self.z_low, self.z_high = self.low * as_f32(lane % 4 >= 2), self.high * as_f32(lane % 4 < 2)
        self.edge = jnp.zeros((1, count_x, LANES), F32)

    def load(self, ref, first, stride):
        pick = lambda y: ref[pl.ds(first + stride * y, self.count_x, stride=stride * self.count_y), :]
        return jnp.stack([pick(y) for y in range(self.count_y)])

    def below_x(self, v):
        return pltpu.roll(v, 1, 1) * self.x_low

    def above_x(self, v):
        return pltpu.roll(v, self.count_x - 1, 1) * self.x_high

    def below_y(self, v):
        return jnp.concatenate([self.edge, v[:-1]], axis=0)

    def above_y(self, v):
        return jnp.concatenate([v[1:], self.edge], axis=0)

    def beside(self, v, d):
        return turn(v, d) * self.low + turn(v, -d) * self.high

    def gather_y(self, first, second):
        return (first + self.below_y(second)) * self.even + (second + self.above_y(first)) * self.odd

    def quad_sum(self, v):
        v = (v + turn(v, -1) + turn(v, -2) + turn(v, -3)) * self.first
        return v + turn(v, 1) + turn(v, 2) + turn(v, 3)

    def restrict(self, r, e):
        t = e[0] + e[1]
        near = 3.0 * t + self.below_x(e[1]) + self.above_x(e[0]) + self.below_y(t) * self.odd
        near = near + self.above_y(t) * self.even + turn(t, 4) * self.z_low + turn(t, -4) * self.z_high
        return self.quad_sum(KEPT * (r[0] + r[1]) + 2.0 * near)

    def solve_2(self, r2, weight):
        start = weight * r2
        weight = 4.0 * weight
        e = start
        for _ in range(SWEEPS - 1):
            near = self.below_x(e) + self.above_x(e) + self.below_y(e) + self.above_y(e) + self.beside(e, 4)
            e = (KEPT * e + start) + weight * near
        return e


def pack_y(cells, x, shifts):
    return (
        cells[x, 0] * shifts.even + cells[x, -1] * shifts.odd,
        cells[x, 1] * shifts.odd + cells[x, 2] * shifts.even,
    )


def put_rows(slot_ref, row, column):
    for m in range(3):
        slot_ref[row + m] = column[m : m + 1]


def fine_level(r, f1, weight0, place, shifts):
    first = memo(lambda x, y: weight0(x, y) * r(x, y))
    e0 = memo(lambda x, y: first(x, y) + f1(x // 2, y // 2))

    def at(x, y):
        value = KEPT * e0(x, y) + first(x, y) + weight0(x, y) * beside_all(e0, x, y, shifts, 1)
        return place.keep(value, x, y, BRICK)

    return memo(at)


def stiffness_apply(z, hot, x_ref, effective_ref, grad_ref, nodes, forces_a, forces_b, picked_a, picked_b, spread_sums, shifts):
    blocks = grad_ref.shape[2]
    turns = [(b, c) for b in range(3) for c in range(3)]
    span = BRICK + 2

    def halves(x):
        high = x.astype(jnp.bfloat16).astype(F32)
        return jnp.concatenate([high, x - high], axis=0)

    split = {}
    for x in range(span):
        for y in range(span):
            whole = halves(z(x - 1, y - 1))
            split[x, y, 1] = whole
            split[x, y, 0] = turn(whole, 1) * shifts.low[1]
            split[x, y, 2] = turn(whole, -1) * shifts.high[1]
    for u, (b, c) in enumerate(turns):
        for j in range(BRICK):
            for x in range(0, span, 2):
                pair = jnp.concatenate([split[x, j + b, c], split[x + 1, j + b, c]], axis=0).astype(jnp.bfloat16)
                row = (u * span + x) * 8
                nodes[row : row + 16, j * LANES : (j + 1) * LANES] = pair

    node_x = x_ref[...]
    half = blocks // 2
    lanes_a, lanes_b = slice(0, half * LANES), slice(half * LANES, blocks * LANES)
    picked_a[...] = jnp.dot(nodes[...], hot[:, lanes_a], preferred_element_type=F32)
    picked_b[...] = jnp.dot(nodes[...], hot[:, lanes_b], preferred_element_type=F32)

    first = POISSON / ((1.0 + POISSON) * (1.0 - 2.0 * POISSON))
    shear_of = 0.5 / (1.0 + POISSON)
    row8 = lax.broadcasted_iota(jnp.int32, (8, LANES), 0)
    row_is = [as_f32(row8 % 4 == m) for m in range(3)]
    is_high = row8 < 4
    zero = jnp.zeros((8, LANES), F32)
    wide = lambda row: jnp.broadcast_to(row, (8, LANES))
    for s in range(blocks):
        lanes = slice(s % half * LANES, (s % half + 1) * LANES)
        picked, forces = (picked_a, forces_a) if s < half else (picked_b, forces_b)
        grad = lambda l, a, b, c: wide(grad_ref[l, 9 * a + 3 * b + c, s : s + 1, :])
        at_x = [wide(node_x[s : s + 1]) == i for i in range(BRICK)]
        h = [None] * 3
        for u, (b, c) in enumerate(turns):
            tiles = [picked[(u * span + x) * 8 : (u * span + x) * 8 + 8, lanes] for x in range(span)]
            for a in range(3):
                value = tiles[3 + a]
                for i in (2, 1, 0):
                    value = jnp.where(at_x[i], tiles[i + a], value)
                for l in range(3):
                    term = value * grad(l, a, b, c)
                    h[l] = term if h[l] is None else h[l] + term
        h = [x[0:4] + x[4:8] for x in h]
        h = [[h[l][m : m + 1] for l in range(3)] for m in range(3)]
        effective = effective_ref[s : s + 1]
        shear = effective * shear_of
        bulk = effective * first * (h[0][0] + h[1][1] + h[2][2])
        stress = []
        for l in range(3):
            column = 0.0
            for m in range(3):
                entry = shear * (h[m][l] + h[l][m])
                if l == m:
                    entry = entry + bulk
                column = column + wide(entry) * row_is[m]
            stress.append(column)
        for u, (b, c) in enumerate(turns):
            parts = []
            for a in range(3):
                f = stress[0] * grad(0, a, b, c) + stress[1] * grad(1, a, b, c) + stress[2] * grad(2, a, b, c)
                high = f.astype(jnp.bfloat16).astype(F32)
                parts.append(jnp.where(is_high, high, f - high))
            tiles = []
            for x in range(span):
                tile = zero
                for a in range(3):
                    if 0 <= x - a < BRICK:
                        tile = jnp.where(at_x[x - a], parts[a], tile)
                tiles.append(tile)
            for x in range(0, span, 2):
                row = (u * span + x) * 8
                pair = jnp.concatenate([tiles[x], tiles[x + 1]], axis=0).astype(jnp.bfloat16)
                forces[row : row + 16, lanes] = pair
        if s == half - 1:
            spread_sums[...] = lax.dot_general(
                forces_a[...], hot[:, lanes_a], (((1,), (1,)), ((), ())), preferred_element_type=F32
            )
    spread_sums[...] += lax.dot_general(
        forces_b[...], hot[:, lanes_b], (((1,), (1,)), ((), ())), preferred_element_type=F32
    )
    out = {}
    for x in range(span):
        for y in range(span):
            sums = [0.0, 0.0, 0.0]
            for u, (b, c) in enumerate(turns):
                j = y - b
                if 0 <= j < BRICK:
                    row = (u * span + x) * 8
                    sums[c] = sums[c] + spread_sums[row : row + 8, j * LANES : (j + 1) * LANES]
            total = sums[1] + turn(sums[0], -1) * shifts.high[1] + turn(sums[2], 1) * shifts.low[1]
            out[x - 1, y - 1] = total[0:4] + total[4:8]
    return out


def particle_kernel(counts, base_ref, stiff_ref, valid_ref, hot_ref, x_ref, effective_ref):
    span = BRICK + 2
    base = base_ref[...]
    plane = base // (LANES + 2)
    depth = base - plane * (LANES + 2)
    node_x = plane // span
    node_y = plane - node_x * span
    x_ref[...] = node_x
    effective_ref[...] = stiff_ref[...] * valid_ref[...].astype(F32)
    sub = lax.broadcasted_iota(jnp.int32, (LANES, LANES), 0)
    for s in range(base_ref.shape[0]):
        for j in range(BRICK):
            wanted = jnp.where(node_y[s : s + 1] == j, depth[s : s + 1], -1)
            hot_ref[j * LANES : (j + 1) * LANES, s * LANES : (s + 1) * LANES] = as_f32(sub == wanted).astype(jnp.bfloat16)


def side_parts(even_ref, odd_ref, is_even, inside_low, inside_high):
    odd = 1.0 - is_even
    below_odd, below_even = inside_low * is_even, inside_low * odd
    above_odd, above_even = inside_high * odd, inside_high * is_even

    def below(row, size):
        return odd_ref[row : row + size, :] * below_odd + even_ref[row : row + size, :] * below_even

    def above(row, size):
        return odd_ref[row : row + size, :] * above_odd + even_ref[row : row + size, :] * above_even

    return below, above


def put_sides(to_even_ref, to_odd_ref, row, size, up, down, is_even):
    odd = 1.0 - is_even
    to_even_ref[row : row + size, :] = (up * is_even + down * odd)[0:size]
    to_odd_ref[row : row + size, :] = (down * is_even + up * odd)[0:size]


def clear_tail(*refs):
    for ref in refs:
        ref[ref.shape[0] - 8 :, :] = jnp.zeros((8, LANES), F32)


def weight_of(mass):
    return DAMPING / (mass + 6.0)


def spread_mass(column):
    return jnp.broadcast_to(column[3:4], (4, LANES))


def live_rows():
    return as_f32(lax.broadcasted_iota(jnp.int32, (4, LANES), 0) < 3)


FIRST_ROWS = 20
SECOND_ROWS = 13


def pack_kernel(counts, fields_ref, own_ref, even_ref, odd_ref, slot_ref):
    place, shifts = Place(*counts), Shifts()
    own = {}
    for x in range(BRICK):
        for y in range(BRICK):
            own[x, y] = jnp.concatenate([fields_ref[m, x, y : y + 1, :] for m in range(4)], axis=0)
            own_ref[x, y] = own[x, y]
    odd_x = 1.0 - place.even_x
    for k, (x, y) in enumerate(SIDE_X):
        up, down = own[x + 4, y], own[-1 - x, y]
        even_ref[k] = up * place.even_x + down * odd_x
        odd_ref[k] = down * place.even_x + up * odd_x
    live = live_rows()
    mass0 = memo(lambda x, y: spread_mass(own[x, y]))
    weight0 = memo(lambda x, y: weight_of(mass0(x, y)))
    r = memo(lambda x, y: own[x, y] * live)
    cells = [(x, y) for x in (0, 1) for y in range(-1, 3)] + [(x, y) for x in (-1, 2) for y in (0, 1)]
    part = contribution(r, weight0, INNER, cells, shifts)
    for x in (0, 1):
        for k, column in enumerate(pack_y(part, x, shifts)):
            put_rows(slot_ref, 6 * x + 3 * k, column)
    for k, x in enumerate((-1, 2)):
        put_rows(slot_ref, 12 + 3 * k, part[x, 0] * shifts.even + part[x, 1] * shifts.odd)
    for x in (0, 1):
        mass1 = [
            shifts.pair_sum(sum(own[2 * x + i, 2 * y + j][3:4] for i in range(2) for j in range(2))) for y in (0, 1)
        ]
        slot_ref[18 + x] = mass1[0] * shifts.even + mass1[1] * shifts.odd


def widen_kernel(counts, own_ref, even_ref, odd_ref, wide_ref, to_even_ref, to_odd_ref):
    place = Place(*counts)
    odd_x = 1.0 - place.even_x
    left = (place.in_x[-1] * place.even_x, place.in_x[-1] * odd_x)
    right = (place.in_x[1] * odd_x, place.in_x[1] * place.even_x)

    def value(x, y):
        if 0 <= x < BRICK:
            return own_ref[x, y]
        odd, even = left if x < 0 else right
        k = SIDE_X.index((x, y) if x < 0 else mirror_x(x, y))
        return odd_ref[k] * odd + even_ref[k] * even

    value = memo(value)
    for x in range(-2, 6):
        for y in range(BRICK):
            wide_ref[x + 2, y] = value(x, y)
    odd_y = 1.0 - place.even_y
    for k, (x, y) in enumerate(SIDE):
        up, down = value(x, y + 4), value(x, -1 - y)
        to_even_ref[k] = up * place.even_y + down * odd_y
        to_odd_ref[k] = down * place.even_y + up * odd_y


def start_kernel(counts, wide_ref, even_ref, odd_ref, r_ref, mass0_ref, weight0_ref):
    place = Place(*counts)
    live = live_rows()
    odd_y = 1.0 - place.even_y
    below = (place.in_y[-1] * place.even_y, place.in_y[-1] * odd_y)
    above = (place.in_y[1] * odd_y, place.in_y[1] * place.even_y)
    for x in range(-2, 6):
        for y in range(-2, 6):
            if 0 <= y < BRICK:
                value = wide_ref[x + 2, y]
            else:
                key = (x, y) if y < 0 else mirror(x, y)
                odd, even = below if y < 0 else above
                if key in SIDE:
                    k = SIDE.index(key)
                    value = odd_ref[k] * odd + even_ref[k] * even
                else:
                    value = jnp.zeros((4, LANES), F32)
            r_ref[x + 2, y + 2] = value * live
            mass = spread_mass(value)
            mass0_ref[x + 2, y + 2] = mass
            weight0_ref[x + 2, y + 2] = weight_of(mass)


def reader(ref, offset):
    return memo(lambda x, y: ref[x + offset, y + offset])


def cycle(place, shifts, levels, r, r1, mass1, weight0, middle, coarse):
    width = place.count_x
    margin = 8 * (width + 1)

    def put(ref, row, value):
        for y in range(place.count_y):
            ref[pl.ds(margin + 8 * width * y + row, width, stride=8), :] = value[y]

    def get(ref, x, y):
        brick = (place.gy + y) * width + place.gx + x
        return ref[pl.ds(pl.multiple_of(margin + brick * 8, 8), 8), :]

    weight1 = [DAMPING / (m + 12.0) for m in mass1]
    weight2 = DAMPING / (levels.quad_sum(mass1[0] + mass1[1]) + 24.0)
    middle[...] = jnp.zeros_like(middle)
    coarse[...] = jnp.zeros_like(coarse)
    for x in range(2):
        put(middle, 4 * x + 3, weight1[x])
    for m in range(3):
        e = [weight1[x] * r1[m][x] for x in range(2)]
        for x in range(2):
            put(middle, 4 * x + m, e[x])
        put(coarse, m, levels.solve_2(levels.restrict(r1[m], e), weight2))

    def brick_at(x, y):
        rows = get(middle, x, y)
        first, second = rows * shifts.even, rows * shifts.odd
        return first + turn(first, 1), second + turn(second, -1)

    brick_at = memo(brick_at)

    def first_at(x, y):
        both = brick_at(x // 2, y // 2)[y % 2]
        return place.keep(both[4 * (x % 2) : 4 * (x % 2) + 4], x, y, 2)

    first = memo(first_at)
    e2 = memo(lambda x, y: place.keep(get(coarse, x, y)[0:4], x, y, 1))
    e1 = memo(lambda x, y: first(x, y) + e2(x // 2, y // 2))
    live = live_rows()

    def f1_at(x, y):
        weight = 2.0 * spread_mass(first(x, y))
        value = KEPT * e1(x, y) + first(x, y) + weight * beside_all(e1, x, y, shifts, 2)
        return place.keep(value * live, x, y, 2)

    return fine_level(r, memo(f1_at), weight0, place, shifts)


def apply(z, mass0, particles, work, shifts):
    image = stiffness_apply(z, *particles, *work, shifts)
    for x, y in INNER:
        image[x, y] = image[x, y] + mass0(x, y) * z(x, y)
    return image


def total_of(pairs):
    acc = 0.0
    for a, b in pairs:
        acc = acc + a * b
    return jnp.sum(jnp.sum(acc, axis=0, keepdims=True), axis=1, keepdims=True)


def dots_row(*values):
    lane = lane_index()
    row = 0.0
    for k, v in enumerate(values):
        row = row + as_f32(lane == k) * v
    return row


INNER = [(x, y) for x in range(BRICK) for y in range(BRICK)]
RIMMED = [(x, y) for x in range(-1, BRICK + 1) for y in range(-1, BRICK + 1)]


def first_kernel(counts, level_ref, r_ref, mass0_ref, weight0_ref,
                 hot_ref, x_ref, effective_ref, grad_ref, z_ref, image_ref, even_ref, odd_ref, dots_ref, mass1_ref,
                 *scratch):
    particles = (hot_ref, x_ref, effective_ref, grad_ref)
    place, shifts = Place(*counts), Shifts()
    levels = Levels(*counts, shifts)
    rows = lambda q: levels.load(level_ref, q, FIRST_ROWS)
    r1 = []
    for m in range(3):
        pair = [levels.gather_y(rows(6 * x + m), rows(6 * x + 3 + m)) for x in range(2)]
        pair[1] = pair[1] + levels.above_x(rows(12 + m))
        pair[0] = pair[0] + levels.below_x(rows(15 + m))
        r1.append(pair)
    mass1 = [rows(18), rows(19)]
    for x in range(2):
        mass1_ref[x] = mass1[x]
    r = reader(r_ref, 2)
    middle, coarse, *work = scratch
    z = cycle(place, shifts, levels, r, r1, mass1, reader(weight0_ref, 2), middle, coarse)
    image = apply(z, reader(mass0_ref, 2), particles, work, shifts)
    for x, y in RIMMED:
        z_ref[x + 1, y + 1] = z(x, y)
    for x, y in RIMMED:
        image_ref[x + 1, y + 1] = image[x, y]
    clear_tail(even_ref, odd_ref)
    for k, (x, y) in enumerate(SIDE_Y_IMAGE):
        put_sides(even_ref, odd_ref, 3 * k, 3, image[x, y + 4], image[x, -1 - y], place.even_y)
    rz = total_of((r(x, y), z(x, y)) for x, y in INNER)
    zaz = total_of((image[x, y], z(x, y)) for x, y in RIMMED)
    dots_ref[...] = dots_row(rz, zaz)


def along_y_kernel(counts, image_ref, even_ref, odd_ref, weight0_ref, dots_ref,
                   long_ref, to_even_ref, to_odd_ref, slot_ref):
    place, shifts = Place(*counts), Shifts()
    below, above = side_parts(even_ref, odd_ref, place.even_y, place.in_y[-1], place.in_y[1])

    def value(x, y):
        total = None
        if -1 <= y <= 4:
            total = place.keep(image_ref[x + 1, y + 1], x, y, BRICK)
        for part, key in ((below, (x, y)), (above, mirror(x, y))):
            if key in SIDE_Y_IMAGE:
                more = place.keep(part(3 * SIDE_Y_IMAGE.index(key), 4), x, 0, BRICK)
                total = more if total is None else total + more
        return total

    value = memo(value)
    cells = [(x, y) for x in range(-1, 3) for y in (0, 1)]
    part = contribution(value, reader(weight0_ref, 2), RIMMED, cells, shifts)
    for x in range(-1, 3):
        put_rows(slot_ref, 3 * (x + 1), part[x, 0] * shifts.even + part[x, 1] * shifts.odd)
    slot_ref[12] = dots_ref[...]
    clear_tail(to_even_ref, to_odd_ref)
    for k, (x, y) in enumerate(SIDE_X_IMAGE):
        put_sides(to_even_ref, to_odd_ref, 3 * k, 3, value(x + 4, y), value(-1 - x, y), place.even_x)
    for x in range(-1, BRICK + 1):
        for y in range(-2, 6):
            long_ref[x + 1, y + 2] = value(x, y)


def middle_kernel(counts, long_ref, even_ref, odd_ref, w_ref):
    place = Place(*counts)
    left, right = side_parts(even_ref, odd_ref, place.even_x, place.in_x[-1], place.in_x[1])
    live = live_rows()
    for x in range(-2, 6):
        for y in range(-2, 6):
            total = jnp.zeros((4, LANES), F32)
            if -1 <= x <= 4:
                total = total + long_ref[x + 1, y + 2]
            for part, key in ((left, (x, y)), (right, mirror_x(x, y))):
                if key in SIDE_X_IMAGE:
                    total = total + part(3 * SIDE_X_IMAGE.index(key), 4)
            w_ref[x + 2, y + 2] = total * live


def sums_of(ref, count, first, stride):
    return jnp.sum(ref[pl.ds(first, count, stride=stride), :], axis=0, keepdims=True)


def second_kernel(counts, change_ref, z1_ref, mass1_ref, r_ref, w_ref, mass0_ref, weight0_ref,
                  hot_ref, x_ref, effective_ref, grad_ref, z_ref, image_ref, x_even_ref, x_odd_ref, y_even_ref, y_odd_ref,
                  slots_ref, *scratch):
    particles = (hot_ref, x_ref, effective_ref, grad_ref)
    place, shifts = Place(*counts), Shifts()
    bricks = counts[0] * counts[1]
    levels = Levels(*counts, shifts)
    sums = sums_of(change_ref, bricks, 12, SECOND_ROWS)
    step = sums[:, 0:1] / sums[:, 1:2]
    rows = lambda q: levels.load(change_ref, q, SECOND_ROWS)
    r1 = []
    for m in range(3):
        r1.append([rows(3 + m) + levels.below_x(rows(9 + m)), rows(6 + m) + levels.above_x(rows(m))])
    w = reader(w_ref, 2)
    middle, coarse, *work = scratch
    of_w = cycle(place, shifts, levels, w, r1, [mass1_ref[0], mass1_ref[1]], reader(weight0_ref, 2), middle, coarse)
    z = memo(lambda x, y: z1_ref[x + 1, y + 1] - step * of_w(x, y))
    image = apply(z, reader(mass0_ref, 2), particles, work, shifts)
    r = memo(lambda x, y: r_ref[x + 2, y + 2] - step * w(x, y))
    for x, y in INNER:
        z_ref[x, y] = z(x, y)
        image_ref[x, y] = image[x, y]
    rz = total_of((r(x, y), z(x, y)) for x, y in INNER)
    zaz = total_of((image[x, y], z(x, y)) for x, y in RIMMED)
    zw = total_of((w_ref[x + 2, y + 2], z(x, y)) for x, y in INNER)
    row = dots_row(rz, zaz, zw)
    none = jnp.zeros((3, 1, LANES), F32)

    def fill(k, carry):
        slots_ref[k, 0:3] = none
        slots_ref[k, 3] = row
        return carry

    lax.fori_loop(0, bricks, fill, 0)
    for dx in (-1, 1):
        for dy in (-1, 1):
            there_x = (place.gx + dx >= 0) & (place.gx + dx < counts[0])
            there_y = (place.gy + dy >= 0) & (place.gy + dy < counts[1])
            column = image[BRICK if dx > 0 else -1, BRICK if dy > 0 else -1]

            @pl.when(there_x & there_y)
            def _(column=column, dx=dx, dy=dy):
                other = (place.gx + dx) * counts[1] + place.gy + dy
                for m in range(3):
                    slots_ref[other, m] = column[m : m + 1]

    clear_tail(x_even_ref, x_odd_ref, y_even_ref, y_odd_ref)
    for k in range(BRICK):
        put_sides(x_even_ref, x_odd_ref, 3 * k, 3, image[BRICK, k], image[-1, k], place.even_x)
        put_sides(y_even_ref, y_odd_ref, 3 * k, 3, image[k, BRICK], image[k, -1], place.even_y)


def last_kernel(counts, slots_ref, x_even_ref, x_odd_ref, y_even_ref, y_odd_ref, change_ref, z1_ref, z2_ref, r_ref, w_ref, image_ref, solution_ref, residual_ref):
    place = Place(*counts)
    bricks = counts[0] * counts[1]
    sums1 = sums_of(change_ref, bricks, 12, SECOND_ROWS)
    sums2 = jnp.sum(slots_ref[:, 3], axis=0)
    rz1, zaz1 = sums1[:, 0:1], sums1[:, 1:2]
    rz2, zaz2, zw = sums2[:, 0:1], sums2[:, 1:2], sums2[:, 2:3]
    step1 = rz1 / zaz1
    ratio = rz2 / rz1
    step2 = rz2 / (zaz2 + 2.0 * ratio * zw + ratio * ratio * zaz1)
    image = {(x, y): image_ref[x, y] for x, y in INNER}
    left, right = side_parts(x_even_ref, x_odd_ref, place.even_x, place.in_x[-1], place.in_x[1])
    below, above = side_parts(y_even_ref, y_odd_ref, place.even_y, place.in_y[-1], place.in_y[1])
    end = BRICK - 1
    for k in range(BRICK):
        for at, part in (((0, k), left), ((end, k), right), ((k, 0), below), ((k, end), above)):
            image[at] = image[at] + part(3 * k, 4)
    for dx in (-1, 1):
        for dy in (-1, 1):
            other_x = jnp.clip(place.gx + dx, 0, counts[0] - 1)
            other_y = jnp.clip(place.gy + dy, 0, counts[1] - 1)
            other = other_x * counts[1] + other_y
            column = jnp.concatenate([slots_ref[other, m] for m in range(3)] + [jnp.zeros((1, LANES), F32)], axis=0)
            at = (end if dx > 0 else 0, end if dy > 0 else 0)
            image[at] = image[at] + place.keep(column, dx, dy, 1)
    for x, y in INNER:
        w = w_ref[x + 2, y + 2]
        z1 = z1_ref[x + 1, y + 1]
        solution = step1 * z1 + step2 * (z2_ref[x, y] + ratio * z1)
        residual = r_ref[x + 2, y + 2] - step1 * w - step2 * (image[x, y] + ratio * w)
        for m in range(3):
            solution_ref[m, x, y : y + 1, :] = solution[m : m + 1]
            residual_ref[m, x, y : y + 1, :] = residual[m : m + 1]


def call(kernel, counts, shapes, *args, scratch=()):
    shapes = [s if isinstance(s[0], tuple) else (s, F32) for s in shapes]
    return pl.pallas_call(
        functools.partial(kernel, counts),
        out_shape=[jax.ShapeDtypeStruct(*s) for s in shapes],
        scratch_shapes=scratch,
        compiler_params=pltpu.CompilerParams(vmem_limit_bytes=VMEM_BYTES),
    )(*args)


def per_device(counts, right_side, node_mass, gradients, stiffness, valid, node_base):
    bricks = counts[0] * counts[1]
    blocks = gradients.shape[2]
    grid = (counts[1], counts[0], LANES)
    tiles = 9 * (BRICK + 2) * 8
    depth = BRICK * LANES
    width = blocks * LANES
    scratch = (
        *[pltpu.VMEM((8 * (bricks + 2 * (counts[0] + 1)), LANES), F32)] * 2,
        pltpu.VMEM((tiles, depth), jnp.bfloat16),
        *[pltpu.VMEM((tiles, width // 2), jnp.bfloat16)] * 2,
        *[pltpu.VMEM((tiles, width // 2), F32)] * 2,
        pltpu.VMEM((tiles, depth), F32),
    )
    rows = lambda columns: (-(-(3 * len(columns) + 1) // 8) * 8, LANES)
    block = lambda *dims: (*dims, 4, LANES)

    def share(slot):
        sent = jnp.broadcast_to(slot[None], (bricks, *slot.shape))
        return lax.all_to_all(sent, AXES, 0, 0).reshape(bricks * slot.shape[0], LANES)

    fields = jnp.concatenate([right_side, node_mass[None]], axis=0)
    own, to_even, to_odd, slot = call(
        pack_kernel, counts, [block(4, 4), block(8), block(8), (FIRST_ROWS, 1, LANES)], fields
    )
    level = share(slot)
    even, odd = exchange(to_even, to_odd, "gx", counts)
    side = block(len(SIDE))
    wide, to_even, to_odd = call(widen_kernel, counts, [block(8, 4), side, side], own, even, odd)
    even, odd = exchange(to_even, to_odd, "gy", counts)
    row = (blocks, LANES)
    prepared = call(
        particle_kernel, counts, [((depth, width), jnp.bfloat16), (row, jnp.int32), row],
        node_base[0, 0], stiffness[0, 0], valid[0, 0],
    )
    particles = (*prepared, gradients[0, 0].transpose(1, 2, 0, 3))
    r, *fields = call(start_kernel, counts, [block(8, 8)] * 3, wide, even, odd)

    side = rows(SIDE_Y_IMAGE)
    z1, image, to_even, to_odd, dots, mass1 = call(
        first_kernel, counts,
        [block(6, 6), block(6, 6), side, side, (1, LANES), (2, *grid)],
        level, r, *fields, *particles, scratch=scratch,
    )
    even, odd = exchange(to_even, to_odd, "gy", counts)
    side = rows(SIDE_X_IMAGE)
    long, to_even, to_odd, slot = call(
        along_y_kernel, counts, [block(6, 8), side, side, (SECOND_ROWS, 1, LANES)], image, even, odd, fields[1], dots
    )
    change = share(slot)
    even, odd = exchange(to_even, to_odd, "gx", counts)
    (w,) = call(middle_kernel, counts, [block(8, 8)], long, even, odd)
    side = (2 * 8, LANES)
    z2, image, x_even, x_odd, y_even, y_odd, slots = call(
        second_kernel, counts, [block(4, 4), block(4, 4), side, side, side, side, (bricks, 4, 1, LANES)],
        change, z1, mass1, r, w, *fields, *particles, scratch=scratch,
    )
    sides = (*exchange(x_even, x_odd, "gx", counts), *exchange(y_even, y_odd, "gy", counts))
    slots = lax.all_to_all(slots, AXES, 0, 0)
    return tuple(
        call(last_kernel, counts, [right_side.shape, right_side.shape], slots, *sides, change, z1, z2, r, w, image)
    )


def solution(mesh):
    counts = (mesh.shape["gx"], mesh.shape["gy"])
    return jax.shard_map(
        functools.partial(per_device, counts),
        mesh=mesh,
        in_specs=(
            P(None, "gx", "gy", None),
            P("gx", "gy", None),
            P("gx", "gy", None, None, None, None),
            P("gx", "gy", None, None),
            P("gx", "gy", None, None),
            P("gx", "gy", None, None),
        ),
        out_specs=(P(None, "gx", "gy", None), P(None, "gx", "gy", None)),
        check_vma=False,
    )
```

```python
import functools

import jax
import jax.numpy as jnp
from jax import lax
from jax.experimental import pallas as pl
from jax.experimental.pallas import tpu as pltpu
from jax.sharding import PartitionSpec as P

POISSON = 0.3
DAMPING = 0.7
KEPT = 1.0 - DAMPING
SWEEPS = 4
LANES = 128
BRICK = 4
AXES = ("gx", "gy")
VMEM_BYTES = 24 * 1024 * 1024
F32 = jnp.float32


def pairings(axis, counts):
    count_x, count_y = counts
    even, odd = [], []
    for x in range(count_x):
        for y in range(count_y):
            k, count = (x, count_x) if axis == "gx" else (y, count_y)
            move = lambda to: (to, y) if axis == "gx" else (x, to)
            even.append(((x, y), move(k ^ 1)))
            if 0 < k < count - 1:
                odd.append(((x, y), move(k + 1 if k % 2 else k - 1)))
            else:
                odd.append(((x, y), (x, y ^ 1) if axis == "gx" else (x ^ 1, y)))
    flat = lambda pairs: [(a * count_y + b, c * count_y + d) for (a, b), (c, d) in pairs]
    return flat(even), flat(odd)


def exchange(first, second, axis, counts):
    even, odd = pairings(axis, counts)
    return lax.ppermute(first, AXES, even), lax.ppermute(second, AXES, odd)


SIDE = [(x, -1) for x in range(-2, 6)] + [(x, -2) for x in range(-1, 5)]
SIDE_X = [(x, y) for x in (-2, -1) for y in range(BRICK)]
SIDE_Y_IMAGE = [(x, y) for y in (-2, -1, 0) for x in range(-1, 5)]
SIDE_X_IMAGE = [(0, y) for y in range(-2, 6)] + [(y, x) for x, y in SIDE]


def mirror(x, y):
    return x, BRICK - 1 - y


def mirror_x(x, y):
    return BRICK - 1 - x, y


def lane_index():
    return lax.broadcasted_iota(jnp.int32, (1, LANES), 1)


def as_f32(cond):
    return jnp.where(cond, 1.0, 0.0).astype(F32)


def turn(x, shift):
    return pltpu.roll(x, shift % LANES, x.ndim - 1)


class Place:
    def __init__(self, count_x, count_y):
        self.gx = lax.axis_index("gx")
        self.gy = lax.axis_index("gy")
        self.count_x, self.count_y = count_x, count_y
        flag = lambda cond: jnp.where(cond, 1.0, 0.0).astype(F32)
        self.even_x = flag(self.gx % 2 == 0)
        self.even_y = flag(self.gy % 2 == 0)
        self.in_x = {-1: flag(self.gx > 0), 0: None, 1: flag(self.gx < count_x - 1)}
        self.in_y = {-1: flag(self.gy > 0), 0: None, 1: flag(self.gy < count_y - 1)}

    def keep(self, value, x, y, size):
        side_x = -1 if x < 0 else 1 if x >= size else 0
        side_y = -1 if y < 0 else 1 if y >= size else 0
        if side_x:
            value = value * self.in_x[side_x]
        if side_y:
            value = value * self.in_y[side_y]
        return value


class Shifts:
    def __init__(self):
        lane = lane_index()
        self.low = {d: as_f32(lane >= d) for d in (1, 2, 4)}
        self.high = {d: as_f32(lane < LANES - d) for d in (1, 2, 4)}
        self.even = as_f32(lane % 2 == 0)
        self.odd = 1.0 - self.even

    def beside(self, x, d):
        return turn(x, d) * self.low[d] + turn(x, -d) * self.high[d]

    def pair_sum(self, x):
        t = (x + turn(x, -1)) * self.even
        return t + turn(t, 1)


def memo(fn):
    kept = {}

    def wrapped(x, y):
        if (x, y) not in kept:
            kept[(x, y)] = fn(x, y)
        return kept[(x, y)]

    return wrapped


def beside_all(e, x, y, shifts, step):
    return e(x + 1, y) + e(x - 1, y) + e(x, y + 1) + e(x, y - 1) + shifts.beside(e(x, y), step)


def contribution(w, weight0, columns, cells, shifts):
    inside = set(columns)
    e0 = memo(lambda x, y: weight0(x, y) * w(x, y) if (x, y) in inside else None)

    def rest(x, y):
        beside = [v for v in (e0(x + 1, y), e0(x - 1, y), e0(x, y + 1), e0(x, y - 1)) if v is not None]
        total = sum(beside) if beside else None
        c = e0(x, y)
        if c is None:
            return total
        near = shifts.beside(c, 1) if total is None else total + shifts.beside(c, 1)
        return KEPT * w(x, y) + near

    out = {}
    for x, y in cells:
        parts = [rest(2 * x + i, 2 * y + j) for i in range(2) for j in range(2)]
        out[x, y] = shifts.pair_sum(sum(v for v in parts if v is not None))
    return out


class Levels:
    def __init__(self, count_x, count_y, shifts):
        self.count_x, self.count_y, self.shifts = count_x, count_y, shifts
        row = lax.broadcasted_iota(jnp.int32, (1, count_x, LANES), 1)
        lane = lax.broadcasted_iota(jnp.int32, (1, 1, LANES), 2)
        self.x_low, self.x_high = as_f32(row > 0), as_f32(row < count_x - 1)
        self.even = as_f32(lane % 2 == 0)
        self.odd = 1.0 - self.even
        self.first = as_f32(lane % 4 == 0)
        self.low, self.high = as_f32(lane >= 4), as_f32(lane < LANES - 4)
        self.z_low, self.z_high = self.low * as_f32(lane % 4 >= 2), self.high * as_f32(lane % 4 < 2)
        self.edge = jnp.zeros((1, count_x, LANES), F32)

    def load(self, ref, first, stride):
        pick = lambda y: ref[pl.ds(first + stride * y, self.count_x, stride=stride * self.count_y), :]
        return jnp.stack([pick(y) for y in range(self.count_y)])

    def below_x(self, v):
        return pltpu.roll(v, 1, 1) * self.x_low

    def above_x(self, v):
        return pltpu.roll(v, self.count_x - 1, 1) * self.x_high

    def below_y(self, v):
        return jnp.concatenate([self.edge, v[:-1]], axis=0)

    def above_y(self, v):
        return jnp.concatenate([v[1:], self.edge], axis=0)

    def beside(self, v, d):
        return turn(v, d) * self.low + turn(v, -d) * self.high

    def gather_y(self, first, second):
        return (first + self.below_y(second)) * self.even + (second + self.above_y(first)) * self.odd

    def quad_sum(self, v):
        v = (v + turn(v, -1) + turn(v, -2) + turn(v, -3)) * self.first
        return v + turn(v, 1) + turn(v, 2) + turn(v, 3)

    def restrict(self, r, e):
        t = e[0] + e[1]
        near = 3.0 * t + self.below_x(e[1]) + self.above_x(e[0]) + self.below_y(t) * self.odd
        near = near + self.above_y(t) * self.even + turn(t, 4) * self.z_low + turn(t, -4) * self.z_high
        return self.quad_sum(KEPT * (r[0] + r[1]) + 2.0 * near)

    def solve_2(self, r2, weight):
        start = weight * r2
        weight = 4.0 * weight
        e = start
        for _ in range(SWEEPS - 1):
            near = self.below_x(e) + self.above_x(e) + self.below_y(e) + self.above_y(e) + self.beside(e, 4)
            e = (KEPT * e + start) + weight * near
        return e


def pack_y(cells, x, shifts):
    return (
        cells[x, 0] * shifts.even + cells[x, -1] * shifts.odd,
        cells[x, 1] * shifts.odd + cells[x, 2] * shifts.even,
    )


def put_rows(slot_ref, row, column):
    for m in range(3):
        slot_ref[row + m] = column[m : m + 1]


def fine_level(r, f1, weight0, place, shifts):
    first = memo(lambda x, y: weight0(x, y) * r(x, y))
    e0 = memo(lambda x, y: first(x, y) + f1(x // 2, y // 2))

    def at(x, y):
        value = KEPT * e0(x, y) + first(x, y) + weight0(x, y) * beside_all(e0, x, y, shifts, 1)
        return place.keep(value, x, y, BRICK)

    return memo(at)


def stiffness_apply(z, hot, x_ref, effective_ref, grad_ref, nodes, forces_a, forces_b, picked_a, picked_b, spread_sums, shifts):
    blocks = grad_ref.shape[2]
    turns = [(b, c) for b in range(3) for c in range(3)]
    span = BRICK + 2

    def halves(x):
        high = x.astype(jnp.bfloat16).astype(F32)
        return jnp.concatenate([high, x - high], axis=0)

    split = {}
    for x in range(span):
        for y in range(span):
            whole = halves(z(x - 1, y - 1))
            split[x, y, 1] = whole
            split[x, y, 0] = turn(whole, 1) * shifts.low[1]
            split[x, y, 2] = turn(whole, -1) * shifts.high[1]
    for u, (b, c) in enumerate(turns):
        for j in range(BRICK):
            for x in range(0, span, 2):
                pair = jnp.concatenate([split[x, j + b, c], split[x + 1, j + b, c]], axis=0).astype(jnp.bfloat16)
                row = (u * span + x) * 8
                nodes[row : row + 16, j * LANES : (j + 1) * LANES] = pair

    node_x = x_ref[...]
    half = blocks // 2
    lanes_a, lanes_b = slice(0, half * LANES), slice(half * LANES, blocks * LANES)
    picked_a[...] = jnp.dot(nodes[...], hot[:, lanes_a], preferred_element_type=F32)
    picked_b[...] = jnp.dot(nodes[...], hot[:, lanes_b], preferred_element_type=F32)

    first = POISSON / ((1.0 + POISSON) * (1.0 - 2.0 * POISSON))
    shear_of = 0.5 / (1.0 + POISSON)
    row8 = lax.broadcasted_iota(jnp.int32, (8, LANES), 0)
    row_is = [as_f32(row8 % 4 == m) for m in range(3)]
    is_high = row8 < 4
    zero = jnp.zeros((8, LANES), F32)
    wide = lambda row: jnp.broadcast_to(row, (8, LANES))
    for s in range(blocks):
        lanes = slice(s % half * LANES, (s % half + 1) * LANES)
        picked, forces = (picked_a, forces_a) if s < half else (picked_b, forces_b)
        grad = lambda l, a, b, c: wide(grad_ref[l, 9 * a + 3 * b + c, s : s + 1, :])
        at_x = [wide(node_x[s : s + 1]) == i for i in range(BRICK)]
        h = [None] * 3
        for u, (b, c) in enumerate(turns):
            tiles = [picked[(u * span + x) * 8 : (u * span + x) * 8 + 8, lanes] for x in range(span)]
            for a in range(3):
                value = tiles[3 + a]
                for i in (2, 1, 0):
                    value = jnp.where(at_x[i], tiles[i + a], value)
                for l in range(3):
                    term = value * grad(l, a, b, c)
                    h[l] = term if h[l] is None else h[l] + term
        h = [x[0:4] + x[4:8] for x in h]
        h = [[h[l][m : m + 1] for l in range(3)] for m in range(3)]
        effective = effective_ref[s : s + 1]
        shear = effective * shear_of
        bulk = effective * first * (h[0][0] + h[1][1] + h[2][2])
        stress = []
        for l in range(3):
            column = 0.0
            for m in range(3):
                entry = shear * (h[m][l] + h[l][m])
                if l == m:
                    entry = entry + bulk
                column = column + wide(entry) * row_is[m]
            stress.append(column)
        for u, (b, c) in enumerate(turns):
            parts = []
            for a in range(3):
                f = stress[0] * grad(0, a, b, c) + stress[1] * grad(1, a, b, c) + stress[2] * grad(2, a, b, c)
                high = f.astype(jnp.bfloat16).astype(F32)
                parts.append(jnp.where(is_high, high, f - high))
            tiles = []
            for x in range(span):
                tile = zero
                for a in range(3):
                    if 0 <= x - a < BRICK:
                        tile = jnp.where(at_x[x - a], parts[a], tile)
                tiles.append(tile)
            for x in range(0, span, 2):
                row = (u * span + x) * 8
                pair = jnp.concatenate([tiles[x], tiles[x + 1]], axis=0).astype(jnp.bfloat16)
                forces[row : row + 16, lanes] = pair
        if s == half - 1:
            spread_sums[...] = lax.dot_general(
                forces_a[...], hot[:, lanes_a], (((1,), (1,)), ((), ())), preferred_element_type=F32
            )
    spread_sums[...] += lax.dot_general(
        forces_b[...], hot[:, lanes_b], (((1,), (1,)), ((), ())), preferred_element_type=F32
    )
    out = {}
    for x in range(span):
        for y in range(span):
            sums = [0.0, 0.0, 0.0]
            for u, (b, c) in enumerate(turns):
                j = y - b
                if 0 <= j < BRICK:
                    row = (u * span + x) * 8
                    sums[c] = sums[c] + spread_sums[row : row + 8, j * LANES : (j + 1) * LANES]
            total = sums[1] + turn(sums[0], -1) * shifts.high[1] + turn(sums[2], 1) * shifts.low[1]
            out[x - 1, y - 1] = total[0:4] + total[4:8]
    return out


def particle_kernel(counts, base_ref, stiff_ref, valid_ref, hot_ref, x_ref, effective_ref):
    span = BRICK + 2
    base = base_ref[...]
    plane = base // (LANES + 2)
    depth = base - plane * (LANES + 2)
    node_x = plane // span
    node_y = plane - node_x * span
    x_ref[...] = node_x
    effective_ref[...] = stiff_ref[...] * valid_ref[...].astype(F32)
    sub = lax.broadcasted_iota(jnp.int32, (LANES, LANES), 0)
    for s in range(base_ref.shape[0]):
        for j in range(BRICK):
            wanted = jnp.where(node_y[s : s + 1] == j, depth[s : s + 1], -1)
            hot_ref[j * LANES : (j + 1) * LANES, s * LANES : (s + 1) * LANES] = as_f32(sub == wanted).astype(jnp.bfloat16)


def side_parts(even_ref, odd_ref, is_even, inside_low, inside_high):
    odd = 1.0 - is_even
    below_odd, below_even = inside_low * is_even, inside_low * odd
    above_odd, above_even = inside_high * odd, inside_high * is_even

    def below(row, size):
        return odd_ref[row : row + size, :] * below_odd + even_ref[row : row + size, :] * below_even

    def above(row, size):
        return odd_ref[row : row + size, :] * above_odd + even_ref[row : row + size, :] * above_even

    return below, above


def put_sides(to_even_ref, to_odd_ref, row, size, up, down, is_even):
    odd = 1.0 - is_even
    to_even_ref[row : row + size, :] = (up * is_even + down * odd)[0:size]
    to_odd_ref[row : row + size, :] = (down * is_even + up * odd)[0:size]


def clear_tail(*refs):
    for ref in refs:
        ref[ref.shape[0] - 8 :, :] = jnp.zeros((8, LANES), F32)


def weight_of(mass):
    return DAMPING / (mass + 6.0)


def spread_mass(column):
    return jnp.broadcast_to(column[3:4], (4, LANES))


def live_rows():
    return as_f32(lax.broadcasted_iota(jnp.int32, (4, LANES), 0) < 3)


FIRST_ROWS = 20
SECOND_ROWS = 13


def pack_kernel(counts, fields_ref, own_ref, even_ref, odd_ref, slot_ref):
    place, shifts = Place(*counts), Shifts()
    own = {}
    for x in range(BRICK):
        for y in range(BRICK):
            own[x, y] = jnp.concatenate([fields_ref[m, x, y : y + 1, :] for m in range(4)], axis=0)
            own_ref[x, y] = own[x, y]
    odd_x = 1.0 - place.even_x
    for k, (x, y) in enumerate(SIDE_X):
        up, down = own[x + 4, y], own[-1 - x, y]
        even_ref[k] = up * place.even_x + down * odd_x
        odd_ref[k] = down * place.even_x + up * odd_x
    live = live_rows()
    mass0 = memo(lambda x, y: spread_mass(own[x, y]))
    weight0 = memo(lambda x, y: weight_of(mass0(x, y)))
    r = memo(lambda x, y: own[x, y] * live)
    cells = [(x, y) for x in (0, 1) for y in range(-1, 3)] + [(x, y) for x in (-1, 2) for y in (0, 1)]
    part = contribution(r, weight0, INNER, cells, shifts)
    rows = []
    for x in (0, 1):
        for column in pack_y(part, x, shifts):
            rows += [column[m : m + 1] for m in range(3)]
    for x in (-1, 2):
        column = part[x, 0] * shifts.even + part[x, 1] * shifts.odd
        rows += [column[m : m + 1] for m in range(3)]
    for x in (0, 1):
        mass1 = [
            shifts.pair_sum(sum(own[2 * x + i, 2 * y + j][3:4] for i in range(2) for j in range(2))) for y in (0, 1)
        ]
        rows.append(mass1[0] * shifts.even + mass1[1] * shifts.odd)
    for k in range(FIRST_ROWS // 4):
        slot_ref[k] = jnp.concatenate(rows[4 * k : 4 * k + 4], axis=0)


def widen_kernel(counts, own_ref, even_ref, odd_ref, wide_ref, to_even_ref, to_odd_ref):
    place = Place(*counts)
    odd_x = 1.0 - place.even_x
    left = (place.in_x[-1] * place.even_x, place.in_x[-1] * odd_x)
    right = (place.in_x[1] * odd_x, place.in_x[1] * place.even_x)

    def value(x, y):
        if 0 <= x < BRICK:
            return own_ref[x, y]
        odd, even = left if x < 0 else right
        k = SIDE_X.index((x, y) if x < 0 else mirror_x(x, y))
        return odd_ref[k] * odd + even_ref[k] * even

    value = memo(value)
    for x in range(-2, 6):
        for y in range(BRICK):
            wide_ref[x + 2, y] = value(x, y)
    odd_y = 1.0 - place.even_y
    for k, (x, y) in enumerate(SIDE):
        up, down = value(x, y + 4), value(x, -1 - y)
        to_even_ref[k] = up * place.even_y + down * odd_y
        to_odd_ref[k] = down * place.even_y + up * odd_y


def start_kernel(counts, wide_ref, even_ref, odd_ref, r_ref, mass0_ref, weight0_ref):
    place = Place(*counts)
    live = live_rows()
    odd_y = 1.0 - place.even_y
    below = (place.in_y[-1] * place.even_y, place.in_y[-1] * odd_y)
    above = (place.in_y[1] * odd_y, place.in_y[1] * place.even_y)
    for x in range(-2, 6):
        for y in range(-2, 6):
            if 0 <= y < BRICK:
                value = wide_ref[x + 2, y]
            else:
                key = (x, y) if y < 0 else mirror(x, y)
                odd, even = below if y < 0 else above
                if key in SIDE:
                    k = SIDE.index(key)
                    value = odd_ref[k] * odd + even_ref[k] * even
                else:
                    value = jnp.zeros((4, LANES), F32)
            r_ref[x + 2, y + 2] = value * live
            mass = spread_mass(value)
            mass0_ref[x + 2, y + 2] = mass
            weight0_ref[x + 2, y + 2] = weight_of(mass)


def reader(ref, offset):
    return memo(lambda x, y: ref[x + offset, y + offset])


def cycle(place, shifts, levels, r, r1, mass1, weight0, middle, coarse):
    width = place.count_x
    margin = 8 * (width + 1)

    def put(ref, row, value):
        for y in range(place.count_y):
            ref[pl.ds(margin + 8 * width * y + row, width, stride=8), :] = value[y]

    def get(ref, x, y):
        brick = (place.gy + y) * width + place.gx + x
        return ref[pl.ds(pl.multiple_of(margin + brick * 8, 8), 8), :]

    weight1 = [DAMPING / (m + 12.0) for m in mass1]
    weight2 = DAMPING / (levels.quad_sum(mass1[0] + mass1[1]) + 24.0)
    middle[...] = jnp.zeros_like(middle)
    coarse[...] = jnp.zeros_like(coarse)
    for x in range(2):
        put(middle, 4 * x + 3, weight1[x])
    for m in range(3):
        e = [weight1[x] * r1[m][x] for x in range(2)]
        for x in range(2):
            put(middle, 4 * x + m, e[x])
        put(coarse, m, levels.solve_2(levels.restrict(r1[m], e), weight2))

    def brick_at(x, y):
        rows = get(middle, x, y)
        first, second = rows * shifts.even, rows * shifts.odd
        return first + turn(first, 1), second + turn(second, -1)

    brick_at = memo(brick_at)

    def first_at(x, y):
        both = brick_at(x // 2, y // 2)[y % 2]
        return place.keep(both[4 * (x % 2) : 4 * (x % 2) + 4], x, y, 2)

    first = memo(first_at)
    e2 = memo(lambda x, y: place.keep(get(coarse, x, y)[0:4], x, y, 1))
    e1 = memo(lambda x, y: first(x, y) + e2(x // 2, y // 2))
    live = live_rows()

    def f1_at(x, y):
        weight = 2.0 * spread_mass(first(x, y))
        value = KEPT * e1(x, y) + first(x, y) + weight * beside_all(e1, x, y, shifts, 2)
        return place.keep(value * live, x, y, 2)

    return fine_level(r, memo(f1_at), weight0, place, shifts)


def apply(z, mass0, particles, work, shifts):
    image = stiffness_apply(z, *particles, *work, shifts)
    for x, y in INNER:
        image[x, y] = image[x, y] + mass0(x, y) * z(x, y)
    return image


def total_of(pairs):
    acc = 0.0
    for a, b in pairs:
        acc = acc + a * b
    return jnp.sum(jnp.sum(acc, axis=0, keepdims=True), axis=1, keepdims=True)


def dots_row(*values):
    lane = lane_index()
    row = 0.0
    for k, v in enumerate(values):
        row = row + as_f32(lane == k) * v
    return row


INNER = [(x, y) for x in range(BRICK) for y in range(BRICK)]
RIMMED = [(x, y) for x in range(-1, BRICK + 1) for y in range(-1, BRICK + 1)]


def first_kernel(counts, level_ref, r_ref, mass0_ref, weight0_ref,
                 hot_ref, x_ref, effective_ref, grad_ref, z_ref, image_ref, even_ref, odd_ref, dots_ref, mass1_ref,
                 *scratch):
    particles = (hot_ref, x_ref, effective_ref, grad_ref)
    place, shifts = Place(*counts), Shifts()
    levels = Levels(*counts, shifts)
    rows = lambda q: levels.load(level_ref, q, FIRST_ROWS)
    r1 = []
    for m in range(3):
        pair = [levels.gather_y(rows(6 * x + m), rows(6 * x + 3 + m)) for x in range(2)]
        pair[1] = pair[1] + levels.above_x(rows(12 + m))
        pair[0] = pair[0] + levels.below_x(rows(15 + m))
        r1.append(pair)
    mass1 = [rows(18), rows(19)]
    for x in range(2):
        mass1_ref[x] = mass1[x]
    r = reader(r_ref, 2)
    middle, coarse, *work = scratch
    z = cycle(place, shifts, levels, r, r1, mass1, reader(weight0_ref, 2), middle, coarse)
    image = apply(z, reader(mass0_ref, 2), particles, work, shifts)
    for x, y in RIMMED:
        z_ref[x + 1, y + 1] = z(x, y)
    for x, y in RIMMED:
        image_ref[x + 1, y + 1] = image[x, y]
    clear_tail(even_ref, odd_ref)
    for k, (x, y) in enumerate(SIDE_Y_IMAGE):
        put_sides(even_ref, odd_ref, 3 * k, 3, image[x, y + 4], image[x, -1 - y], place.even_y)
    rz = total_of((r(x, y), z(x, y)) for x, y in INNER)
    zaz = total_of((image[x, y], z(x, y)) for x, y in RIMMED)
    dots_ref[...] = dots_row(rz, zaz)


def along_y_kernel(counts, image_ref, even_ref, odd_ref, weight0_ref, dots_ref,
                   long_ref, to_even_ref, to_odd_ref, slot_ref):
    place, shifts = Place(*counts), Shifts()
    below, above = side_parts(even_ref, odd_ref, place.even_y, place.in_y[-1], place.in_y[1])

    def value(x, y):
        total = None
        if -1 <= y <= 4:
            total = place.keep(image_ref[x + 1, y + 1], x, y, BRICK)
        for part, key in ((below, (x, y)), (above, mirror(x, y))):
            if key in SIDE_Y_IMAGE:
                more = place.keep(part(3 * SIDE_Y_IMAGE.index(key), 4), x, 0, BRICK)
                total = more if total is None else total + more
        return total

    value = memo(value)
    cells = [(x, y) for x in range(-1, 3) for y in (0, 1)]
    part = contribution(value, reader(weight0_ref, 2), RIMMED, cells, shifts)
    for x in range(-1, 3):
        put_rows(slot_ref, 3 * (x + 1), part[x, 0] * shifts.even + part[x, 1] * shifts.odd)
    slot_ref[12] = dots_ref[...]
    clear_tail(to_even_ref, to_odd_ref)
    for k, (x, y) in enumerate(SIDE_X_IMAGE):
        put_sides(to_even_ref, to_odd_ref, 3 * k, 3, value(x + 4, y), value(-1 - x, y), place.even_x)
    for x in range(-1, BRICK + 1):
        for y in range(-2, 6):
            long_ref[x + 1, y + 2] = value(x, y)


def middle_kernel(counts, long_ref, even_ref, odd_ref, w_ref):
    place = Place(*counts)
    left, right = side_parts(even_ref, odd_ref, place.even_x, place.in_x[-1], place.in_x[1])
    live = live_rows()
    for x in range(-2, 6):
        for y in range(-2, 6):
            total = jnp.zeros((4, LANES), F32)
            if -1 <= x <= 4:
                total = total + long_ref[x + 1, y + 2]
            for part, key in ((left, (x, y)), (right, mirror_x(x, y))):
                if key in SIDE_X_IMAGE:
                    total = total + part(3 * SIDE_X_IMAGE.index(key), 4)
            w_ref[x + 2, y + 2] = total * live


def sums_of(ref, count, first, stride):
    return jnp.sum(ref[pl.ds(first, count, stride=stride), :], axis=0, keepdims=True)


def second_kernel(counts, change_ref, z1_ref, mass1_ref, r_ref, w_ref, mass0_ref, weight0_ref,
                  hot_ref, x_ref, effective_ref, grad_ref, z_ref, image_ref, x_even_ref, x_odd_ref, y_even_ref, y_odd_ref,
                  slots_ref, *scratch):
    particles = (hot_ref, x_ref, effective_ref, grad_ref)
    place, shifts = Place(*counts), Shifts()
    bricks = counts[0] * counts[1]
    levels = Levels(*counts, shifts)
    sums = sums_of(change_ref, bricks, 12, SECOND_ROWS)
    step = sums[:, 0:1] / sums[:, 1:2]
    rows = lambda q: levels.load(change_ref, q, SECOND_ROWS)
    r1 = []
    for m in range(3):
        r1.append([rows(3 + m) + levels.below_x(rows(9 + m)), rows(6 + m) + levels.above_x(rows(m))])
    w = reader(w_ref, 2)
    middle, coarse, *work = scratch
    of_w = cycle(place, shifts, levels, w, r1, [mass1_ref[0], mass1_ref[1]], reader(weight0_ref, 2), middle, coarse)
    z = memo(lambda x, y: z1_ref[x + 1, y + 1] - step * of_w(x, y))
    image = apply(z, reader(mass0_ref, 2), particles, work, shifts)
    r = memo(lambda x, y: r_ref[x + 2, y + 2] - step * w(x, y))
    for x, y in INNER:
        z_ref[x, y] = z(x, y)
        image_ref[x, y] = image[x, y]
    rz = total_of((r(x, y), z(x, y)) for x, y in INNER)
    zaz = total_of((image[x, y], z(x, y)) for x, y in RIMMED)
    zw = total_of((w_ref[x + 2, y + 2], z(x, y)) for x, y in INNER)
    row = dots_row(rz, zaz, zw)
    plain = jnp.concatenate([jnp.zeros((3, LANES), F32), row], axis=0)

    def fill(k, carry):
        slots_ref[k, 0] = plain
        return carry

    lax.fori_loop(0, bricks, fill, 0)
    for dx in (-1, 1):
        for dy in (-1, 1):
            there_x = (place.gx + dx >= 0) & (place.gx + dx < counts[0])
            there_y = (place.gy + dy >= 0) & (place.gy + dy < counts[1])
            column = image[BRICK if dx > 0 else -1, BRICK if dy > 0 else -1]

            @pl.when(there_x & there_y)
            def _(column=column, dx=dx, dy=dy):
                other = (place.gx + dx) * counts[1] + place.gy + dy
                slots_ref[other, 0] = jnp.concatenate([column[0:3], row], axis=0)

    clear_tail(x_even_ref, x_odd_ref, y_even_ref, y_odd_ref)
    for k in range(BRICK):
        put_sides(x_even_ref, x_odd_ref, 3 * k, 3, image[BRICK, k], image[-1, k], place.even_x)
        put_sides(y_even_ref, y_odd_ref, 3 * k, 3, image[k, BRICK], image[k, -1], place.even_y)


def last_kernel(counts, slots_ref, x_even_ref, x_odd_ref, y_even_ref, y_odd_ref, change_ref, z1_ref, z2_ref, r_ref, w_ref, image_ref, solution_ref, residual_ref):
    place = Place(*counts)
    bricks = counts[0] * counts[1]
    sums1 = sums_of(change_ref, bricks, 12, SECOND_ROWS)
    sums2 = jnp.sum(slots_ref[:, 0], axis=0)[3:4]
    rz1, zaz1 = sums1[:, 0:1], sums1[:, 1:2]
    rz2, zaz2, zw = sums2[:, 0:1], sums2[:, 1:2], sums2[:, 2:3]
    step1 = rz1 / zaz1
    ratio = rz2 / rz1
    step2 = rz2 / (zaz2 + 2.0 * ratio * zw + ratio * ratio * zaz1)
    image = {(x, y): image_ref[x, y] for x, y in INNER}
    left, right = side_parts(x_even_ref, x_odd_ref, place.even_x, place.in_x[-1], place.in_x[1])
    below, above = side_parts(y_even_ref, y_odd_ref, place.even_y, place.in_y[-1], place.in_y[1])
    end = BRICK - 1
    for k in range(BRICK):
        for at, part in (((0, k), left), ((end, k), right), ((k, 0), below), ((k, end), above)):
            image[at] = image[at] + part(3 * k, 4)
    for dx in (-1, 1):
        for dy in (-1, 1):
            other_x = jnp.clip(place.gx + dx, 0, counts[0] - 1)
            other_y = jnp.clip(place.gy + dy, 0, counts[1] - 1)
            other = other_x * counts[1] + other_y
            column = slots_ref[other, 0]
            at = (end if dx > 0 else 0, end if dy > 0 else 0)
            image[at] = image[at] + place.keep(column, dx, dy, 1)
    for x, y in INNER:
        w = w_ref[x + 2, y + 2]
        z1 = z1_ref[x + 1, y + 1]
        solution = step1 * z1 + step2 * (z2_ref[x, y] + ratio * z1)
        residual = r_ref[x + 2, y + 2] - step1 * w - step2 * (image[x, y] + ratio * w)
        for m in range(3):
            solution_ref[m, x, y : y + 1, :] = solution[m : m + 1]
            residual_ref[m, x, y : y + 1, :] = residual[m : m + 1]


def call(kernel, counts, shapes, *args, scratch=()):
    shapes = [s if isinstance(s[0], tuple) else (s, F32) for s in shapes]
    return pl.pallas_call(
        functools.partial(kernel, counts),
        out_shape=[jax.ShapeDtypeStruct(*s) for s in shapes],
        scratch_shapes=scratch,
        compiler_params=pltpu.CompilerParams(vmem_limit_bytes=VMEM_BYTES),
    )(*args)


def per_device(counts, right_side, node_mass, gradients, stiffness, valid, node_base):
    bricks = counts[0] * counts[1]
    blocks = gradients.shape[2]
    grid = (counts[1], counts[0], LANES)
    tiles = 9 * (BRICK + 2) * 8
    depth = BRICK * LANES
    width = blocks * LANES
    scratch = (
        *[pltpu.VMEM((8 * (bricks + 2 * (counts[0] + 1)), LANES), F32)] * 2,
        pltpu.VMEM((tiles, depth), jnp.bfloat16),
        *[pltpu.VMEM((tiles, width // 2), jnp.bfloat16)] * 2,
        *[pltpu.VMEM((tiles, width // 2), F32)] * 2,
        pltpu.VMEM((tiles, depth), F32),
    )
    rows = lambda columns: (-(-(3 * len(columns) + 1) // 8) * 8, LANES)
    block = lambda *dims: (*dims, 4, LANES)

    def share(slot):
        sent = jnp.broadcast_to(slot[None], (bricks, *slot.shape))
        return lax.all_to_all(sent, AXES, 0, 0).reshape(-1, LANES)

    fields = jnp.concatenate([right_side, node_mass[None]], axis=0)
    own, to_even, to_odd, slot = call(
        pack_kernel, counts, [block(4, 4), block(8), block(8), block(FIRST_ROWS // 4)], fields
    )
    level = share(slot)
    even, odd = exchange(to_even, to_odd, "gx", counts)
    side = block(len(SIDE))
    wide, to_even, to_odd = call(widen_kernel, counts, [block(8, 4), side, side], own, even, odd)
    even, odd = exchange(to_even, to_odd, "gy", counts)
    row = (blocks, LANES)
    prepared = call(
        particle_kernel, counts, [((depth, width), jnp.bfloat16), (row, jnp.int32), row],
        node_base[0, 0], stiffness[0, 0], valid[0, 0],
    )
    particles = (*prepared, gradients[0, 0].transpose(1, 2, 0, 3))
    r, *fields = call(start_kernel, counts, [block(8, 8)] * 3, wide, even, odd)

    side = rows(SIDE_Y_IMAGE)
    z1, image, to_even, to_odd, dots, mass1 = call(
        first_kernel, counts,
        [block(6, 6), block(6, 6), side, side, (1, LANES), (2, *grid)],
        level, r, *fields, *particles, scratch=scratch,
    )
    even, odd = exchange(to_even, to_odd, "gy", counts)
    side = rows(SIDE_X_IMAGE)
    long, to_even, to_odd, slot = call(
        along_y_kernel, counts, [block(6, 8), side, side, (SECOND_ROWS, 1, LANES)], image, even, odd, fields[1], dots
    )
    change = share(slot)
    even, odd = exchange(to_even, to_odd, "gx", counts)
    (w,) = call(middle_kernel, counts, [block(8, 8)], long, even, odd)
    side = (2 * 8, LANES)
    z2, image, x_even, x_odd, y_even, y_odd, slots = call(
        second_kernel, counts, [block(4, 4), block(4, 4), side, side, side, side, (bricks, 1, 4, LANES)],
        change, z1, mass1, r, w, *fields, *particles, scratch=scratch,
    )
    sides = (*exchange(x_even, x_odd, "gx", counts), *exchange(y_even, y_odd, "gy", counts))
    slots = lax.all_to_all(slots, AXES, 0, 0)
    return tuple(
        call(last_kernel, counts, [right_side.shape, right_side.shape], slots, *sides, change, z1, z2, r, w, image)
    )


def solution(mesh):
    counts = (mesh.shape["gx"], mesh.shape["gy"])
    return jax.shard_map(
        functools.partial(per_device, counts),
        mesh=mesh,
        in_specs=(
            P(None, "gx", "gy", None),
            P("gx", "gy", None),
            P("gx", "gy", None, None, None, None),
            P("gx", "gy", None, None),
            P("gx", "gy", None, None),
            P("gx", "gy", None, None),
        ),
        out_specs=(P(None, "gx", "gy", None), P(None, "gx", "gy", None)),
        check_vma=False,
    )
```

```python
import functools

import jax
import jax.numpy as jnp
from jax import lax
from jax.experimental import pallas as pl
from jax.experimental.pallas import tpu as pltpu
from jax.sharding import PartitionSpec as P

POISSON = 0.3
DAMPING = 0.7
KEPT = 1.0 - DAMPING
SWEEPS = 4
LANES = 128
BRICK = 4
AXES = ("gx", "gy")
VMEM_BYTES = 24 * 1024 * 1024
F32 = jnp.float32


def pairings(axis, counts):
    count_x, count_y = counts
    even, odd = [], []
    for x in range(count_x):
        for y in range(count_y):
            k, count = (x, count_x) if axis == "gx" else (y, count_y)
            move = lambda to: (to, y) if axis == "gx" else (x, to)
            even.append(((x, y), move(k ^ 1)))
            if 0 < k < count - 1:
                odd.append(((x, y), move(k + 1 if k % 2 else k - 1)))
            else:
                odd.append(((x, y), (x, y ^ 1) if axis == "gx" else (x ^ 1, y)))
    flat = lambda pairs: [(a * count_y + b, c * count_y + d) for (a, b), (c, d) in pairs]
    return flat(even), flat(odd)


def exchange(first, second, axis, counts):
    even, odd = pairings(axis, counts)
    return lax.ppermute(first, AXES, even), lax.ppermute(second, AXES, odd)


SIDE = [(x, -1) for x in range(-2, 6)] + [(x, -2) for x in range(-1, 5)]
SIDE_X = [(x, y) for x in (-2, -1) for y in range(BRICK)]
SIDE_Y_IMAGE = [(x, y) for y in (-2, -1, 0) for x in range(-1, 5)]
SIDE_X_IMAGE = [(0, y) for y in range(-2, 6)] + [(y, x) for x, y in SIDE]


def mirror(x, y):
    return x, BRICK - 1 - y


def mirror_x(x, y):
    return BRICK - 1 - x, y


def lane_index():
    return lax.broadcasted_iota(jnp.int32, (1, LANES), 1)


def as_f32(cond):
    return jnp.where(cond, 1.0, 0.0).astype(F32)


def turn(x, shift):
    return pltpu.roll(x, shift % LANES, x.ndim - 1)


class Place:
    def __init__(self, count_x, count_y):
        self.gx = lax.axis_index("gx")
        self.gy = lax.axis_index("gy")
        self.count_x, self.count_y = count_x, count_y
        flag = lambda cond: jnp.where(cond, 1.0, 0.0).astype(F32)
        self.even_x = flag(self.gx % 2 == 0)
        self.even_y = flag(self.gy % 2 == 0)
        self.in_x = {-1: flag(self.gx > 0), 0: None, 1: flag(self.gx < count_x - 1)}
        self.in_y = {-1: flag(self.gy > 0), 0: None, 1: flag(self.gy < count_y - 1)}

    def keep(self, value, x, y, size):
        side_x = -1 if x < 0 else 1 if x >= size else 0
        side_y = -1 if y < 0 else 1 if y >= size else 0
        if side_x:
            value = value * self.in_x[side_x]
        if side_y:
            value = value * self.in_y[side_y]
        return value


class Shifts:
    def __init__(self):
        lane = lane_index()
        self.low = {d: as_f32(lane >= d) for d in (1, 2, 4)}
        self.high = {d: as_f32(lane < LANES - d) for d in (1, 2, 4)}
        self.even = as_f32(lane % 2 == 0)
        self.odd = 1.0 - self.even

    def beside(self, x, d):
        return turn(x, d) * self.low[d] + turn(x, -d) * self.high[d]

    def pair_sum(self, x):
        t = (x + turn(x, -1)) * self.even
        return t + turn(t, 1)


def memo(fn):
    kept = {}

    def wrapped(x, y):
        if (x, y) not in kept:
            kept[(x, y)] = fn(x, y)
        return kept[(x, y)]

    return wrapped


def beside_all(e, x, y, shifts, step):
    return e(x + 1, y) + e(x - 1, y) + e(x, y + 1) + e(x, y - 1) + shifts.beside(e(x, y), step)


def contribution(w, weight0, columns, cells, shifts):
    inside = set(columns)
    e0 = memo(lambda x, y: weight0(x, y) * w(x, y) if (x, y) in inside else None)

    def rest(x, y):
        beside = [v for v in (e0(x + 1, y), e0(x - 1, y), e0(x, y + 1), e0(x, y - 1)) if v is not None]
        total = sum(beside) if beside else None
        c = e0(x, y)
        if c is None:
            return total
        near = shifts.beside(c, 1) if total is None else total + shifts.beside(c, 1)
        return KEPT * w(x, y) + near

    out = {}
    for x, y in cells:
        parts = [rest(2 * x + i, 2 * y + j) for i in range(2) for j in range(2)]
        out[x, y] = shifts.pair_sum(sum(v for v in parts if v is not None))
    return out


class Levels:
    def __init__(self, count_x, count_y, shifts):
        self.count_x, self.count_y, self.shifts = count_x, count_y, shifts
        row = lax.broadcasted_iota(jnp.int32, (1, count_x, LANES), 1)
        lane = lax.broadcasted_iota(jnp.int32, (1, 1, LANES), 2)
        self.x_low, self.x_high = as_f32(row > 0), as_f32(row < count_x - 1)
        self.even = as_f32(lane % 2 == 0)
        self.odd = 1.0 - self.even
        self.first = as_f32(lane % 4 == 0)
        self.low, self.high = as_f32(lane >= 4), as_f32(lane < LANES - 4)
        self.z_low, self.z_high = self.low * as_f32(lane % 4 >= 2), self.high * as_f32(lane % 4 < 2)
        self.edge = jnp.zeros((1, count_x, LANES), F32)

    def load(self, ref, first, stride):
        pick = lambda y: ref[pl.ds(first + stride * y, self.count_x, stride=stride * self.count_y), :]
        return jnp.stack([pick(y) for y in range(self.count_y)])

    def below_x(self, v):
        return pltpu.roll(v, 1, 1) * self.x_low

    def above_x(self, v):
        return pltpu.roll(v, self.count_x - 1, 1) * self.x_high

    def below_y(self, v):
        return jnp.concatenate([self.edge, v[:-1]], axis=0)

    def above_y(self, v):
        return jnp.concatenate([v[1:], self.edge], axis=0)

    def beside(self, v, d):
        return turn(v, d) * self.low + turn(v, -d) * self.high

    def gather_y(self, first, second):
        return (first + self.below_y(second)) * self.even + (second + self.above_y(first)) * self.odd

    def quad_sum(self, v):
        v = (v + turn(v, -1) + turn(v, -2) + turn(v, -3)) * self.first
        return v + turn(v, 1) + turn(v, 2) + turn(v, 3)

    def restrict(self, r, e):
        t = e[0] + e[1]
        near = 3.0 * t + self.below_x(e[1]) + self.above_x(e[0]) + self.below_y(t) * self.odd
        near = near + self.above_y(t) * self.even + turn(t, 4) * self.z_low + turn(t, -4) * self.z_high
        return self.quad_sum(KEPT * (r[0] + r[1]) + 2.0 * near)

    def solve_2(self, r2, weight):
        start = weight * r2
        weight = 4.0 * weight
        e = start
        for _ in range(SWEEPS - 1):
            near = self.below_x(e) + self.above_x(e) + self.below_y(e) + self.above_y(e) + self.beside(e, 4)
            e = (KEPT * e + start) + weight * near
        return e


def pack_y(cells, x, shifts):
    return (
        cells[x, 0] * shifts.even + cells[x, -1] * shifts.odd,
        cells[x, 1] * shifts.odd + cells[x, 2] * shifts.even,
    )


def put_rows(slot_ref, row, column):
    for m in range(3):
        slot_ref[row + m] = column[m : m + 1]


def fine_level(r, f1, weight0, place, shifts):
    first = memo(lambda x, y: weight0(x, y) * r(x, y))
    e0 = memo(lambda x, y: first(x, y) + f1(x // 2, y // 2))

    def at(x, y):
        value = KEPT * e0(x, y) + first(x, y) + weight0(x, y) * beside_all(e0, x, y, shifts, 1)
        return place.keep(value, x, y, BRICK)

    return memo(at)


def stiffness_apply(z, hot, x_ref, effective_ref, grad_ref, nodes, forces_a, forces_b, picked_a, picked_b, spread_sums, shifts):
    blocks = grad_ref.shape[2]
    turns = [(b, c) for b in range(3) for c in range(3)]
    span = BRICK + 2

    def halves(x):
        high = x.astype(jnp.bfloat16).astype(F32)
        return jnp.concatenate([high, x - high], axis=0)

    split = {}
    for x in range(span):
        for y in range(span):
            whole = halves(z(x - 1, y - 1))
            split[x, y, 1] = whole
            split[x, y, 0] = turn(whole, 1) * shifts.low[1]
            split[x, y, 2] = turn(whole, -1) * shifts.high[1]
    for u, (b, c) in enumerate(turns):
        for j in range(BRICK):
            for x in range(0, span, 2):
                pair = jnp.concatenate([split[x, j + b, c], split[x + 1, j + b, c]], axis=0).astype(jnp.bfloat16)
                row = (u * span + x) * 8
                nodes[row : row + 16, j * LANES : (j + 1) * LANES] = pair

    node_x = x_ref[...]
    half = blocks // 2
    lanes_a, lanes_b = slice(0, half * LANES), slice(half * LANES, blocks * LANES)
    picked_a[...] = jnp.dot(nodes[...], hot[:, lanes_a], preferred_element_type=F32)
    picked_b[...] = jnp.dot(nodes[...], hot[:, lanes_b], preferred_element_type=F32)

    first = POISSON / ((1.0 + POISSON) * (1.0 - 2.0 * POISSON))
    shear_of = 0.5 / (1.0 + POISSON)
    row8 = lax.broadcasted_iota(jnp.int32, (8, LANES), 0)
    row_is = [as_f32(row8 % 4 == m) for m in range(3)]
    is_high = row8 < 4
    zero = jnp.zeros((8, LANES), F32)
    wide = lambda row: jnp.broadcast_to(row, (8, LANES))
    for s in range(blocks):
        lanes = slice(s % half * LANES, (s % half + 1) * LANES)
        picked, forces = (picked_a, forces_a) if s < half else (picked_b, forces_b)
        grad = lambda l, a, b, c: wide(grad_ref[l, 9 * a + 3 * b + c, s : s + 1, :])
        at_x = [wide(node_x[s : s + 1]) == i for i in range(BRICK)]
        h = [None] * 3
        for u, (b, c) in enumerate(turns):
            tiles = [picked[(u * span + x) * 8 : (u * span + x) * 8 + 8, lanes] for x in range(span)]
            for a in range(3):
                value = tiles[3 + a]
                for i in (2, 1, 0):
                    value = jnp.where(at_x[i], tiles[i + a], value)
                for l in range(3):
                    term = value * grad(l, a, b, c)
                    h[l] = term if h[l] is None else h[l] + term
        h = [x[0:4] + x[4:8] for x in h]
        h = [[h[l][m : m + 1] for l in range(3)] for m in range(3)]
        effective = effective_ref[s : s + 1]
        shear = effective * shear_of
        bulk = effective * first * (h[0][0] + h[1][1] + h[2][2])
        stress = []
        for l in range(3):
            column = 0.0
            for m in range(3):
                entry = shear * (h[m][l] + h[l][m])
                if l == m:
                    entry = entry + bulk
                column = column + wide(entry) * row_is[m]
            stress.append(column)
        for u, (b, c) in enumerate(turns):
            parts = []
            for a in range(3):
                f = stress[0] * grad(0, a, b, c) + stress[1] * grad(1, a, b, c) + stress[2] * grad(2, a, b, c)
                high = f.astype(jnp.bfloat16).astype(F32)
                parts.append(jnp.where(is_high, high, f - high))
            tiles = []
            for x in range(span):
                tile = zero
                for a in range(3):
                    if 0 <= x - a < BRICK:
                        tile = jnp.where(at_x[x - a], parts[a], tile)
                tiles.append(tile)
            for x in range(0, span, 2):
                row = (u * span + x) * 8
                pair = jnp.concatenate([tiles[x], tiles[x + 1]], axis=0).astype(jnp.bfloat16)
                forces[row : row + 16, lanes] = pair
        if s == half - 1:
            spread_sums[...] = lax.dot_general(
                forces_a[...], hot[:, lanes_a], (((1,), (1,)), ((), ())), preferred_element_type=F32
            )
    spread_sums[...] += lax.dot_general(
        forces_b[...], hot[:, lanes_b], (((1,), (1,)), ((), ())), preferred_element_type=F32
    )
    out = {}
    for x in range(span):
        for y in range(span):
            sums = [0.0, 0.0, 0.0]
            for u, (b, c) in enumerate(turns):
                j = y - b
                if 0 <= j < BRICK:
                    row = (u * span + x) * 8
                    sums[c] = sums[c] + spread_sums[row : row + 8, j * LANES : (j + 1) * LANES]
            total = sums[1] + turn(sums[0], -1) * shifts.high[1] + turn(sums[2], 1) * shifts.low[1]
            out[x - 1, y - 1] = total[0:4] + total[4:8]
    return out


def particle_kernel(counts, base_ref, stiff_ref, valid_ref, hot_ref, x_ref, effective_ref):
    span = BRICK + 2
    base = base_ref[...]
    plane = base // (LANES + 2)
    depth = base - plane * (LANES + 2)
    node_x = plane // span
    node_y = plane - node_x * span
    x_ref[...] = node_x
    effective_ref[...] = stiff_ref[...] * valid_ref[...].astype(F32)
    sub = lax.broadcasted_iota(jnp.int32, (LANES, LANES), 0)
    for s in range(base_ref.shape[0]):
        for j in range(BRICK):
            wanted = jnp.where(node_y[s : s + 1] == j, depth[s : s + 1], -1)
            hot_ref[j * LANES : (j + 1) * LANES, s * LANES : (s + 1) * LANES] = as_f32(sub == wanted).astype(jnp.bfloat16)


def side_parts(even_ref, odd_ref, is_even, inside_low, inside_high):
    odd = 1.0 - is_even
    below_odd, below_even = inside_low * is_even, inside_low * odd
    above_odd, above_even = inside_high * odd, inside_high * is_even

    def below(row, size):
        return odd_ref[row : row + size, :] * below_odd + even_ref[row : row + size, :] * below_even

    def above(row, size):
        return odd_ref[row : row + size, :] * above_odd + even_ref[row : row + size, :] * above_even

    return below, above


def put_sides(to_even_ref, to_odd_ref, row, size, up, down, is_even):
    odd = 1.0 - is_even
    to_even_ref[row : row + size, :] = (up * is_even + down * odd)[0:size]
    to_odd_ref[row : row + size, :] = (down * is_even + up * odd)[0:size]


def clear_tail(*refs):
    for ref in refs:
        ref[ref.shape[0] - 8 :, :] = jnp.zeros((8, LANES), F32)


def weight_of(mass):
    return DAMPING / (mass + 6.0)


def spread_mass(column):
    return jnp.broadcast_to(column[3:4], (4, LANES))


def live_rows():
    return as_f32(lax.broadcasted_iota(jnp.int32, (4, LANES), 0) < 3)


FIRST_ROWS = 20
SECOND_ROWS = 13


def pack_kernel(counts, fields_ref, own_ref, even_ref, odd_ref, slot_ref):
    place, shifts = Place(*counts), Shifts()
    own = {}
    for x in range(BRICK):
        for y in range(BRICK):
            own[x, y] = jnp.concatenate([fields_ref[m, x, y : y + 1, :] for m in range(4)], axis=0)
            own_ref[x, y] = own[x, y]
    odd_x = 1.0 - place.even_x
    for k, (x, y) in enumerate(SIDE_X):
        up, down = own[x + 4, y], own[-1 - x, y]
        even_ref[k] = up * place.even_x + down * odd_x
        odd_ref[k] = down * place.even_x + up * odd_x
    live = live_rows()
    mass0 = memo(lambda x, y: spread_mass(own[x, y]))
    weight0 = memo(lambda x, y: weight_of(mass0(x, y)))
    r = memo(lambda x, y: own[x, y] * live)
    cells = [(x, y) for x in (0, 1) for y in range(-1, 3)] + [(x, y) for x in (-1, 2) for y in (0, 1)]
    part = contribution(r, weight0, INNER, cells, shifts)
    rows = []
    for x in (0, 1):
        for column in pack_y(part, x, shifts):
            rows += [column[m : m + 1] for m in range(3)]
    for x in (-1, 2):
        column = part[x, 0] * shifts.even + part[x, 1] * shifts.odd
        rows += [column[m : m + 1] for m in range(3)]
    for x in (0, 1):
        mass1 = [
            shifts.pair_sum(sum(own[2 * x + i, 2 * y + j][3:4] for i in range(2) for j in range(2))) for y in (0, 1)
        ]
        rows.append(mass1[0] * shifts.even + mass1[1] * shifts.odd)
    for k in range(FIRST_ROWS // 4):
        slot_ref[k] = jnp.concatenate(rows[4 * k : 4 * k + 4], axis=0)


def widen_kernel(counts, own_ref, even_ref, odd_ref, wide_ref, to_even_ref, to_odd_ref):
    place = Place(*counts)
    odd_x = 1.0 - place.even_x
    left = (place.in_x[-1] * place.even_x, place.in_x[-1] * odd_x)
    right = (place.in_x[1] * odd_x, place.in_x[1] * place.even_x)

    def value(x, y):
        if 0 <= x < BRICK:
            return own_ref[x, y]
        odd, even = left if x < 0 else right
        k = SIDE_X.index((x, y) if x < 0 else mirror_x(x, y))
        return odd_ref[k] * odd + even_ref[k] * even

    value = memo(value)
    for x in range(-2, 6):
        for y in range(BRICK):
            wide_ref[x + 2, y] = value(x, y)
    odd_y = 1.0 - place.even_y
    for k, (x, y) in enumerate(SIDE):
        up, down = value(x, y + 4), value(x, -1 - y)
        to_even_ref[k] = up * place.even_y + down * odd_y
        to_odd_ref[k] = down * place.even_y + up * odd_y


def start_kernel(counts, wide_ref, even_ref, odd_ref, r_ref, mass0_ref, weight0_ref):
    place = Place(*counts)
    live = live_rows()
    odd_y = 1.0 - place.even_y
    below = (place.in_y[-1] * place.even_y, place.in_y[-1] * odd_y)
    above = (place.in_y[1] * odd_y, place.in_y[1] * place.even_y)
    for x in range(-2, 6):
        for y in range(-2, 6):
            if 0 <= y < BRICK:
                value = wide_ref[x + 2, y]
            else:
                key = (x, y) if y < 0 else mirror(x, y)
                odd, even = below if y < 0 else above
                if key in SIDE:
                    k = SIDE.index(key)
                    value = odd_ref[k] * odd + even_ref[k] * even
                else:
                    value = jnp.zeros((4, LANES), F32)
            r_ref[x + 2, y + 2] = value * live
            mass = spread_mass(value)
            mass0_ref[x + 2, y + 2] = mass
            weight0_ref[x + 2, y + 2] = weight_of(mass)


def reader(ref, offset):
    return memo(lambda x, y: ref[x + offset, y + offset])


def cycle(place, shifts, levels, r, r1, mass1, weight0, middle, coarse):
    width = place.count_x
    margin = 8 * (width + 1)

    def put(ref, row, value):
        for y in range(place.count_y):
            ref[pl.ds(margin + 8 * width * y + row, width, stride=8), :] = value[y]

    def get(ref, x, y):
        brick = (place.gy + y) * width + place.gx + x
        return ref[pl.ds(pl.multiple_of(margin + brick * 8, 8), 8), :]

    weight1 = [DAMPING / (m + 12.0) for m in mass1]
    weight2 = DAMPING / (levels.quad_sum(mass1[0] + mass1[1]) + 24.0)
    middle[...] = jnp.zeros_like(middle)
    coarse[...] = jnp.zeros_like(coarse)
    for x in range(2):
        put(middle, 4 * x + 3, weight1[x])
    for m in range(3):
        e = [weight1[x] * r1[m][x] for x in range(2)]
        for x in range(2):
            put(middle, 4 * x + m, e[x])
        put(coarse, m, levels.solve_2(levels.restrict(r1[m], e), weight2))

    def brick_at(x, y):
        rows = get(middle, x, y)
        first, second = rows * shifts.even, rows * shifts.odd
        return first + turn(first, 1), second + turn(second, -1)

    brick_at = memo(brick_at)

    def first_at(x, y):
        both = brick_at(x // 2, y // 2)[y % 2]
        return place.keep(both[4 * (x % 2) : 4 * (x % 2) + 4], x, y, 2)

    first = memo(first_at)
    e2 = memo(lambda x, y: place.keep(get(coarse, x, y)[0:4], x, y, 1))
    e1 = memo(lambda x, y: first(x, y) + e2(x // 2, y // 2))
    live = live_rows()

    def f1_at(x, y):
        weight = 2.0 * spread_mass(first(x, y))
        value = KEPT * e1(x, y) + first(x, y) + weight * beside_all(e1, x, y, shifts, 2)
        return place.keep(value * live, x, y, 2)

    return fine_level(r, memo(f1_at), weight0, place, shifts)


def apply(z, mass0, particles, work, shifts):
    image = stiffness_apply(z, *particles, *work, shifts)
    for x, y in INNER:
        image[x, y] = image[x, y] + mass0(x, y) * z(x, y)
    return image


def total_of(pairs):
    acc = 0.0
    for a, b in pairs:
        acc = acc + a * b
    return jnp.sum(jnp.sum(acc, axis=0, keepdims=True), axis=1, keepdims=True)


def dots_row(*values):
    lane = lane_index()
    row = 0.0
    for k, v in enumerate(values):
        row = row + as_f32(lane == k) * v
    return row


INNER = [(x, y) for x in range(BRICK) for y in range(BRICK)]
RIMMED = [(x, y) for x in range(-1, BRICK + 1) for y in range(-1, BRICK + 1)]


def first_kernel(counts, level_ref, r_ref, mass0_ref, weight0_ref,
                 hot_ref, x_ref, effective_ref, grad_ref, z_ref, image_ref, even_ref, odd_ref, dots_ref, mass1_ref,
                 *scratch):
    particles = (hot_ref, x_ref, effective_ref, grad_ref)
    place, shifts = Place(*counts), Shifts()
    levels = Levels(*counts, shifts)
    rows = lambda q: levels.load(level_ref, q, FIRST_ROWS)
    r1 = []
    for m in range(3):
        pair = [levels.gather_y(rows(6 * x + m), rows(6 * x + 3 + m)) for x in range(2)]
        pair[1] = pair[1] + levels.above_x(rows(12 + m))
        pair[0] = pair[0] + levels.below_x(rows(15 + m))
        r1.append(pair)
    mass1 = [rows(18), rows(19)]
    for x in range(2):
        mass1_ref[x] = mass1[x]
    r = reader(r_ref, 2)
    middle, coarse, *work = scratch
    z = cycle(place, shifts, levels, r, r1, mass1, reader(weight0_ref, 2), middle, coarse)
    image = apply(z, reader(mass0_ref, 2), particles, work, shifts)
    for x, y in RIMMED:
        z_ref[x + 1, y + 1] = z(x, y)
    for x, y in RIMMED:
        image_ref[x + 1, y + 1] = image[x, y]
    clear_tail(even_ref, odd_ref)
    for k, (x, y) in enumerate(SIDE_Y_IMAGE):
        put_sides(even_ref, odd_ref, 3 * k, 3, image[x, y + 4], image[x, -1 - y], place.even_y)
    rz = total_of((r(x, y), z(x, y)) for x, y in INNER)
    zaz = total_of((image[x, y], z(x, y)) for x, y in RIMMED)
    dots_ref[...] = dots_row(rz, zaz)


def along_y_kernel(counts, image_ref, even_ref, odd_ref, weight0_ref, dots_ref,
                   long_ref, to_even_ref, to_odd_ref, slot_ref):
    place, shifts = Place(*counts), Shifts()
    below, above = side_parts(even_ref, odd_ref, place.even_y, place.in_y[-1], place.in_y[1])

    def value(x, y):
        total = None
        if -1 <= y <= 4:
            total = place.keep(image_ref[x + 1, y + 1], x, y, BRICK)
        for part, key in ((below, (x, y)), (above, mirror(x, y))):
            if key in SIDE_Y_IMAGE:
                more = place.keep(part(3 * SIDE_Y_IMAGE.index(key), 4), x, 0, BRICK)
                total = more if total is None else total + more
        return total

    value = memo(value)
    cells = [(x, y) for x in range(-1, 3) for y in (0, 1)]
    part = contribution(value, reader(weight0_ref, 2), RIMMED, cells, shifts)
    for x in range(-1, 3):
        put_rows(slot_ref, 3 * (x + 1), part[x, 0] * shifts.even + part[x, 1] * shifts.odd)
    slot_ref[12] = dots_ref[...]
    clear_tail(to_even_ref, to_odd_ref)
    for k, (x, y) in enumerate(SIDE_X_IMAGE):
        put_sides(to_even_ref, to_odd_ref, 3 * k, 3, value(x + 4, y), value(-1 - x, y), place.even_x)
    for x in range(-1, BRICK + 1):
        for y in range(-2, 6):
            long_ref[x + 1, y + 2] = value(x, y)


def middle_kernel(counts, long_ref, even_ref, odd_ref, w_ref):
    place = Place(*counts)
    left, right = side_parts(even_ref, odd_ref, place.even_x, place.in_x[-1], place.in_x[1])
    live = live_rows()
    for x in range(-2, 6):
        for y in range(-2, 6):
            total = jnp.zeros((4, LANES), F32)
            if -1 <= x <= 4:
                total = total + long_ref[x + 1, y + 2]
            for part, key in ((left, (x, y)), (right, mirror_x(x, y))):
                if key in SIDE_X_IMAGE:
                    total = total + part(3 * SIDE_X_IMAGE.index(key), 4)
            w_ref[x + 2, y + 2] = total * live


def sums_of(ref, count, first, stride):
    return jnp.sum(ref[pl.ds(first, count, stride=stride), :], axis=0, keepdims=True)


def second_kernel(counts, change_ref, z1_ref, mass1_ref, r_ref, w_ref, mass0_ref, weight0_ref,
                  hot_ref, x_ref, effective_ref, grad_ref, z_ref, image_ref, x_even_ref, x_odd_ref, y_even_ref, y_odd_ref,
                  slots_ref, *scratch):
    particles = (hot_ref, x_ref, effective_ref, grad_ref)
    place, shifts = Place(*counts), Shifts()
    bricks = counts[0] * counts[1]
    levels = Levels(*counts, shifts)
    sums = sums_of(change_ref, bricks, 12, SECOND_ROWS)
    step = sums[:, 0:1] / sums[:, 1:2]
    rows = lambda q: levels.load(change_ref, q, SECOND_ROWS)
    r1 = []
    for m in range(3):
        r1.append([rows(3 + m) + levels.below_x(rows(9 + m)), rows(6 + m) + levels.above_x(rows(m))])
    w = reader(w_ref, 2)
    middle, coarse, *work = scratch
    of_w = cycle(place, shifts, levels, w, r1, [mass1_ref[0], mass1_ref[1]], reader(weight0_ref, 2), middle, coarse)
    z = memo(lambda x, y: z1_ref[x + 1, y + 1] - step * of_w(x, y))
    image = apply(z, reader(mass0_ref, 2), particles, work, shifts)
    r = memo(lambda x, y: r_ref[x + 2, y + 2] - step * w(x, y))
    for x, y in INNER:
        z_ref[x, y] = z(x, y)
        image_ref[x, y] = image[x, y]
    rz = total_of((r(x, y), z(x, y)) for x, y in INNER)
    zaz = total_of((image[x, y], z(x, y)) for x, y in RIMMED)
    zw = total_of((w_ref[x + 2, y + 2], z(x, y)) for x, y in INNER)
    row = dots_row(rz, zaz, zw)
    plain = jnp.concatenate([jnp.zeros((3, LANES), F32), row], axis=0)

    def fill(k, carry):
        slots_ref[k, 0] = plain
        return carry

    lax.fori_loop(0, bricks, fill, 0)
    for dx in (-1, 1):
        for dy in (-1, 1):
            there_x = (place.gx + dx >= 0) & (place.gx + dx < counts[0])
            there_y = (place.gy + dy >= 0) & (place.gy + dy < counts[1])
            column = image[BRICK if dx > 0 else -1, BRICK if dy > 0 else -1]

            @pl.when(there_x & there_y)
            def _(column=column, dx=dx, dy=dy):
                other = (place.gx + dx) * counts[1] + place.gy + dy
                slots_ref[other, 0] = jnp.concatenate([column[0:3], row], axis=0)

    clear_tail(x_even_ref, x_odd_ref, y_even_ref, y_odd_ref)
    for k in range(BRICK):
        put_sides(x_even_ref, x_odd_ref, 3 * k, 3, image[BRICK, k], image[-1, k], place.even_x)
        put_sides(y_even_ref, y_odd_ref, 3 * k, 3, image[k, BRICK], image[k, -1], place.even_y)


def last_kernel(counts, slots_ref, x_even_ref, x_odd_ref, y_even_ref, y_odd_ref, change_ref, z1_ref, z2_ref, r_ref, w_ref, image_ref, solution_ref, residual_ref):
    place = Place(*counts)
    bricks = counts[0] * counts[1]
    sums1 = sums_of(change_ref, bricks, 12, SECOND_ROWS)
    sums2 = jnp.sum(slots_ref[:, 0], axis=0)[3:4]
    rz1, zaz1 = sums1[:, 0:1], sums1[:, 1:2]
    rz2, zaz2, zw = sums2[:, 0:1], sums2[:, 1:2], sums2[:, 2:3]
    step1 = rz1 / zaz1
    ratio = rz2 / rz1
    step2 = rz2 / (zaz2 + 2.0 * ratio * zw + ratio * ratio * zaz1)
    image = {(x, y): image_ref[x, y] for x, y in INNER}
    left, right = side_parts(x_even_ref, x_odd_ref, place.even_x, place.in_x[-1], place.in_x[1])
    below, above = side_parts(y_even_ref, y_odd_ref, place.even_y, place.in_y[-1], place.in_y[1])
    end = BRICK - 1
    for k in range(BRICK):
        for at, part in (((0, k), left), ((end, k), right), ((k, 0), below), ((k, end), above)):
            image[at] = image[at] + part(3 * k, 4)
    for dx in (-1, 1):
        for dy in (-1, 1):
            other_x = jnp.clip(place.gx + dx, 0, counts[0] - 1)
            other_y = jnp.clip(place.gy + dy, 0, counts[1] - 1)
            other = other_x * counts[1] + other_y
            column = slots_ref[other, 0]
            at = (end if dx > 0 else 0, end if dy > 0 else 0)
            image[at] = image[at] + place.keep(column, dx, dy, 1)
    solution, residual = {}, {}
    for x, y in INNER:
        w = w_ref[x + 2, y + 2]
        z1 = z1_ref[x + 1, y + 1]
        solution[x, y] = step1 * z1 + step2 * (z2_ref[x, y] + ratio * z1)
        residual[x, y] = r_ref[x + 2, y + 2] - step1 * w - step2 * (image[x, y] + ratio * w)
    for x in range(BRICK):
        for ref, field in ((solution_ref, solution), (residual_ref, residual)):
            for m in range(3):
                ref[m, x] = jnp.concatenate([field[x, y][m : m + 1] for y in range(BRICK)], axis=0)


def call(kernel, counts, shapes, *args, scratch=()):
    shapes = [s if isinstance(s[0], tuple) else (s, F32) for s in shapes]
    return pl.pallas_call(
        functools.partial(kernel, counts),
        out_shape=[jax.ShapeDtypeStruct(*s) for s in shapes],
        scratch_shapes=scratch,
        compiler_params=pltpu.CompilerParams(vmem_limit_bytes=VMEM_BYTES),
    )(*args)


def per_device(counts, right_side, node_mass, gradients, stiffness, valid, node_base):
    bricks = counts[0] * counts[1]
    blocks = gradients.shape[2]
    grid = (counts[1], counts[0], LANES)
    tiles = 9 * (BRICK + 2) * 8
    depth = BRICK * LANES
    width = blocks * LANES
    scratch = (
        *[pltpu.VMEM((8 * (bricks + 2 * (counts[0] + 1)), LANES), F32)] * 2,
        pltpu.VMEM((tiles, depth), jnp.bfloat16),
        *[pltpu.VMEM((tiles, width // 2), jnp.bfloat16)] * 2,
        *[pltpu.VMEM((tiles, width // 2), F32)] * 2,
        pltpu.VMEM((tiles, depth), F32),
    )
    rows = lambda columns: (-(-(3 * len(columns) + 1) // 8) * 8, LANES)
    block = lambda *dims: (*dims, 4, LANES)

    def share(slot):
        sent = jnp.broadcast_to(slot[None], (bricks, *slot.shape))
        return lax.all_to_all(sent, AXES, 0, 0).reshape(-1, LANES)

    fields = jnp.concatenate([right_side, node_mass[None]], axis=0)
    own, to_even, to_odd, slot = call(
        pack_kernel, counts, [block(4, 4), block(8), block(8), block(FIRST_ROWS // 4)], fields
    )
    level = share(slot)
    even, odd = exchange(to_even, to_odd, "gx", counts)
    side = block(len(SIDE))
    wide, to_even, to_odd = call(widen_kernel, counts, [block(8, 4), side, side], own, even, odd)
    even, odd = exchange(to_even, to_odd, "gy", counts)
    row = (blocks, LANES)
    prepared = call(
        particle_kernel, counts, [((depth, width), jnp.bfloat16), (row, jnp.int32), row],
        node_base[0, 0], stiffness[0, 0], valid[0, 0],
    )
    particles = (*prepared, gradients[0, 0].transpose(1, 2, 0, 3))
    r, *fields = call(start_kernel, counts, [block(8, 8)] * 3, wide, even, odd)

    side = rows(SIDE_Y_IMAGE)
    z1, image, to_even, to_odd, dots, mass1 = call(
        first_kernel, counts,
        [block(6, 6), block(6, 6), side, side, (1, LANES), (2, *grid)],
        level, r, *fields, *particles, scratch=scratch,
    )
    even, odd = exchange(to_even, to_odd, "gy", counts)
    side = rows(SIDE_X_IMAGE)
    long, to_even, to_odd, slot = call(
        along_y_kernel, counts, [block(6, 8), side, side, (SECOND_ROWS, 1, LANES)], image, even, odd, fields[1], dots
    )
    change = share(slot)
    even, odd = exchange(to_even, to_odd, "gx", counts)
    (w,) = call(middle_kernel, counts, [block(8, 8)], long, even, odd)
    side = (2 * 8, LANES)
    z2, image, x_even, x_odd, y_even, y_odd, slots = call(
        second_kernel, counts, [block(4, 4), block(4, 4), side, side, side, side, (bricks, 1, 4, LANES)],
        change, z1, mass1, r, w, *fields, *particles, scratch=scratch,
    )
    sides = (*exchange(x_even, x_odd, "gx", counts), *exchange(y_even, y_odd, "gy", counts))
    slots = lax.all_to_all(slots, AXES, 0, 0)
    return tuple(
        call(last_kernel, counts, [right_side.shape, right_side.shape], slots, *sides, change, z1, z2, r, w, image)
    )


def solution(mesh):
    counts = (mesh.shape["gx"], mesh.shape["gy"])
    return jax.shard_map(
        functools.partial(per_device, counts),
        mesh=mesh,
        in_specs=(
            P(None, "gx", "gy", None),
            P("gx", "gy", None),
            P("gx", "gy", None, None, None, None),
            P("gx", "gy", None, None),
            P("gx", "gy", None, None),
            P("gx", "gy", None, None),
        ),
        out_specs=(P(None, "gx", "gy", None), P(None, "gx", "gy", None)),
        check_vma=False,
    )
```
